128 devices in a mesh: dp: 2 (over z_hi), branch: 8 (over y, z_lo), tensor: 8 (over x, core).
Axes of the slice: x: 4, y: 4, z: 4 (z_hi: 2, z_lo: 2; z = z_hi * 2 + z_lo), core: 2. Of those that a mesh axis runs over, the one named last changes fastest.
Arguments:
- queries: bfloat16 [2, 2048, 8192], P('dp', 'branch', 'tensor'), may hold values from -8 to 8
- prefix_keys: bfloat16 [2, 2048, 1024], P('dp', 'branch', 'tensor'), may hold values from -8 to 8
- prefix_values: bfloat16 [2, 2048, 1024], P('dp', 'branch', 'tensor'), may hold values from -6 to 6
- keys: bfloat16 [2, 2048, 1024], P('dp', 'branch', 'tensor'), may hold values from -6 to 6
- values: bfloat16 [2, 2048, 1024], P('dp', 'branch', 'tensor'), may hold values from -6 to 6
- ancestors: int32 [2, 16, 2], P('dp'), may hold values from -1 to 15, as said below
- advantages: int32 [2, 2048], P('dp', 'branch'), may hold values from -4 to 4
- upstream: bfloat16 [2, 2048, 5120], P('dp', 'branch', 'tensor'), may hold values from -6 to 6
- out_weight: bfloat16 [5120, 8192], P(('dp', 'branch'), 'tensor'), may hold values from -0.0625 to 0.0625
Outputs:
- query_grad: bfloat16 [2, 2048, 8192], P('dp', 'branch', 'tensor')
- prefix_key_grad: bfloat16 [2, 2048, 1024], P('dp', 'branch', 'tensor')
- prefix_value_grad: bfloat16 [2, 2048, 1024], P('dp', 'branch', 'tensor')
- key_grad: bfloat16 [2, 2048, 1024], P('dp', 'branch', 'tensor')
- value_grad: bfloat16 [2, 2048, 1024], P('dp', 'branch', 'tensor')
- weight_grad: float32 [5120, 8192], P(('dp', 'branch'), 'tensor')
The draws below stay inside these ranges and needn't reach their ends.
Inputs may be any that keep to these rules, and one draw needn't show every extreme that they name: ancestors[t, s, 0] is the parent and ancestors[t, s, 1] the grandparent of segment s in tree t, -1 where there is none; segments form up to three levels below the prefix, and every named segment is an ancestor on the path from s to the prefix.
All inputs are finite; a program needn't handle non-finite values.
Results may differ from the reference program's by a relative error of at most 0.03.
Values may be sent and summed in bfloat16 or wider, within the bound.
A program may use at most 128 MiB of HBM per device.

```python
import math
import jax
import jax.numpy as jnp
from jax import lax

D = 5120
H = 64
KVH = 8
HD = 128
SEG = 128
TREES = 2
NSEG = 16
TOK = 2048
PREFIX = 2048


def draw_queries(key, part):
    key = jax.random.fold_in(key, 1)
    shape = (TREES, TOK, H * HD)
    return jnp.clip(jax.random.normal(key, shape, jnp.float32), -4.0, 4.0).astype(jnp.bfloat16)


def draw_prefix_keys(key, part):
    key = jax.random.fold_in(key, 2)
    shape = (TREES, PREFIX, KVH * HD)
    return jnp.clip(jax.random.normal(key, shape, jnp.float32), -4.0, 4.0).astype(jnp.bfloat16)


def draw_ancestors(key, part):
    key = jax.random.fold_in(key, 5)
    first = NSEG // 4
    second = (NSEG - first) // 2
    order = jnp.arange(NSEG, dtype=jnp.int32)
    tables = []
    for tree_id in range(TREES):
        tree_key = jax.random.fold_in(key, tree_id)
        perm_key, upper_key, lower_key = jax.random.split(tree_key, 3)
        shuffled = jax.random.permutation(perm_key, NSEG).astype(jnp.int32)
        leading = shuffled[0]
        shuffled = jnp.where(shuffled == NSEG - 1, leading, shuffled)
        shuffled = shuffled.at[0].set(NSEG - 1)
        level_two = jax.random.randint(upper_key, (NSEG,), 0, first, dtype=jnp.int32)
        level_two = level_two.at[first].set(0)
        level_three = first + jax.random.randint(lower_key, (NSEG,), 0, second, dtype=jnp.int32)
        parent = jnp.where(order < first, -1, jnp.where(order < first + second, level_two, level_three))
        grand = jnp.where(order < first + second, -1, level_two[jnp.clip(parent, 0, NSEG - 1)])
        mapped_parent = jnp.where(parent < 0, -1, shuffled[jnp.clip(parent, 0, NSEG - 1)])
        mapped_grand = jnp.where(grand < 0, -1, shuffled[jnp.clip(grand, 0, NSEG - 1)])
        rows = jnp.stack([mapped_parent, mapped_grand], axis=1)
        tables.append(jnp.zeros((NSEG, 2), jnp.int32).at[shuffled].set(rows))
    return jnp.stack(tables).astype(jnp.int32)


def touch_ends(entries, own_key, low, largest):
    spot = [jax.random.randint(jax.random.fold_in(own_key, axis), (), 0, length) for axis, length in enumerate(entries.shape)]
    longest = entries.shape.index(max(entries.shape))
    next_to = spot[:longest] + [(spot[longest] + 1) % entries.shape[longest]] + spot[longest + 1:]
    return entries.at[tuple(spot)].set(low).at[tuple(next_to)].set(largest)


def level_of(key, extent, cuts, smallest, high):
    gain = 1.0
    for axis_at, blocks in cuts:
        draws = jax.random.uniform(jax.random.fold_in(jax.random.fold_in(key, 6), axis_at), (blocks,), jnp.float32, smallest / len(cuts), high / len(cuts))
        gain = gain * jnp.repeat(jnp.exp(draws), extent[axis_at] // blocks).reshape((-1,) + (1,) * (len(extent) - 1 - axis_at))
    return gain


def scatter_about(own_key, extent, spread, limit, shards=(), kind=jnp.bfloat16):
    factor_of = level_of(own_key, extent, shards, -0.22, 0.18) if shards else 1.0
    values = jax.random.normal(own_key, extent, jnp.float32) * spread * factor_of
    return jnp.minimum(jnp.maximum(values, -limit), limit).astype(kind)


def setup_inputs(seed: int = 0) -> dict:
    streams_of = jax.random.split(jax.random.key(seed), 10)
    queries = draw_queries(jax.random.fold_in(streams_of[9], 71), 0)
    prefix_keys = draw_prefix_keys(jax.random.fold_in(streams_of[9], 71), 0)
    prefix_values = scatter_about(streams_of[2], (TREES, PREFIX, KVH * HD), 1.0, 6.0, ((0, 2), (1, 8), (2, 8)))
    keys = scatter_about(streams_of[3], (TREES, TOK, KVH * HD), 1.0, 6.0, ((0, 2), (1, 8), (2, 8)))
    values = scatter_about(streams_of[4], (TREES, TOK, KVH * HD), 1.0, 6.0, ((0, 2), (1, 8), (2, 8)))
    ancestors = draw_ancestors(jax.random.fold_in(streams_of[9], 71), 0)
    advantages = touch_ends(jax.random.randint(streams_of[6], (TREES, TOK), -4, 5), jax.random.fold_in(streams_of[6], 1), -4, 4).astype(jnp.int32)
    upstream = scatter_about(streams_of[7], (TREES, TOK, D), 1.0, 6.0, ((0, 2), (1, 8), (2, 8)))
    out_weight = scatter_about(streams_of[8], (D, H * HD), (H * HD) ** -0.5, 0.0625, ((0, 16), (1, 8)))
    return dict(queries=queries, prefix_keys=prefix_keys, prefix_values=prefix_values, keys=keys, values=values, ancestors=ancestors, advantages=advantages, upstream=upstream, out_weight=out_weight)


def visibility(own_table):
    positions = jnp.arange(TOK, dtype=jnp.int32)
    query_seg = positions // SEG
    query_pos = positions % SEG
    lineage = own_table[query_seg]
    key_seg = positions // SEG
    key_pos = positions % SEG
    seg_seen = (key_seg[None, :] == lineage[:, 0:1]) | (key_seg[None, :] == lineage[:, 1:2])
    seg_seen = seg_seen | (key_seg[None, :] == query_seg[:, None]) & (key_pos[None, :] <= query_pos[:, None])
    return jnp.concatenate([jnp.ones((TOK, PREFIX), dtype=bool), seg_seen], axis=1)

def head_grads(query_head, grad_head, key_head, value_head, allowed):
    score_scale = 1.0 / math.sqrt(HD)
    scores = jnp.dot(query_head, key_head.T, preferred_element_type=jnp.float32) * score_scale
    row_max = lax.optimization_barrier(jnp.max(jnp.where(allowed, scores, -jnp.inf), axis=1, keepdims=True))
    exponent = jnp.where(allowed, jnp.exp(scores - row_max), jnp.zeros_like(scores))
    shares = exponent / lax.optimization_barrier(jnp.sum(exponent, axis=1, keepdims=True))
    shares_low = shares.astype(jnp.bfloat16)
    attn = jnp.dot(shares_low, value_head, preferred_element_type=jnp.float32).astype(jnp.bfloat16)
    grad_share = jnp.dot(grad_head, value_head.T, preferred_element_type=jnp.float32)
    row_dot = lax.optimization_barrier(jnp.sum(grad_head.astype(jnp.float32) * attn.astype(jnp.float32), axis=1, keepdims=True))
    grad_score = (shares * (grad_share - row_dot)).astype(jnp.bfloat16)
    grad_query = (jnp.dot(grad_score, key_head, preferred_element_type=jnp.float32) * score_scale).astype(jnp.bfloat16)
    key_sum = jnp.dot(grad_score.T, query_head, preferred_element_type=jnp.float32)
    value_sum = jnp.dot(shares_low.T, grad_head, preferred_element_type=jnp.float32)
    return (grad_query, attn, key_sum, value_sum)

def reference(queries, prefix_keys, prefix_values, keys, values, ancestors, advantages, upstream, out_weight):
    group_size = H // KVH
    score_scale = 1.0 / math.sqrt(HD)
    query_out = []
    prefix_key_out = []
    prefix_value_out = []
    key_out = []
    value_out = []
    weight_total = jnp.zeros((D, H * HD), jnp.float32)
    for tree_id in range(TREES):
        weighting = advantages[tree_id].astype(jnp.float32) * 0.25
        cotangent = (upstream[tree_id].astype(jnp.float32) * weighting[:, None]).astype(jnp.bfloat16)
        d_attn = jnp.dot(cotangent, out_weight, preferred_element_type=jnp.float32).astype(jnp.bfloat16)
        ctx_keys = jnp.concatenate([prefix_keys[tree_id], keys[tree_id]], axis=0)
        ctx_values = jnp.concatenate([prefix_values[tree_id], values[tree_id]], axis=0)
        allowed = visibility(ancestors[tree_id])
        tree_queries = queries[tree_id]

        def one_head(head_id):
            kv_id = head_id // group_size
            query_head = lax.dynamic_slice_in_dim(tree_queries, (head_id * HD).astype(jnp.int32), HD, 1)
            grad_head = lax.dynamic_slice_in_dim(d_attn, (head_id * HD).astype(jnp.int32), HD, 1)
            key_head = lax.dynamic_slice_in_dim(ctx_keys, (kv_id * HD).astype(jnp.int32), HD, 1)
            value_head = lax.dynamic_slice_in_dim(ctx_values, (kv_id * HD).astype(jnp.int32), HD, 1)
            return head_grads(query_head, grad_head, key_head, value_head, allowed)
        grad_query, attn, key_sum, value_sum = lax.map(one_head, jnp.arange(H, dtype=jnp.int32))
        query_out.append(grad_query.transpose(1, 0, 2).reshape(TOK, H * HD))
        attn_flat = attn.transpose(1, 0, 2).reshape(TOK, H * HD)
        key_total = key_sum.reshape(KVH, group_size, PREFIX + TOK, HD).sum(axis=1)
        value_total = value_sum.reshape(KVH, group_size, PREFIX + TOK, HD).sum(axis=1)
        key_total = (key_total.transpose(1, 0, 2).reshape(PREFIX + TOK, KVH * HD) * score_scale).astype(jnp.bfloat16)
        value_total = value_total.transpose(1, 0, 2).reshape(PREFIX + TOK, KVH * HD).astype(jnp.bfloat16)
        prefix_key_out.append(key_total[:PREFIX])
        key_out.append(key_total[PREFIX:])
        prefix_value_out.append(value_total[:PREFIX])
        value_out.append(value_total[PREFIX:])
        weight_total = weight_total + lax.dot_general(cotangent, attn_flat, (((0,), (0,)), ((), ())), preferred_element_type=jnp.float32)
    return (jnp.stack(query_out), jnp.stack(prefix_key_out), jnp.stack(prefix_value_out), jnp.stack(key_out), jnp.stack(value_out), weight_total)
```

```python
import math

import jax
import jax.numpy as jnp
from jax import lax
from jax.experimental import pallas as pl
from jax.experimental.pallas import tpu as pltpu
from jax.sharding import PartitionSpec as P

HD = 128
SEG = 128
GROUP = 8
TOKL = 256
KVB = 8
WROWS = 320
NCOL = 1024
UCOL = 640
CTX = 2048
SEGCTX = 384
ALLCTX = CTX + SEGCTX
ROWS = 512
SCALE = 1.0 / math.sqrt(HD)
LOG2E = 1.4426950408889634
BF = jnp.bfloat16
F32 = jnp.float32
VM = pl.BlockSpec(memory_space=pltpu.VMEM)
VLIM = 56 * 2**20


def coords():
    b = lax.axis_index("branch")
    t = lax.axis_index("tensor")
    return t // 2, b // 2, lax.axis_index("dp") * 2 + b % 2, t % 2


def place(x, y, z, c):
    return {"dp": z // 2, "branch": y * 2 + z % 2, "tensor": x * 2 + c}


def rcopy(src, dst, ss, rs, dev):
    return pltpu.make_async_remote_copy(
        src_ref=src, dst_ref=dst, send_sem=ss, recv_sem=rs,
        device_id=dev, device_id_type=pl.DeviceIdType.MESH,
    )


def signal(sem, dev):
    pl.semaphore_signal(sem, inc=1, device_id=dev, device_id_type=pl.DeviceIdType.MESH)


def nt_dot(a, b):
    return lax.dot_general(a, b, (((1,), (1,)), ((), ())), preferred_element_type=F32)


def gather_kernel(
    up, adv, w, pk, pv, sk, sv,
    dattn, kvg, cott,
    cot, cotb, wg, dpart, drecv,
    cot_s, cot_r, sib_s, sib_r, w_s, w_r, kz_s, kz_r, ko_s, ko_r, kf_s, kf_r, d_s, d_r,
):
    x, y, z, c = coords()
    me_b = y * 2 + z % 2
    sib_b = y * 2 + 1 - z % 2
    zsib = z + 1 - 2 * (z % 2)
    target_y = 2 * (x % 2) + c
    is_recv = c == y % 2
    self_send = target_y == y
    half = x // 2
    sib = place(x, y, z, 1 - c)

    bar = pltpu.get_barrier_semaphore()
    for d in range(1, 4):
        signal(bar, place(x, y, (z + d) % 4, c))
        signal(bar, place(x, (y + d) % 4, z, c))
    signal(bar, sib)

    @pl.when(is_recv)
    def _():
        for h in range(2):
            for yy in range(4):
                sx = 2 * h + y // 2

                @pl.when(jnp.logical_not((sx == x) & (yy == y)))
                def _():
                    signal(bar, place(sx, yy, z, c))

    kvg[0, me_b] = pk[...]
    kvg[1, me_b] = pv[...]
    kvg[2, me_b] = sk[...]
    kvg[3, me_b] = sv[...]
    wrow = jnp.broadcast_to(adv[...].astype(F32) * 0.25, (TOKL, TOKL))
    ri = lax.broadcasted_iota(jnp.int32, (TOKL, TOKL), 0)
    ci = lax.broadcasted_iota(jnp.int32, (TOKL, TOKL), 1)
    diag = jnp.where(ri == ci, wrow, 0.0).astype(BF)
    cot[...] = jnp.dot(diag, up[...], preferred_element_type=F32).astype(BF)

    pl.semaphore_wait(bar, 11 - self_send.astype(jnp.int32))

    def kz():
        return rcopy(kvg.at[:, me_b], kvg.at[:, me_b], kz_s, kz_r, place(x, y, zsib, c))

    def ko(d):
        return rcopy(kvg.at[:, me_b], kvg.at[:, me_b], ko_s.at[d - 1], ko_r.at[d - 1],
                     place(x, (y + d) % 4, z, c))

    def kf(d):
        return rcopy(kvg.at[:, sib_b], kvg.at[:, sib_b], kf_s.at[d - 1], kf_r.at[d - 1],
                     place(x, (y + d) % 4, z, c))

    def wc(d):
        return rcopy(w, wg.at[pl.ds(pl.multiple_of(z * WROWS, 64), WROWS)], w_s.at[d - 1], w_r.at[d - 1],
                     place(x, y, (z + d) % 4, c))

    def cc(d):
        return rcopy(cot, cotb.at[half, y], cot_s.at[d], cot_r.at[half, y],
                     place((x + d) % 4, target_y, z, c))

    kz().start()
    for d in (1, 3, 2):
        cc(d).start()

    @pl.when(jnp.logical_not(self_send))
    def _():
        cc(0).start()

    for d in (1, 3, 2):
        wc(d).start()
    for d in (1, 3, 2):
        ko(d).start()
    wg[pl.ds(pl.multiple_of(z * WROWS, 64), WROWS), :] = w[...]

    @pl.when(self_send)
    def _():
        cotb[half, y] = cot[...]

    kz().wait()
    for d in (1, 3, 2):
        kf(d).start()

    def sc(h, yy):
        return rcopy(cotb.at[h, yy], cotb.at[h, yy], sib_s.at[h, yy], sib_r.at[h, yy], sib)

    @pl.when(is_recv)
    def _():
        for h in range(2):
            for yy in range(4):
                @pl.when(jnp.logical_not((2 * h + y // 2 == x) & (yy == y)))
                def _():
                    rcopy(cot, cotb.at[h, yy], cot_s.at[0], cot_r.at[h, yy], sib).wait_recv()
                sc(h, yy).start()

    @pl.when(jnp.logical_not(is_recv))
    def _():
        for h in range(2):
            for yy in range(4):
                sc(h, yy).wait_recv()

    for d in range(1, 4):
        wc(d).wait()

    def block(yy):
        return jnp.dot(cotb[0, yy], wg[0:UCOL, :], preferred_element_type=F32) + jnp.dot(
            cotb[1, yy], wg[UCOL:2 * UCOL, :], preferred_element_type=F32)

    def dc(d):
        return rcopy(dpart.at[d - 1], drecv.at[d - 1], d_s.at[d - 1], d_r.at[d - 1],
                     place(x, (y + d) % 4, z, c))

    @pl.loop(1, 4)
    def _(d):
        dpart[d - 1] = block((y + d) % 4).astype(BF)
        dc(d).start()

    own = block(y)
    for h in range(2):
        for yy in range(4):
            cott[pl.ds(h * UCOL, UCOL), pl.ds(yy * TOKL, TOKL)] = cotb[h, yy].T

    for d in range(1, 4):
        dc(d).wait()
    dattn[...] = (own + drecv[0].astype(F32) + drecv[1].astype(F32) + drecv[2].astype(F32)).astype(BF)

    for d in range(1, 4):
        ko(d).wait()
        kf(d).wait()
        cc(d).wait_send()

    @pl.when(jnp.logical_not(self_send))
    def _():
        cc(0).wait_send()

    @pl.when(is_recv)
    def _():
        for h in range(2):
            for yy in range(4):
                sc(h, yy).wait_send()


def attention_kernel(anc, q, do, kv, dq, attn, dkv, s_f, p_b, kc, vc, dkt, dvt, segk, segv):
    first = lax.axis_index("branch") * 2
    cexp = SCALE * LOG2E
    chunks = [(i * 512, 512) for i in range(4)] + [(CTX, SEGCTX)]
    dkt[...] = jnp.zeros_like(dkt)
    dvt[...] = jnp.zeros_like(dvt)
    segk[...] = jnp.zeros_like(segk)
    segv[...] = jnp.zeros_like(segv)
    kc[0:CTX, :] = kv[0]
    vc[0:CTX, :] = kv[1]

    @pl.loop(0, 2)
    def _(s):
        seg = first + s
        a0 = anc[0, seg, 0]
        a1 = anc[0, seg, 1]
        for i, a in enumerate((a0, a1, seg)):
            rows = pl.ds(pl.multiple_of(jnp.maximum(a, 0) * SEG, SEG), SEG)
            kc[CTX + i * SEG:CTX + (i + 1) * SEG, :] = kv[2, rows, :]
            vc[CTX + i * SEG:CTX + (i + 1) * SEG, :] = kv[3, rows, :]
        dkt[:, CTX:] = jnp.zeros((HD, SEGCTX), F32)
        dvt[:, CTX:] = jnp.zeros((HD, SEGCTX), F32)
        tok = pl.ds(pl.multiple_of(s * SEG, SEG), SEG)
        col = lax.broadcasted_iota(jnp.int32, (ROWS, SEGCTX), 1)
        row = lax.broadcasted_iota(jnp.int32, (ROWS, SEGCTX), 0) % SEG
        seen = jnp.where(col < SEG, (a0 >= 0).astype(jnp.int32),
                         jnp.where(col < 2 * SEG, (a1 >= 0).astype(jnp.int32),
                                   (col - 2 * SEG <= row).astype(jnp.int32))) > 0

        for hb in range(GROUP * SEG // ROWS):
            nh = ROWS // SEG
            heads = [pl.ds((hb * nh + i) * HD, HD) for i in range(nh)]
            qb = jnp.concatenate([q[tok, h] for h in heads], axis=0)
            mx = None
            for st, n in chunks:
                sc = nt_dot(qb, kc[st:st + n, :])
                if st == CTX:
                    sc = jnp.where(seen, sc, -1e30)
                s_f[:, st:st + n] = sc
                for t in range(n // 128):
                    part = sc[:, t * 128:(t + 1) * 128]
                    mx = part if mx is None else jnp.maximum(mx, part)
            m = jnp.max(mx, axis=1, keepdims=True)
            lsum = None
            o = None
            for st, n in chunks:
                p = jnp.exp2((s_f[:, st:st + n] - m) * cexp)
                for t in range(n // 128):
                    part = p[:, t * 128:(t + 1) * 128]
                    lsum = part if lsum is None else lsum + part
                pb = p.astype(BF)
                p_b[:, st:st + n] = pb
                oc = jnp.dot(pb, vc[st:st + n, :], preferred_element_type=F32)
                o = oc if o is None else o + oc
            il = 1.0 / jnp.sum(lsum, axis=1, keepdims=True)
            ob = (o * il).astype(BF)
            for i, h in enumerate(heads):
                attn[tok, h] = ob[i * SEG:(i + 1) * SEG]
            dob = jnp.concatenate([do[tok, h] for h in heads], axis=0)
            dos = (dob.astype(F32) * il).astype(BF)
            delta = jnp.sum(dos.astype(F32) * ob.astype(F32), axis=1, keepdims=True)
            qt = qb.T
            dot_ = dos.T
            dqa = None
            for st, n in chunks:
                dp = nt_dot(dos, vc[st:st + n, :])
                pb = p_b[:, st:st + n]
                ds = (pb.astype(F32) * (dp - delta)).astype(BF)
                dqc = jnp.dot(ds, kc[st:st + n, :], preferred_element_type=F32)
                dqa = dqc if dqa is None else dqa + dqc
                dkt[:, st:st + n] += jnp.dot(qt, ds, preferred_element_type=F32)
                dvt[:, st:st + n] += jnp.dot(dot_, pb, preferred_element_type=F32)
            dqb = (dqa * SCALE).astype(BF)
            for i, h in enumerate(heads):
                dq[tok, h] = dqb[i * SEG:(i + 1) * SEG]

        for i, a in enumerate((a0, a1, seg)):
            cols = pl.ds(pl.multiple_of(jnp.maximum(a, 0) * SEG, SEG), SEG)
            segk[cols, :] += dkt[:, CTX + i * SEG:CTX + (i + 1) * SEG].T
            segv[cols, :] += dvt[:, CTX + i * SEG:CTX + (i + 1) * SEG].T

    for i in range(4):
        dkv[0, i * 512:(i + 1) * 512, :] = (dkt[:, i * 512:(i + 1) * 512].T * SCALE).astype(BF)
        dkv[1, i * 512:(i + 1) * 512, :] = dvt[:, i * 512:(i + 1) * 512].T.astype(BF)
    dkv[2] = (segk[...] * SCALE).astype(BF)
    dkv[3] = segv[...].astype(BF)


def reduce_kernel(
    attn, cott, dkv,
    opk, opv, osk, osv, owg,
    attng, gpart, grecv, krecv, kpart, zrecv,
    a_s, a_r, k_s, k_r, z_s, z_r, g_s, g_r,
):
    x, y, z, c = coords()
    zsib = z + 1 - 2 * (z % 2)
    bar = pltpu.get_barrier_semaphore()
    for d in range(1, 4):
        signal(bar, place(x, y, (z + d) % 4, c))
        signal(bar, place(x, (y + d) % 4, z, c))
    pl.semaphore_wait(bar, 6)

    def ac(d):
        return rcopy(attn, attng.at[pl.ds(pl.multiple_of(y * TOKL, TOKL), TOKL)], a_s.at[d - 1], a_r.at[d - 1],
                     place(x, (y + d) % 4, z, c))

    def kc(d):
        yy = (y + d) % 4
        return rcopy(dkv.at[:, pl.ds(pl.multiple_of(yy * 512, 512), 512)], krecv.at[d - 1], k_s.at[d - 1],
                     k_r.at[d - 1], place(x, yy, z, c))

    def gc(d):
        return rcopy(gpart.at[d - 1], grecv.at[d - 1], g_s.at[d - 1], g_r.at[d - 1],
                     place(x, y, (z + d) % 4, c))

    def zc():
        return rcopy(kpart, zrecv, z_s, z_r, place(x, y, zsib, c))

    for d in (1, 3, 2):
        ac(d).start()
    for d in (1, 3, 2):
        kc(d).start()
    attng[pl.ds(pl.multiple_of(y * TOKL, TOKL), TOKL), :] = attn[...]
    for d in range(1, 4):
        ac(d).wait()

    def block(zz):
        return jnp.dot(cott[pl.ds(pl.multiple_of(zz * WROWS, 64), WROWS), :], attng[...],
                       preferred_element_type=F32)

    @pl.loop(1, 4)
    def _(d):
        gpart[d - 1] = block((z + d) % 4).astype(BF)
        gc(d).start()

    owg[...] = block(z)
    for d in range(1, 4):
        kc(d).wait()
    zl = z % 2

    def ksum(i, zz):
        r = pl.ds(pl.multiple_of(zz * 256, 256), 256)
        own = dkv[i, pl.ds(pl.multiple_of(y * 512 + zz * 256, 256), 256), :].astype(F32)
        return own + krecv[0, i, r, :].astype(F32) + krecv[1, i, r, :].astype(F32) + krecv[2, i, r, :].astype(F32)

    for i in range(4):
        kpart[i] = ksum(i, 1 - zl).astype(BF)
    zc().start()
    zc().wait()
    for i, o in enumerate((opk, opv, osk, osv)):
        o[...] = (ksum(i, zl) + zrecv[i].astype(F32)).astype(BF)
    for d in range(1, 4):
        gc(d).wait()
    owg[...] += grecv[0].astype(F32) + grecv[1].astype(F32) + grecv[2].astype(F32)


def on_device(
    queries, prefix_keys, prefix_values, keys, values, ancestors, advantages, upstream, out_weight
):
    dma = pltpu.SemaphoreType.DMA
    sds = jax.ShapeDtypeStruct
    dattn, kvg, cott = pl.pallas_call(
        gather_kernel,
        out_shape=(
            sds((TOKL, NCOL), BF),
            sds((4, KVB, 256, HD), BF),
            sds((2 * UCOL, 4 * TOKL), BF),
        ),
        in_specs=[VM] * 7,
        out_specs=(VM, VM, VM),
        scratch_shapes=[
            pltpu.VMEM((TOKL, UCOL), BF),
            pltpu.VMEM((2, 4, TOKL, UCOL), BF),
            pltpu.VMEM((4 * WROWS, NCOL), BF),
            pltpu.VMEM((3, TOKL, NCOL), BF),
            pltpu.VMEM((3, TOKL, NCOL), BF),
            dma((4,)), dma((2, 4)), dma((2, 4)), dma((2, 4)),
            dma((3,)), dma((3,)), dma, dma, dma((3,)), dma((3,)), dma((3,)), dma((3,)),
            dma((3,)), dma((3,)),
        ],
        compiler_params=pltpu.CompilerParams(
            collective_id=0, has_side_effects=True, vmem_limit_bytes=VLIM),
        name="gather",
    )(upstream[0], advantages, out_weight, prefix_keys[0], prefix_values[0], keys[0], values[0])

    dq, attn, dkv = pl.pallas_call(
        attention_kernel,
        out_shape=(
            sds((TOKL, NCOL), BF),
            sds((TOKL, NCOL), BF),
            sds((4, CTX, HD), BF),
        ),
        in_specs=[pl.BlockSpec(memory_space=pltpu.SMEM), VM, VM, VM],
        out_specs=(VM, VM, VM),
        scratch_shapes=[
            pltpu.VMEM((ROWS, ALLCTX), F32),
            pltpu.VMEM((ROWS, ALLCTX), BF),
            pltpu.VMEM((ALLCTX, HD), BF),
            pltpu.VMEM((ALLCTX, HD), BF),
            pltpu.VMEM((HD, ALLCTX), F32),
            pltpu.VMEM((HD, ALLCTX), F32),
            pltpu.VMEM((CTX, HD), F32),
            pltpu.VMEM((CTX, HD), F32),
        ],
        compiler_params=pltpu.CompilerParams(vmem_limit_bytes=VLIM),
        name="attention",
    )(ancestors, queries[0], dattn, kvg.reshape(4, CTX, HD))

    opk, opv, osk, osv, owg = pl.pallas_call(
        reduce_kernel,
        out_shape=tuple([sds((256, HD), BF)] * 4 + [sds((WROWS, NCOL), F32)]),
        in_specs=[VM] * 3,
        out_specs=tuple([VM] * 5),
        scratch_shapes=[
            pltpu.VMEM((4 * TOKL, NCOL), BF),
            pltpu.VMEM((3, WROWS, NCOL), BF),
            pltpu.VMEM((3, WROWS, NCOL), BF),
            pltpu.VMEM((3, 4, 512, HD), BF),
            pltpu.VMEM((4, 256, HD), BF),
            pltpu.VMEM((4, 256, HD), BF),
            dma((3,)), dma((3,)), dma((3,)), dma((3,)), dma, dma, dma((3,)), dma((3,)),
        ],
        compiler_params=pltpu.CompilerParams(
            collective_id=1, has_side_effects=True, vmem_limit_bytes=VLIM),
        name="reduce",
    )(attn, cott, dkv)
    return dq[None], opk[None], opv[None], osk[None], osv[None], owg


def solution(mesh):
    return jax.shard_map(
        on_device,
        mesh=mesh,
        in_specs=(
            P("dp", "branch", "tensor"),
            P("dp", "branch", "tensor"),
            P("dp", "branch", "tensor"),
            P("dp", "branch", "tensor"),
            P("dp", "branch", "tensor"),
            P("dp", None, None),
            P("dp", "branch"),
            P("dp", "branch", "tensor"),
            P(("dp", "branch"), "tensor"),
        ),
        out_specs=(
            P("dp", "branch", "tensor"),
            P("dp", "branch", "tensor"),
            P("dp", "branch", "tensor"),
            P("dp", "branch", "tensor"),
            P("dp", "branch", "tensor"),
            P(("dp", "branch"), "tensor"),
        ),
        check_vma=False,
    )
```

```python
import math

import jax
import jax.numpy as jnp
from jax import lax
from jax.experimental import pallas as pl
from jax.experimental.pallas import tpu as pltpu
from jax.sharding import PartitionSpec as P

HD = 128
SEG = 128
GROUP = 8
TOKL = 256
KVB = 8
WROWS = 320
NCOL = 1024
UCOL = 640
CTX = 2048
SEGCTX = 384
ALLCTX = CTX + SEGCTX
CH = 512
ROWS = 512
SCALE = 1.0 / math.sqrt(HD)
LOG2E = 1.4426950408889634
BF = jnp.bfloat16
F32 = jnp.float32
VM = pl.BlockSpec(memory_space=pltpu.VMEM)
VLIM = 60 * 2**20


def coords():
    b = lax.axis_index("branch")
    t = lax.axis_index("tensor")
    return t // 2, b // 2, lax.axis_index("dp") * 2 + b % 2, t % 2


def place(x, y, z, c):
    return {"dp": z // 2, "branch": y * 2 + z % 2, "tensor": x * 2 + c}


def rcopy(src, dst, ss, rs, dev):
    return pltpu.make_async_remote_copy(
        src_ref=src, dst_ref=dst, send_sem=ss, recv_sem=rs,
        device_id=dev, device_id_type=pl.DeviceIdType.MESH,
    )


def signal(sem, dev):
    pl.semaphore_signal(sem, inc=1, device_id=dev, device_id_type=pl.DeviceIdType.MESH)


def nt_dot(a, b):
    return lax.dot_general(a, b, (((1,), (1,)), ((), ())), preferred_element_type=F32)


class GatherRing:
    def __init__(self, me, dev, view, ss, rs):
        self.me, self.dev, self.view, self.ss, self.rs = me, dev, view, ss, rs

    def copy(self, node, piece, kind, step):
        v = self.view(node, piece)
        i = kind * 2 + piece
        return rcopy(v, v, self.ss.at[i], self.rs.at[i], self.dev(step))

    def right(self, p):
        return self.copy(self.me, p, 0, 1)

    def left(self, p):
        return self.copy(self.me, p, 1, 3)

    def fwd(self, p):
        if p == 0:
            return self.copy((self.me + 3) % 4, 0, 2, 1)
        return self.copy((self.me + 1) % 4, 1, 2, 3)

    def send(self, p):
        self.right(p).start()
        self.left(p).start()

    def forward(self, p):
        (self.right if p == 0 else self.left)(p).wait_recv()
        self.fwd(p).start()

    def wait_near(self):
        self.right(1).wait_recv()
        self.left(0).wait_recv()

    def wait_far(self):
        self.fwd(0).wait_recv()
        self.fwd(1).wait_recv()

    def wait_sends(self):
        for p in range(2):
            self.right(p).wait_send()
            self.left(p).wait_send()
            self.fwd(p).wait_send()


class SumRing:
    def __init__(self, dev, sb, rb, ss, rs):
        self.dev, self.sb, self.rb, self.ss, self.rs = dev, sb, rb, ss, rs

    def copy(self, i):
        return rcopy(self.sb.at[i], self.rb.at[i], self.ss.at[i], self.rs.at[i], self.dev(1 if i % 2 == 0 else 3))

    def send(self, i, value):
        self.sb[i] = value.astype(BF)
        self.copy(i).start()

    def add_send(self, i, value):
        self.copy(i - 4).wait_recv()
        self.send(i, value + self.rb[i - 4].astype(F32))

    def wait_result(self):
        for i in range(2, 6):
            self.copy(i).wait_recv()

    def result(self, p, own):
        a, b = ((4, 3), (2, 5))[p]
        return own + self.rb[a].astype(F32) + self.rb[b].astype(F32)

    def wait_sends(self):
        for i in range(6):
            self.copy(i).wait_send()


def whole_kernel(
    anc, up, adv, w, pk, pv, sk, sv, q,
    odq, okv, owg,
    cot, cotb, cott, wg, kvg, kcs, vcs,
    dsb, drb, dnear, dattn,
    s_f, p_b, p_s, attng, il_b, delta, qt, dos, dost, dqa,
    acc, accs, segt, ksb, krb, zsb, zrb, kown,
    gsb, grb, gnear,
    c_s, c_r, x_s, x_r, b_s, b_r, w_s, w_r, kz_s, kz_r, k_s, k_r,
    d_s, d_r, a_s, a_r, r_s, r_r, zk_s, zk_r, g_s, g_r,
):
    x, y, z, c = coords()
    zl = z % 2
    first = lax.axis_index("branch") * 2
    target_y = 2 * (x % 2) + c
    is_recv = c == y % 2
    is_src = target_y == y
    half = x // 2
    sib = place(x, y, z, 1 - c)
    cexp = SCALE * LOG2E

    def ydev(d):
        return place(x, (y + d) % 4, z, c)

    def zdev(d):
        return place(x, y, (z + d) % 4, c)

    bar = pltpu.get_barrier_semaphore()
    for d in range(1, 4):
        signal(bar, ydev(d))
    signal(bar, zdev(1))
    signal(bar, zdev(3))
    signal(bar, sib)

    @pl.when(is_recv)
    def _():
        for h in range(2):
            sx = 2 * h + y // 2

            @pl.when(sx != x)
            def _():
                signal(bar, place(sx, y, z, c))

    rows_b = lambda b: pl.ds(pl.multiple_of(b * 256, 256), 256)
    own_rows = rows_b(y * 2 + zl)
    for i, r in enumerate((pk, pv, sk, sv)):
        kvg[i, own_rows, :] = r[...]
    wrow = jnp.broadcast_to(adv[...].astype(F32) * 0.25, (TOKL, TOKL))
    ri = lax.broadcasted_iota(jnp.int32, (TOKL, TOKL), 0)
    ci = lax.broadcasted_iota(jnp.int32, (TOKL, TOKL), 1)
    diag = jnp.where(ri == ci, wrow, 0.0).astype(BF)
    cot[...] = jnp.dot(diag, up[...], preferred_element_type=F32).astype(BF)
    w_half = WROWS // 2
    wview = lambda n, p: wg.at[pl.ds(pl.multiple_of(n * WROWS + p * w_half, 32), w_half)]
    wg[pl.ds(pl.multiple_of(z * WROWS, 64), WROWS), :] = w[...]

    pl.semaphore_wait(bar, 6 + 3 * is_src.astype(jnp.int32))

    wring = GatherRing(z, zdev, wview, w_s, w_r)
    kring = GatherRing(y, ydev, lambda n, p: kvg.at[:, rows_b(n * 2 + p)], k_s, k_r)
    aring = GatherRing(
        y, ydev, lambda n, p: attng.at[pl.ds(pl.multiple_of(n * TOKL + p * SEG, SEG), SEG)], a_s, a_r)
    dring = SumRing(ydev, dsb, drb, d_s, d_r)
    rring = SumRing(ydev, ksb, krb, r_s, r_r)
    gring = SumRing(zdev, gsb, grb, g_s, g_r)

    def kz():
        v = kvg.at[:, own_rows]
        return rcopy(v, v, kz_s, kz_r, place(x, y, z + 1 - 2 * zl, c))

    def cy():
        return rcopy(cot, cotb.at[half, y], c_s, c_r.at[y], place(x, target_y, z, c))

    def cx(yy, d):
        v = cotb.at[half, yy]
        return rcopy(v, v, x_s.at[yy, d - 1], x_r.at[half, yy], place((x + d) % 4, y, z, c))

    def cb(h, yy):
        v = cotb.at[h, yy]
        return rcopy(v, v, b_s.at[h, yy], b_r.at[h, yy], sib)

    kz().start()

    @pl.when(jnp.logical_not(is_src))
    def _():
        cy().start()

    kring.send(zl)
    for p in range(2):
        wring.send(p)

    @pl.when(is_src)
    def _():
        cotb[half, y] = cot[...]
        for k in range(4):
            yy = (y + (0, 1, 3, 2)[k]) % 4
            if k > 0:
                rcopy(cot, cotb.at[half, yy], c_s, c_r.at[yy], sib).wait_recv()
            for d in (1, 3, 2):
                cx(yy, d).start()
            cb(half, yy).start()

    kz().wait_recv()
    kring.send(1 - zl)

    @pl.when(is_recv)
    def _():
        for yy in range(4):
            for h in range(2):
                @pl.when(jnp.logical_not(is_src & (half == h)))
                def _():
                    v = cotb.at[h, yy]
                    rcopy(v, v, b_s.at[h, yy], x_r.at[h, yy], sib).wait_recv()
                    cb(h, yy).start()

    for p in range(2):
        kring.forward(p)
    for p in range(2):
        wring.forward(p)
    kring.wait_near()
    kring.wait_far()

    named = [[jnp.broadcast_to(anc[0, pl.ds(first + s, 1), i:i + 1], (1, HD)) for i in range(2)] for s in range(2)]

    def hot(s, i, j):
        return (named[s][i] == j).astype(F32)

    for s in range(2):
        own_seg = pl.ds(pl.multiple_of((first + s) * SEG, SEG), SEG)
        for k, dst in enumerate((kcs, vcs)):
            for i in range(2):
                tot = None
                for j in range(16):
                    v = kvg[2 + k, j * SEG:(j + 1) * SEG, :].astype(F32) * hot(s, i, j)
                    tot = v if tot is None else tot + v
                dst[s, i * SEG:(i + 1) * SEG, :] = tot.astype(BF)
            dst[s, 2 * SEG:, :] = kvg[2 + k, own_seg, :]

    nh = ROWS // SEG

    def forward(rb):
        s, hb = rb // 2, rb % 2
        tok = slice(s * SEG, (s + 1) * SEG)
        rows = slice(rb * ROWS, (rb + 1) * ROWS)
        col = lax.broadcasted_iota(jnp.int32, (ROWS, SEG), 1)
        row = lax.broadcasted_iota(jnp.int32, (ROWS, SEG), 0) % SEG
        shut = [jnp.where(named[s][i] >= 0, 0.0, -1e30) for i in range(2)]
        shut.append(jnp.where(col <= row, 0.0, -1e30))
        heads = [slice((hb * nh + i) * HD, (hb * nh + i + 1) * HD) for i in range(nh)]
        qb = jnp.concatenate([q[tok, h] for h in heads], axis=0)
        qt[rb] = qb.T
        mx = None
        for j in range(5):
            kc = kvg[0, j * CH:(j + 1) * CH, :] if j < 4 else kcs[s]
            sc = nt_dot(qb, kc)
            n = sc.shape[1]
            if j == 4:
                sc = jnp.concatenate([sc[:, i * SEG:(i + 1) * SEG] + shut[i] for i in range(3)], axis=1)
            s_f[:, j * CH:j * CH + n] = sc
            for t in range(n // 128):
                part = sc[:, t * 128:(t + 1) * 128]
                mx = part if mx is None else jnp.maximum(mx, part)
        m = jnp.max(mx, axis=1, keepdims=True)
        lsum = None
        o = None
        for j in range(5):
            vc = kvg[1, j * CH:(j + 1) * CH, :] if j < 4 else vcs[s]
            n = vc.shape[0]
            p = jnp.exp2((s_f[:, j * CH:j * CH + n] - m) * cexp)
            for t in range(n // 128):
                part = p[:, t * 128:(t + 1) * 128]
                lsum = part if lsum is None else lsum + part
            pb = p.astype(BF)
            if j < 4:
                p_b[j, rows, :] = pb
            else:
                p_s[rows, :] = pb
            oc = jnp.dot(pb, vc, preferred_element_type=F32)
            o = oc if o is None else o + oc
        il = jnp.broadcast_to(1.0 / jnp.sum(lsum, axis=1, keepdims=True), (ROWS, HD))
        il_b[rows, :] = il
        ob = (o * il).astype(BF)
        for i, h in enumerate(heads):
            attng[pl.ds(pl.multiple_of(y * TOKL + s * SEG, SEG), SEG), h] = ob[i * SEG:(i + 1) * SEG]

    forward(0)

    wring.wait_near()
    wring.wait_far()

    @pl.when(jnp.logical_not(is_recv))
    def _():
        for h in range(2):
            for yy in range(4):
                cb(h, yy).wait_recv()

    def proj(yy, rows):
        return jnp.dot(cotb[0, yy, rows, :], wg[0:UCOL, :], preferred_element_type=F32) + jnp.dot(
            cotb[1, yy, rows, :], wg[UCOL:2 * UCOL, :], preferred_element_type=F32)

    lo, hi = slice(0, SEG), slice(SEG, 2 * SEG)
    dring.send(0, proj((y + 2) % 4, lo))
    dring.send(1, proj((y + 2) % 4, hi))
    dring.send(2, proj((y + 1) % 4, hi))
    dring.send(3, proj((y + 3) % 4, lo))
    dnear[0] = proj((y + 1) % 4, lo)
    dnear[1] = proj((y + 3) % 4, hi)
    dnear[2] = proj(y, lo)
    dnear[3] = proj(y, hi)

    forward(1)
    dring.add_send(4, dnear[0])
    dring.add_send(5, dnear[1])
    aring.send(0)
    forward(2)
    forward(3)
    aring.send(1)
    for h in range(2):
        for yy in range(4):
            cott[h * UCOL:(h + 1) * UCOL, yy * TOKL:(yy + 1) * TOKL] = cotb[h, yy].T

    dring.wait_result()
    for p in range(2):
        dattn[p * SEG:(p + 1) * SEG, :] = dring.result(p, dnear[2 + p]).astype(BF)
    for rb in range(4):
        s, hb = rb // 2, rb % 2
        rows = slice(rb * ROWS, (rb + 1) * ROWS)
        tok = slice(s * SEG, (s + 1) * SEG)
        arow = pl.ds(pl.multiple_of(y * TOKL + s * SEG, SEG), SEG)
        heads = [slice((hb * nh + i) * HD, (hb * nh + i + 1) * HD) for i in range(nh)]
        dob = jnp.concatenate([dattn[tok, h] for h in heads], axis=0)
        at = jnp.concatenate([attng[arow, h] for h in heads], axis=0)
        db = (dob.astype(F32) * il_b[rows, :]).astype(BF)
        dos[rows, :] = db
        dost[rb] = db.T
        dl = jnp.sum(db.astype(F32) * at.astype(F32), axis=1, keepdims=True)
        delta[rows, :] = jnp.broadcast_to(dl, (ROWS, HD))

    aring.forward(0)

    def back(rb, kc, vc, pb):
        rows = pl.ds(pl.multiple_of(rb * ROWS, ROWS), ROWS)
        dl = delta[rows, :]
        n = vc.shape[0]
        dp = nt_dot(dos[rows, :], vc)
        ds = (pb.astype(F32) * (dp - jnp.concatenate([dl] * (n // HD), axis=1))).astype(BF)
        return (rows, jnp.dot(ds, kc, preferred_element_type=F32),
                jnp.dot(qt[rb], ds, preferred_element_type=F32),
                jnp.dot(dost[rb], pb, preferred_element_type=F32))

    for rb in range(4):
        s = rb // 2
        rows, dqc, dk, dv = back(rb, kcs[s], vcs[s], p_s[rb * ROWS:(rb + 1) * ROWS, :])
        dqa[rows, :] = dqc
        if rb % 2 == 0:
            accs[s, 0] = dk
            accs[s, 1] = dv
        else:
            accs[s, 0] += dk
            accs[s, 1] += dv
    for j in range(16):
        for k in range(2):
            tot = None
            for s in range(2):
                for i in range(2):
                    v = accs[s, k, :, i * SEG:(i + 1) * SEG] * hot(s, i, j)
                    tot = v if tot is None else tot + v
            segt[j // 4, k, :, (j % 4) * SEG:(j % 4 + 1) * SEG] = tot
    for s in range(2):
        own_cols = pl.ds(pl.multiple_of((zl * 2 + s) * SEG, SEG), SEG)
        for k in range(2):
            segt[y, k, :, own_cols] += accs[s, k, :, 2 * SEG:]
    rring.send(0, segt[(y + 2) % 4])
    rring.send(3, segt[(y + 3) % 4])

    def prefix(j):
        acc[...] = jnp.zeros_like(acc)
        crow = pl.ds(pl.multiple_of(j * CH, CH), CH)

        @pl.loop(0, 4)
        def _(rb):
            rows = pl.ds(pl.multiple_of(rb * ROWS, ROWS), ROWS)
            _, dqc, dk, dv = back(rb, kvg[0, crow, :], kvg[1, crow, :], p_b[j, rows, :])
            dqa[rows, :] += dqc
            acc[0] += dk
            acc[1] += dv

    prefix((y + 2) % 4)
    rring.send(1, acc[...])
    aring.forward(1)
    prefix((y + 1) % 4)
    rring.send(2, acc[...])
    rring.add_send(4, segt[(y + 1) % 4])
    prefix((y + 3) % 4)
    rring.add_send(5, acc[...])

    aring.wait_near()
    aring.wait_far()

    def wgrad(zz, p):
        rows = pl.ds(pl.multiple_of(zz * WROWS + p * w_half, 32), w_half)
        return jnp.dot(cott[rows, :], attng[...], preferred_element_type=F32)

    gring.send(0, wgrad((z + 2) % 4, 0))
    gring.send(1, wgrad((z + 2) % 4, 1))
    gring.send(2, wgrad((z + 1) % 4, 1))
    gring.send(3, wgrad((z + 3) % 4, 0))
    gnear[0] = wgrad((z + 1) % 4, 0)
    gnear[1] = wgrad((z + 3) % 4, 1)

    prefix(y)
    for rb in range(4):
        s, hb = rb // 2, rb % 2
        dqb = (dqa[rb * ROWS:(rb + 1) * ROWS, :] * SCALE).astype(BF)
        for i in range(nh):
            odq[s * SEG:(s + 1) * SEG, (hb * nh + i) * HD:(hb * nh + i + 1) * HD] = dqb[i * SEG:(i + 1) * SEG]

    gring.add_send(4, gnear[0])
    gring.add_send(5, gnear[1])
    for p in range(2):
        owg[p * w_half:(p + 1) * w_half, :] = wgrad(z, p)

    rring.wait_result()
    kown[0:2] = rring.result(1, acc[...])
    kown[2:4] = rring.result(0, segt[y])
    lanes = lambda v: pl.ds(pl.multiple_of(v * 256, 256), 256)
    zsb[...] = kown[:, :, lanes(1 - zl)].astype(BF)

    def zk():
        return rcopy(zsb, zrb, zk_s, zk_r, place(x, y, z + 1 - 2 * zl, c))

    zk().start()
    zk().wait_recv()
    for i in range(4):
        t = kown[i, :, lanes(zl)] + zrb[i].astype(F32)
        if i % 2 == 0:
            t = t * SCALE
        okv[i] = t.T.astype(BF)

    gring.wait_result()
    for p in range(2):
        rows = slice(p * w_half, (p + 1) * w_half)
        owg[rows, :] = gring.result(p, owg[rows, :])

    kz().wait_send()
    zk().wait_send()

    @pl.when(jnp.logical_not(is_src))
    def _():
        cy().wait_send()

    @pl.when(is_src)
    def _():
        for yy in range(4):
            for d in range(1, 4):
                cx(yy, d).wait_send()

    @pl.when(is_recv)
    def _():
        for h in range(2):
            for yy in range(4):
                cb(h, yy).wait_send()

    for ring in (wring, kring, aring, dring, rring, gring):
        ring.wait_sends()


def finish_kernel(dq, kv, wgr, o0, o1, o2, o3, o4, o5):
    o0[...] = dq[...]
    for i, o in enumerate((o1, o2, o3, o4)):
        o[...] = kv[i]
    o5[...] = wgr[...]


def on_device(
    queries, prefix_keys, prefix_values, keys, values, ancestors, advantages, upstream, out_weight
):
    dma = pltpu.SemaphoreType.DMA
    sds = jax.ShapeDtypeStruct
    vm = pltpu.VMEM
    half_w = WROWS // 2
    dq, okv, owg = pl.pallas_call(
        whole_kernel,
        out_shape=(
            sds((TOKL, NCOL), BF),
            sds((4, 256, HD), BF),
            sds((WROWS, NCOL), F32),
        ),
        in_specs=[VM] * 9,
        out_specs=(VM, VM, VM),
        scratch_shapes=[
            vm((TOKL, UCOL), BF),
            vm((2, 4, TOKL, UCOL), BF),
            vm((2 * UCOL, 4 * TOKL), BF),
            vm((4 * WROWS, NCOL), BF),
            vm((4, CTX, HD), BF),
            vm((2, SEGCTX, HD), BF),
            vm((2, SEGCTX, HD), BF),
            vm((6, SEG, NCOL), BF),
            vm((6, SEG, NCOL), BF),
            vm((4, SEG, NCOL), F32),
            vm((TOKL, NCOL), BF),
            vm((ROWS, ALLCTX), F32),
            vm((4, 4 * ROWS, CH), BF),
            vm((4 * ROWS, SEGCTX), BF),
            vm((4 * TOKL, NCOL), BF),
            vm((4 * ROWS, HD), F32),
            vm((4 * ROWS, HD), F32),
            vm((4, HD, ROWS), BF),
            vm((4 * ROWS, HD), BF),
            vm((4, HD, ROWS), BF),
            vm((4 * ROWS, HD), F32),
            vm((2, HD, CH), F32),
            vm((2, 2, HD, SEGCTX), F32),
            vm((4, 2, HD, CH), F32),
            vm((6, 2, HD, CH), BF),
            vm((6, 2, HD, CH), BF),
            vm((4, HD, 256), BF),
            vm((4, HD, 256), BF),
            vm((4, HD, CH), F32),
            vm((6, half_w, NCOL), BF),
            vm((6, half_w, NCOL), BF),
            vm((2, half_w, NCOL), F32),
            dma, dma((4,)), dma((4, 3)), dma((2, 4)), dma((2, 4)), dma((2, 4)),
            dma((6,)), dma((6,)), dma, dma, dma((6,)), dma((6,)),
            dma((6,)), dma((6,)), dma((6,)), dma((6,)), dma((6,)), dma((6,)),
            dma, dma, dma((6,)), dma((6,)),
        ],
        compiler_params=pltpu.CompilerParams(
            collective_id=0, has_side_effects=True, vmem_limit_bytes=VLIM),
        name="whole",
    )(ancestors, upstream[0], advantages, out_weight, prefix_keys[0], prefix_values[0], keys[0], values[0],
      queries[0])
    outs = pl.pallas_call(
        finish_kernel,
        out_shape=tuple([sds((TOKL, NCOL), BF)] + [sds((256, HD), BF)] * 4 + [sds((WROWS, NCOL), F32)]),
        in_specs=[VM] * 3,
        out_specs=tuple([VM] * 6),
        name="finish",
    )(dq, okv, owg)
    return tuple(o[None] for o in outs[:5]) + (outs[5],)


def solution(mesh):
    return jax.shard_map(
        on_device,
        mesh=mesh,
        in_specs=(
            P("dp", "branch", "tensor"),
            P("dp", "branch", "tensor"),
            P("dp", "branch", "tensor"),
            P("dp", "branch", "tensor"),
            P("dp", "branch", "tensor"),
            P("dp", None, None),
            P("dp", "branch"),
            P("dp", "branch", "tensor"),
            P(("dp", "branch"), "tensor"),
        ),
        out_specs=(
            P("dp", "branch", "tensor"),
            P("dp", "branch", "tensor"),
            P("dp", "branch", "tensor"),
            P("dp", "branch", "tensor"),
            P("dp", "branch", "tensor"),
            P(("dp", "branch"), "tensor"),
        ),
        check_vma=False,
    )
```

```python
import math

import jax
import jax.numpy as jnp
from jax import lax
from jax.experimental import pallas as pl
from jax.experimental.pallas import tpu as pltpu
from jax.sharding import PartitionSpec as P

HD = 128
SEG = 128
GROUP = 8
TOKL = 256
KVB = 8
WROWS = 320
NCOL = 1024
UCOL = 640
CTX = 2048
SEGCTX = 384
ALLCTX = CTX + SEGCTX
CH = 512
ROWS = 512
SCALE = 1.0 / math.sqrt(HD)
LOG2E = 1.4426950408889634
BF = jnp.bfloat16
F32 = jnp.float32
VM = pl.BlockSpec(memory_space=pltpu.VMEM)
VLIM = 60 * 2**20


def coords():
    b = lax.axis_index("branch")
    t = lax.axis_index("tensor")
    return t // 2, b // 2, lax.axis_index("dp") * 2 + b % 2, t % 2


def place(x, y, z, c):
    return {"dp": z // 2, "branch": y * 2 + z % 2, "tensor": x * 2 + c}


def rcopy(src, dst, ss, rs, dev):
    return pltpu.make_async_remote_copy(
        src_ref=src, dst_ref=dst, send_sem=ss, recv_sem=rs,
        device_id=dev, device_id_type=pl.DeviceIdType.MESH,
    )


def signal(sem, dev):
    pl.semaphore_signal(sem, inc=1, device_id=dev, device_id_type=pl.DeviceIdType.MESH)


def nt_dot(a, b):
    return lax.dot_general(a, b, (((1,), (1,)), ((), ())), preferred_element_type=F32)


class GatherRing:
    def __init__(self, me, dev, view, ss, rs):
        self.me, self.dev, self.view, self.ss, self.rs = me, dev, view, ss, rs

    def copy(self, node, piece, kind, step):
        v = self.view(node, piece)
        i = kind * 2 + piece
        return rcopy(v, v, self.ss.at[i], self.rs.at[i], self.dev(step))

    def right(self, p):
        return self.copy(self.me, p, 0, 1)

    def left(self, p):
        return self.copy(self.me, p, 1, 3)

    def fwd(self, p):
        if p == 0:
            return self.copy((self.me + 3) % 4, 0, 2, 1)
        return self.copy((self.me + 1) % 4, 1, 2, 3)

    def send(self, p):
        self.right(p).start()
        self.left(p).start()

    def forward(self, p):
        (self.right if p == 0 else self.left)(p).wait_recv()
        self.fwd(p).start()

    def wait_near(self):
        self.right(1).wait_recv()
        self.left(0).wait_recv()

    def wait_far(self):
        self.fwd(0).wait_recv()
        self.fwd(1).wait_recv()

    def wait_sends(self):
        for p in range(2):
            self.right(p).wait_send()
            self.left(p).wait_send()
            self.fwd(p).wait_send()


class SumRing:
    def __init__(self, dev, sb, rb, ss, rs):
        self.dev, self.sb, self.rb, self.ss, self.rs = dev, sb, rb, ss, rs

    def copy(self, i):
        return rcopy(self.sb.at[i], self.rb.at[i], self.ss.at[i], self.rs.at[i], self.dev(1 if i % 2 == 0 else 3))

    def send(self, i, value):
        self.sb[i] = value.astype(BF)
        self.copy(i).start()

    def add_send(self, i, value):
        self.copy(i - 4).wait_recv()
        self.send(i, value + self.rb[i - 4].astype(F32))

    def wait_result(self):
        for i in range(2, 6):
            self.copy(i).wait_recv()

    def result(self, p, own):
        a, b = ((4, 3), (2, 5))[p]
        return own + self.rb[a].astype(F32) + self.rb[b].astype(F32)

    def wait_sends(self):
        for i in range(6):
            self.copy(i).wait_send()


def whole_kernel(
    anc, up, adv, w, pk, pv, sk, sv, q,
    odq, okv, owg,
    cot, cotb, cott, wg, kvg, kcs, vcs,
    dsb, drb, dnear, dattn,
    s_f, p_b, p_s, attng, il_b, delta, qt, dos, dost, dqa,
    acc, accs, segt, ksb, krb, zsb, zrb, kown,
    gsb, grb, gnear,
    c_s, c_r, x_s, x_r, b_s, b_r, w_s, w_r, kz_s, kz_r, k_s, k_r,
    d_s, d_r, a_s, a_r, r_s, r_r, zk_s, zk_r, g_s, g_r,
):
    x, y, z, c = coords()
    zl = z % 2
    first = lax.axis_index("branch") * 2
    target_y = 2 * (x % 2) + c
    is_recv = c == y % 2
    is_src = target_y == y
    half = x // 2
    sib = place(x, y, z, 1 - c)
    cexp = SCALE * LOG2E

    def ydev(d):
        return place(x, (y + d) % 4, z, c)

    def zdev(d):
        return place(x, y, (z + d) % 4, c)

    def xdev(d):
        return place((x + d) % 4, y, z, c)

    bar = pltpu.get_barrier_semaphore()
    for d in range(1, 4):
        signal(bar, ydev(d))
    signal(bar, zdev(1))
    signal(bar, zdev(3))
    signal(bar, sib)

    @pl.when(is_recv)
    def _():
        signal(bar, xdev(1))
        signal(bar, xdev(3))

    rows_b = lambda b: pl.ds(pl.multiple_of(b * 256, 256), 256)
    own_rows = rows_b(y * 2 + zl)
    for i, r in enumerate((pk, pv, sk, sv)):
        kvg[i, own_rows, :] = r[...]
    wrow = jnp.broadcast_to(adv[...].astype(F32) * 0.25, (TOKL, TOKL))
    ri = lax.broadcasted_iota(jnp.int32, (TOKL, TOKL), 0)
    ci = lax.broadcasted_iota(jnp.int32, (TOKL, TOKL), 1)
    diag = jnp.where(ri == ci, wrow, 0.0).astype(BF)
    cot[...] = jnp.dot(diag, up[...], preferred_element_type=F32).astype(BF)
    w_half = WROWS // 2
    wview = lambda n, p: wg.at[pl.ds(pl.multiple_of(n * WROWS + p * w_half, 32), w_half)]
    wg[pl.ds(pl.multiple_of(z * WROWS, 64), WROWS), :] = w[...]

    pl.semaphore_wait(bar, 6 + 2 * is_recv.astype(jnp.int32))

    wring = GatherRing(z, zdev, wview, w_s, w_r)
    kring = GatherRing(y, ydev, lambda n, p: kvg.at[:, rows_b(n * 2 + p)], k_s, k_r)
    aring = GatherRing(
        y, ydev, lambda n, p: attng.at[pl.ds(pl.multiple_of(n * TOKL + p * SEG, SEG), SEG)], a_s, a_r)
    dring = SumRing(ydev, dsb, drb, d_s, d_r)
    rring = SumRing(ydev, ksb, krb, r_s, r_r)
    gring = SumRing(zdev, gsb, grb, g_s, g_r)

    def kz():
        v = kvg.at[:, own_rows]
        return rcopy(v, v, kz_s, kz_r, place(x, y, z + 1 - 2 * zl, c))

    def cy():
        return rcopy(cot, cotb.at[half, y], c_s, c_r.at[y], place(x, target_y, z, c))

    def cx(h, yy, k):
        v = cotb.at[h, yy]
        return rcopy(v, v, x_s.at[yy, k], x_r.at[h, yy], xdev((1, 3)[k]))

    def cb(h, yy):
        v = cotb.at[h, yy]
        return rcopy(v, v, b_s.at[h, yy], b_r.at[h, yy], sib)

    is_mid = is_recv & jnp.logical_not(is_src)
    left_half = ((x + 3) % 4) // 2
    right_half = ((x + 1) % 4) // 2

    def mid_block(d):
        yy = (y + d) % 4
        cx(left_half, yy, 0).wait_recv()

        @pl.when(yy < 2)
        def _():
            cx(left_half, yy, 0).start()

        cb(left_half, yy).start()
        cx(right_half, yy, 1).wait_recv()

        @pl.when(yy >= 2)
        def _():
            cx(right_half, yy, 1).start()

        cb(right_half, yy).start()

    kz().start()

    @pl.when(jnp.logical_not(is_src))
    def _():
        cy().start()

    kring.send(zl)

    @pl.when(zl == 0)
    def _():
        for p in range(2):
            wring.left(p).start()

    @pl.when(zl == 1)
    def _():
        for p in range(2):
            wring.right(p).start()

    @pl.when(is_src)
    def _():
        cotb[half, y] = cot[...]
        for k in range(2):
            cx(half, y, k).start()
        cb(half, y).start()

    kz().wait_recv()
    kring.send(1 - zl)

    @pl.when(zl == 0)
    def _():
        for p in range(2):
            wring.right(p).start()

    @pl.when(zl == 1)
    def _():
        for p in range(2):
            wring.left(p).start()

    @pl.when(is_src)
    def _():
        for d in (1, 3, 2):
            yy = (y + d) % 4
            rcopy(cot, cotb.at[half, yy], c_s, c_r.at[yy], sib).wait_recv()
            for k in range(2):
                cx(half, yy, k).start()
            cb(half, yy).start()

    @pl.when(is_mid)
    def _():
        mid_block(0)
        mid_block(1)

    for p in range(2):
        kring.forward(p)

    @pl.when(is_mid)
    def _():
        mid_block(3)
        mid_block(2)

    for p in range(2):
        wring.forward(p)
    kring.wait_near()
    kring.wait_far()

    named = [[jnp.broadcast_to(anc[0, pl.ds(first + s, 1), i:i + 1], (1, HD)) for i in range(2)] for s in range(2)]

    def hot(s, i, j):
        return (named[s][i] == j).astype(F32)

    for s in range(2):
        own_seg = pl.ds(pl.multiple_of((first + s) * SEG, SEG), SEG)
        for k, dst in enumerate((kcs, vcs)):
            for i in range(2):
                tot = None
                for j in range(16):
                    v = kvg[2 + k, j * SEG:(j + 1) * SEG, :].astype(F32) * hot(s, i, j)
                    tot = v if tot is None else tot + v
                dst[s, i * SEG:(i + 1) * SEG, :] = tot.astype(BF)
            dst[s, 2 * SEG:, :] = kvg[2 + k, own_seg, :]

    nh = ROWS // SEG

    def forward(rb):
        s, hb = rb // 2, rb % 2
        tok = slice(s * SEG, (s + 1) * SEG)
        rows = slice(rb * ROWS, (rb + 1) * ROWS)
        col = lax.broadcasted_iota(jnp.int32, (ROWS, SEG), 1)
        row = lax.broadcasted_iota(jnp.int32, (ROWS, SEG), 0) % SEG
        shut = [jnp.where(named[s][i] >= 0, 0.0, -1e30) for i in range(2)]
        shut.append(jnp.where(col <= row, 0.0, -1e30))
        heads = [slice((hb * nh + i) * HD, (hb * nh + i + 1) * HD) for i in range(nh)]
        qb = jnp.concatenate([q[tok, h] for h in heads], axis=0)
        qt[rb] = qb.T
        mx = None
        for j in range(5):
            kc = kvg[0, j * CH:(j + 1) * CH, :] if j < 4 else kcs[s]
            sc = nt_dot(qb, kc)
            n = sc.shape[1]
            if j == 4:
                sc = jnp.concatenate([sc[:, i * SEG:(i + 1) * SEG] + shut[i] for i in range(3)], axis=1)
            s_f[:, j * CH:j * CH + n] = sc
            for t in range(n // 128):
                part = sc[:, t * 128:(t + 1) * 128]
                mx = part if mx is None else jnp.maximum(mx, part)
        m = jnp.max(mx, axis=1, keepdims=True)
        lsum = None
        o = None
        for j in range(5):
            vc = kvg[1, j * CH:(j + 1) * CH, :] if j < 4 else vcs[s]
            n = vc.shape[0]
            p = jnp.exp2((s_f[:, j * CH:j * CH + n] - m) * cexp)
            for t in range(n // 128):
                part = p[:, t * 128:(t + 1) * 128]
                lsum = part if lsum is None else lsum + part
            pb = p.astype(BF)
            if j < 4:
                p_b[j, rows, :] = pb
            else:
                p_s[rows, :] = pb
            oc = jnp.dot(pb, vc, preferred_element_type=F32)
            o = oc if o is None else o + oc
        il = jnp.broadcast_to(1.0 / jnp.sum(lsum, axis=1, keepdims=True), (ROWS, HD))
        il_b[rows, :] = il
        ob = (o * il).astype(BF)
        for i, h in enumerate(heads):
            attng[pl.ds(pl.multiple_of(y * TOKL + s * SEG, SEG), SEG), h] = ob[i * SEG:(i + 1) * SEG]

    forward(0)
    forward(1)
    aring.send(0)
    forward(2)

    @pl.when(is_src)
    def _():
        for d in (0, 1, 3, 2):
            cx(1 - half, (y + d) % 4, 0).wait_recv()
            cb(1 - half, (y + d) % 4).start()

    forward(3)
    aring.send(1)

    wring.wait_near()
    wring.wait_far()

    @pl.when(jnp.logical_not(is_recv))
    def _():
        for h in range(2):
            for yy in range(4):
                cb(h, yy).wait_recv()

    def proj(yy, rows):
        return jnp.dot(cotb[0, yy, rows, :], wg[0:UCOL, :], preferred_element_type=F32) + jnp.dot(
            cotb[1, yy, rows, :], wg[UCOL:2 * UCOL, :], preferred_element_type=F32)

    lo, hi = slice(0, SEG), slice(SEG, 2 * SEG)
    dring.send(0, proj((y + 2) % 4, lo))
    dring.send(1, proj((y + 2) % 4, hi))
    dring.send(2, proj((y + 1) % 4, hi))
    dring.send(3, proj((y + 3) % 4, lo))
    dnear[0] = proj((y + 1) % 4, lo)
    dnear[1] = proj((y + 3) % 4, hi)
    dnear[2] = proj(y, lo)
    dnear[3] = proj(y, hi)

    for h in range(2):
        for yy in range(4):
            cott[h * UCOL:(h + 1) * UCOL, yy * TOKL:(yy + 1) * TOKL] = cotb[h, yy].T
    for p in range(2):
        aring.forward(p)
    dring.add_send(4, dnear[0])
    dring.add_send(5, dnear[1])

    aring.wait_near()
    aring.wait_far()

    def wgrad(zz, p):
        rows = pl.ds(pl.multiple_of(zz * WROWS + p * w_half, 32), w_half)
        return jnp.dot(cott[rows, :], attng[...], preferred_element_type=F32)

    gring.send(0, wgrad((z + 2) % 4, 0))
    gring.send(1, wgrad((z + 2) % 4, 1))
    gring.send(2, wgrad((z + 1) % 4, 1))
    gring.send(3, wgrad((z + 3) % 4, 0))
    gnear[0] = wgrad((z + 1) % 4, 0)
    gnear[1] = wgrad((z + 3) % 4, 1)

    dring.wait_result()
    for p in range(2):
        dattn[p * SEG:(p + 1) * SEG, :] = dring.result(p, dnear[2 + p]).astype(BF)
    for rb in range(4):
        s, hb = rb // 2, rb % 2
        rows = slice(rb * ROWS, (rb + 1) * ROWS)
        tok = slice(s * SEG, (s + 1) * SEG)
        arow = pl.ds(pl.multiple_of(y * TOKL + s * SEG, SEG), SEG)
        heads = [slice((hb * nh + i) * HD, (hb * nh + i + 1) * HD) for i in range(nh)]
        dob = jnp.concatenate([dattn[tok, h] for h in heads], axis=0)
        at = jnp.concatenate([attng[arow, h] for h in heads], axis=0)
        db = (dob.astype(F32) * il_b[rows, :]).astype(BF)
        dos[rows, :] = db
        dost[rb] = db.T
        dl = jnp.sum(db.astype(F32) * at.astype(F32), axis=1, keepdims=True)
        delta[rows, :] = jnp.broadcast_to(dl, (ROWS, HD))

    def back(rb, kc, vc, pb):
        rows = pl.ds(pl.multiple_of(rb * ROWS, ROWS), ROWS)
        dl = delta[rows, :]
        n = vc.shape[0]
        dp = nt_dot(dos[rows, :], vc)
        ds = (pb.astype(F32) * (dp - jnp.concatenate([dl] * (n // HD), axis=1))).astype(BF)
        return (rows, jnp.dot(ds, kc, preferred_element_type=F32),
                jnp.dot(qt[rb], ds, preferred_element_type=F32),
                jnp.dot(dost[rb], pb, preferred_element_type=F32))

    for rb in range(4):
        s = rb // 2
        rows, dqc, dk, dv = back(rb, kcs[s], vcs[s], p_s[rb * ROWS:(rb + 1) * ROWS, :])
        dqa[rows, :] = dqc
        if rb % 2 == 0:
            accs[s, 0] = dk
            accs[s, 1] = dv
        else:
            accs[s, 0] += dk
            accs[s, 1] += dv
    for j in range(16):
        for k in range(2):
            tot = None
            for s in range(2):
                for i in range(2):
                    v = accs[s, k, :, i * SEG:(i + 1) * SEG] * hot(s, i, j)
                    tot = v if tot is None else tot + v
            segt[j // 4, k, :, (j % 4) * SEG:(j % 4 + 1) * SEG] = tot
    for s in range(2):
        own_cols = pl.ds(pl.multiple_of((zl * 2 + s) * SEG, SEG), SEG)
        for k in range(2):
            segt[y, k, :, own_cols] += accs[s, k, :, 2 * SEG:]
    rring.send(0, segt[(y + 2) % 4])
    rring.send(3, segt[(y + 3) % 4])

    def prefix(j):
        acc[...] = jnp.zeros_like(acc)
        crow = pl.ds(pl.multiple_of(j * CH, CH), CH)

        @pl.loop(0, 4)
        def _(rb):
            rows = pl.ds(pl.multiple_of(rb * ROWS, ROWS), ROWS)
            _, dqc, dk, dv = back(rb, kvg[0, crow, :], kvg[1, crow, :], p_b[j, rows, :])
            dqa[rows, :] += dqc
            acc[0] += dk
            acc[1] += dv

    prefix((y + 2) % 4)
    rring.send(1, acc[...])
    gring.add_send(4, gnear[0])
    gring.add_send(5, gnear[1])
    rring.add_send(4, segt[(y + 1) % 4])
    prefix((y + 1) % 4)
    rring.send(2, acc[...])
    prefix((y + 3) % 4)
    rring.add_send(5, acc[...])
    prefix(y)
    for rb in range(4):
        s, hb = rb // 2, rb % 2
        dqb = (dqa[rb * ROWS:(rb + 1) * ROWS, :] * SCALE).astype(BF)
        for i in range(nh):
            odq[s * SEG:(s + 1) * SEG, (hb * nh + i) * HD:(hb * nh + i + 1) * HD] = dqb[i * SEG:(i + 1) * SEG]

    for p in range(2):
        owg[p * w_half:(p + 1) * w_half, :] = wgrad(z, p)

    lanes = lambda v: pl.ds(pl.multiple_of(v * 256, 256), 256)

    def zk(p):
        return rcopy(zsb.at[p], zrb.at[p], zk_s.at[p], zk_r.at[p], place(x, y, z + 1 - 2 * zl, c))

    for p in range(2):
        for i in ((4, 3), (2, 5))[p]:
            rring.copy(i).wait_recv()
        kown[p] = rring.result(p, segt[y] if p == 0 else acc[...])
        zsb[p] = kown[p, :, :, lanes(1 - zl)].astype(BF)
        zk(p).start()

    gring.wait_result()
    for p in range(2):
        rows = slice(p * w_half, (p + 1) * w_half)
        owg[rows, :] = gring.result(p, owg[rows, :])

    for p in range(2):
        zk(p).wait_recv()
        for i in range(2):
            t = kown[p, i, :, lanes(zl)] + zrb[p, i].astype(F32)
            if i == 0:
                t = t * SCALE
            okv[2 * (1 - p) + i] = t.T.astype(BF)

    kz().wait_send()
    for p in range(2):
        zk(p).wait_send()

    @pl.when(jnp.logical_not(is_src))
    def _():
        cy().wait_send()

    @pl.when(is_src)
    def _():
        for yy in range(4):
            for k in range(2):
                cx(half, yy, k).wait_send()

    @pl.when(is_mid)
    def _():
        for yy in range(4):
            cx(0, yy, yy // 2).wait_send()

    @pl.when(is_recv)
    def _():
        for h in range(2):
            for yy in range(4):
                cb(h, yy).wait_send()

    for ring in (wring, kring, aring, dring, rring, gring):
        ring.wait_sends()


def finish_kernel(dq, kv, wgr, o0, o1, o2, o3, o4, o5):
    o0[...] = dq[...]
    for i, o in enumerate((o1, o2, o3, o4)):
        o[...] = kv[i]
    o5[...] = wgr[...]


def on_device(
    queries, prefix_keys, prefix_values, keys, values, ancestors, advantages, upstream, out_weight
):
    dma = pltpu.SemaphoreType.DMA
    sds = jax.ShapeDtypeStruct
    vm = pltpu.VMEM
    half_w = WROWS // 2
    dq, okv, owg = pl.pallas_call(
        whole_kernel,
        out_shape=(
            sds((TOKL, NCOL), BF),
            sds((4, 256, HD), BF),
            sds((WROWS, NCOL), F32),
        ),
        in_specs=[VM] * 9,
        out_specs=(VM, VM, VM),
        scratch_shapes=[
            vm((TOKL, UCOL), BF),
            vm((2, 4, TOKL, UCOL), BF),
            vm((2 * UCOL, 4 * TOKL), BF),
            vm((4 * WROWS, NCOL), BF),
            vm((4, CTX, HD), BF),
            vm((2, SEGCTX, HD), BF),
            vm((2, SEGCTX, HD), BF),
            vm((6, SEG, NCOL), BF),
            vm((6, SEG, NCOL), BF),
            vm((4, SEG, NCOL), F32),
            vm((TOKL, NCOL), BF),
            vm((ROWS, ALLCTX), F32),
            vm((4, 4 * ROWS, CH), BF),
            vm((4 * ROWS, SEGCTX), BF),
            vm((4 * TOKL, NCOL), BF),
            vm((4 * ROWS, HD), F32),
            vm((4 * ROWS, HD), F32),
            vm((4, HD, ROWS), BF),
            vm((4 * ROWS, HD), BF),
            vm((4, HD, ROWS), BF),
            vm((4 * ROWS, HD), F32),
            vm((2, HD, CH), F32),
            vm((2, 2, HD, SEGCTX), F32),
            vm((4, 2, HD, CH), F32),
            vm((6, 2, HD, CH), BF),
            vm((6, 2, HD, CH), BF),
            vm((2, 2, HD, 256), BF),
            vm((2, 2, HD, 256), BF),
            vm((2, 2, HD, CH), F32),
            vm((6, half_w, NCOL), BF),
            vm((6, half_w, NCOL), BF),
            vm((2, half_w, NCOL), F32),
            dma, dma((4,)), dma((4, 2)), dma((2, 4)), dma((2, 4)), dma((2, 4)),
            dma((6,)), dma((6,)), dma, dma, dma((6,)), dma((6,)),
            dma((6,)), dma((6,)), dma((6,)), dma((6,)), dma((6,)), dma((6,)),
            dma((2,)), dma((2,)), dma((6,)), dma((6,)),
        ],
        compiler_params=pltpu.CompilerParams(
            collective_id=0, has_side_effects=True, vmem_limit_bytes=VLIM),
        name="whole",
    )(ancestors, upstream[0], advantages, out_weight, prefix_keys[0], prefix_values[0], keys[0], values[0],
      queries[0])
    outs = pl.pallas_call(
        finish_kernel,
        out_shape=tuple([sds((TOKL, NCOL), BF)] + [sds((256, HD), BF)] * 4 + [sds((WROWS, NCOL), F32)]),
        in_specs=[VM] * 3,
        out_specs=tuple([VM] * 6),
        name="finish",
    )(dq, okv, owg)
    return tuple(o[None] for o in outs[:5]) + (outs[5],)


def solution(mesh):
    return jax.shard_map(
        on_device,
        mesh=mesh,
        in_specs=(
            P("dp", "branch", "tensor"),
            P("dp", "branch", "tensor"),
            P("dp", "branch", "tensor"),
            P("dp", "branch", "tensor"),
            P("dp", "branch", "tensor"),
            P("dp", None, None),
            P("dp", "branch"),
            P("dp", "branch", "tensor"),
            P(("dp", "branch"), "tensor"),
        ),
        out_specs=(
            P("dp", "branch", "tensor"),
            P("dp", "branch", "tensor"),
            P("dp", "branch", "tensor"),
            P("dp", "branch", "tensor"),
            P("dp", "branch", "tensor"),
            P(("dp", "branch"), "tensor"),
        ),
        check_vma=False,
    )
```

```python
import math

import jax
import jax.numpy as jnp
from jax import lax
from jax.experimental import pallas as pl
from jax.experimental.pallas import tpu as pltpu
from jax.sharding import PartitionSpec as P

HD = 128
SEG = 128
GROUP = 8
TOKL = 256
KVB = 8
WROWS = 320
NCOL = 1024
UCOL = 640
CTX = 2048
SEGCTX = 384
ALLCTX = CTX + SEGCTX
CH = 512
ROWS = 512
SCALE = 1.0 / math.sqrt(HD)
LOG2E = 1.4426950408889634
BF = jnp.bfloat16
F32 = jnp.float32
VM = pl.BlockSpec(memory_space=pltpu.VMEM)
VLIM = 60 * 2**20


def coords():
    b = lax.axis_index("branch")
    t = lax.axis_index("tensor")
    return t // 2, b // 2, lax.axis_index("dp") * 2 + b % 2, t % 2


def place(x, y, z, c):
    return {"dp": z // 2, "branch": y * 2 + z % 2, "tensor": x * 2 + c}


def rcopy(src, dst, ss, rs, dev):
    return pltpu.make_async_remote_copy(
        src_ref=src, dst_ref=dst, send_sem=ss, recv_sem=rs,
        device_id=dev, device_id_type=pl.DeviceIdType.MESH,
    )


def signal(sem, dev):
    pl.semaphore_signal(sem, inc=1, device_id=dev, device_id_type=pl.DeviceIdType.MESH)


def nt_dot(a, b):
    return lax.dot_general(a, b, (((1,), (1,)), ((), ())), preferred_element_type=F32)


class GatherRing:
    def __init__(self, me, dev, view, ss, rs):
        self.me, self.dev, self.view, self.ss, self.rs = me, dev, view, ss, rs

    def copy(self, node, piece, kind, step):
        v = self.view(node, piece)
        i = kind * 2 + piece
        return rcopy(v, v, self.ss.at[i], self.rs.at[i], self.dev(step))

    def right(self, p):
        return self.copy(self.me, p, 0, 1)

    def left(self, p):
        return self.copy(self.me, p, 1, 3)

    def fwd(self, p):
        if p == 0:
            return self.copy((self.me + 3) % 4, 0, 2, 1)
        return self.copy((self.me + 1) % 4, 1, 2, 3)

    def send(self, p):
        self.right(p).start()
        self.left(p).start()

    def forward(self, p):
        (self.right if p == 0 else self.left)(p).wait_recv()
        self.fwd(p).start()

    def wait_near(self):
        self.right(1).wait_recv()
        self.left(0).wait_recv()

    def wait_far(self):
        self.fwd(0).wait_recv()
        self.fwd(1).wait_recv()

    def wait_sends(self):
        for p in range(2):
            self.right(p).wait_send()
            self.left(p).wait_send()
            self.fwd(p).wait_send()


class SumRing:
    def __init__(self, dev, sb, rb, ss, rs):
        self.dev, self.sb, self.rb, self.ss, self.rs = dev, sb, rb, ss, rs

    def copy(self, i):
        return rcopy(self.sb.at[i], self.rb.at[i], self.ss.at[i], self.rs.at[i], self.dev(1 if i % 2 == 0 else 3))

    def send(self, i, value):
        self.sb[i] = value.astype(BF)
        self.copy(i).start()

    def add_send(self, i, value):
        self.copy(i - 4).wait_recv()
        self.send(i, value + self.rb[i - 4].astype(F32))

    def wait_result(self):
        for i in range(2, 6):
            self.copy(i).wait_recv()

    def result(self, p, own):
        a, b = ((4, 3), (2, 5))[p]
        return own + self.rb[a].astype(F32) + self.rb[b].astype(F32)

    def wait_sends(self):
        for i in range(6):
            self.copy(i).wait_send()


def whole_kernel(
    anc, up, adv, w, pk, pv, sk, sv, q,
    odq, okv, owg,
    cot, cotb, cott, wg, kvg, kcs, vcs,
    dsb, drb, dnear, dattn,
    s_f, p_b, p_s, attng, il_b, delta, qt, dos, dost, dqa,
    acc, accs, segt, ksb, krb, zsb, zrb, kown,
    gsb, grb, gnear,
    c_s, c_r, x_s, x_r, b_s, b_r, w_s, w_r, kz_s, kz_r, k_s, k_r,
    d_s, d_r, a_s, a_r, r_s, r_r, zk_s, zk_r, g_s, g_r,
):
    x, y, z, c = coords()
    zl = z % 2
    first = lax.axis_index("branch") * 2
    target_y = 2 * (x % 2) + c
    is_recv = c == y % 2
    is_src = target_y == y
    half = x // 2
    sib = place(x, y, z, 1 - c)
    cexp = SCALE * LOG2E

    def ydev(d):
        return place(x, (y + d) % 4, z, c)

    def zdev(d):
        return place(x, y, (z + d) % 4, c)

    def xdev(d):
        return place((x + d) % 4, y, z, c)

    bar = pltpu.get_barrier_semaphore()
    for d in range(1, 4):
        signal(bar, ydev(d))
    signal(bar, zdev(1))
    signal(bar, zdev(3))
    signal(bar, sib)

    @pl.when(is_recv)
    def _():
        signal(bar, xdev(1))
        signal(bar, xdev(3))

    rows_b = lambda b: pl.ds(pl.multiple_of(b * 256, 256), 256)
    own_rows = rows_b(y * 2 + zl)
    for i, r in enumerate((pk, pv, sk, sv)):
        kvg[i, own_rows, :] = r[...]
    wrow = jnp.broadcast_to(adv[...].astype(F32) * 0.25, (TOKL, TOKL))
    ri = lax.broadcasted_iota(jnp.int32, (TOKL, TOKL), 0)
    ci = lax.broadcasted_iota(jnp.int32, (TOKL, TOKL), 1)
    diag = jnp.where(ri == ci, wrow, 0.0).astype(BF)
    cot[...] = jnp.dot(diag, up[...], preferred_element_type=F32).astype(BF)
    w_half = WROWS // 2
    wview = lambda n, p: wg.at[pl.ds(pl.multiple_of(n * WROWS + p * w_half, 32), w_half)]
    wg[pl.ds(pl.multiple_of(z * WROWS, 64), WROWS), :] = w[...]

    pl.semaphore_wait(bar, 6 + 2 * is_recv.astype(jnp.int32))

    wring = GatherRing(z, zdev, wview, w_s, w_r)
    kring = GatherRing(y, ydev, lambda n, p: kvg.at[:, rows_b(n * 2 + p)], k_s, k_r)
    aring = GatherRing(
        y, ydev, lambda n, p: attng.at[pl.ds(pl.multiple_of(n * TOKL + p * SEG, SEG), SEG)], a_s, a_r)
    dring = SumRing(ydev, dsb, drb, d_s, d_r)
    rring = SumRing(ydev, ksb, krb, r_s, r_r)
    gring = SumRing(zdev, gsb, grb, g_s, g_r)

    def kz():
        v = kvg.at[:, own_rows]
        return rcopy(v, v, kz_s, kz_r, place(x, y, z + 1 - 2 * zl, c))

    def cy():
        return rcopy(cot, cotb.at[half, y], c_s, c_r.at[y], place(x, target_y, z, c))

    def cx(h, yy, k):
        v = cotb.at[h, yy]
        return rcopy(v, v, x_s.at[yy, k], x_r.at[h, yy], xdev((1, 3)[k]))

    def cb(h, yy):
        v = cotb.at[h, yy]
        return rcopy(v, v, b_s.at[h, yy], b_r.at[h, yy], sib)

    is_mid = is_recv & jnp.logical_not(is_src)
    left_half = ((x + 3) % 4) // 2
    right_half = ((x + 1) % 4) // 2

    def mid_block(d):
        yy = (y + d) % 4
        cx(left_half, yy, 0).wait_recv()

        @pl.when(yy < 2)
        def _():
            cx(left_half, yy, 0).start()

        cb(left_half, yy).start()
        cx(right_half, yy, 1).wait_recv()

        @pl.when(yy >= 2)
        def _():
            cx(right_half, yy, 1).start()

        cb(right_half, yy).start()

    kz().start()

    @pl.when(jnp.logical_not(is_src))
    def _():
        cy().start()

    kring.send(zl)

    @pl.when(zl == 0)
    def _():
        for p in range(2):
            wring.left(p).start()

    @pl.when(zl == 1)
    def _():
        for p in range(2):
            wring.right(p).start()

    @pl.when(is_src)
    def _():
        cotb[half, y] = cot[...]
        for k in range(2):
            cx(half, y, k).start()
        cb(half, y).start()

    kz().wait_recv()
    kring.send(1 - zl)

    @pl.when(zl == 0)
    def _():
        for p in range(2):
            wring.right(p).start()

    @pl.when(zl == 1)
    def _():
        for p in range(2):
            wring.left(p).start()

    @pl.when(is_src)
    def _():
        for d in (1, 3, 2):
            yy = (y + d) % 4
            rcopy(cot, cotb.at[half, yy], c_s, c_r.at[yy], sib).wait_recv()
            for k in range(2):
                cx(half, yy, k).start()
            cb(half, yy).start()

    @pl.when(is_mid)
    def _():
        mid_block(0)
        mid_block(1)

    for p in range(2):
        kring.forward(p)

    @pl.when(is_mid)
    def _():
        mid_block(3)
        mid_block(2)

    for p in range(2):
        wring.forward(p)
    kring.wait_near()
    kring.wait_far()

    named = [[jnp.broadcast_to(anc[0, pl.ds(first + s, 1), i:i + 1], (1, HD)) for i in range(2)] for s in range(2)]

    def hot(s, i, j):
        return (named[s][i] == j).astype(F32)

    for s in range(2):
        own_seg = pl.ds(pl.multiple_of((first + s) * SEG, SEG), SEG)
        for k, dst in enumerate((kcs, vcs)):
            for i in range(2):
                tot = None
                for j in range(16):
                    v = kvg[2 + k, j * SEG:(j + 1) * SEG, :].astype(F32) * hot(s, i, j)
                    tot = v if tot is None else tot + v
                dst[s, i * SEG:(i + 1) * SEG, :] = tot.astype(BF)
            dst[s, 2 * SEG:, :] = kvg[2 + k, own_seg, :]

    nh = ROWS // SEG

    def forward(rb):
        s, hb = rb // 2, rb % 2
        tok = slice(s * SEG, (s + 1) * SEG)
        rows = slice(rb * ROWS, (rb + 1) * ROWS)
        col = lax.broadcasted_iota(jnp.int32, (ROWS, SEG), 1)
        row = lax.broadcasted_iota(jnp.int32, (ROWS, SEG), 0) % SEG
        shut = [jnp.where(named[s][i] >= 0, 0.0, -1e30) for i in range(2)]
        shut.append(jnp.where(col <= row, 0.0, -1e30))
        heads = [slice((hb * nh + i) * HD, (hb * nh + i + 1) * HD) for i in range(nh)]
        qb = jnp.concatenate([q[tok, h] for h in heads], axis=0)
        qt[rb] = qb.T
        mx = None
        for j in range(5):
            kc = kvg[0, j * CH:(j + 1) * CH, :] if j < 4 else kcs[s]
            sc = nt_dot(qb, kc)
            n = sc.shape[1]
            if j == 4:
                sc = jnp.concatenate([sc[:, i * SEG:(i + 1) * SEG] + shut[i] for i in range(3)], axis=1)
            s_f[:, j * CH:j * CH + n] = sc
            for t in range(n // 128):
                part = sc[:, t * 128:(t + 1) * 128]
                mx = part if mx is None else jnp.maximum(mx, part)
        m = jnp.max(mx, axis=1, keepdims=True)
        lsum = None
        o = None
        for j in range(5):
            vc = kvg[1, j * CH:(j + 1) * CH, :] if j < 4 else vcs[s]
            n = vc.shape[0]
            p = jnp.exp2((s_f[:, j * CH:j * CH + n] - m) * cexp)
            for t in range(n // 128):
                part = p[:, t * 128:(t + 1) * 128]
                lsum = part if lsum is None else lsum + part
            pb = p.astype(BF)
            if j < 4:
                p_b[j, rows, :] = pb
            else:
                p_s[rows, :] = pb
            oc = jnp.dot(pb, vc, preferred_element_type=F32)
            o = oc if o is None else o + oc
        il = jnp.broadcast_to(1.0 / jnp.sum(lsum, axis=1, keepdims=True), (ROWS, HD))
        il_b[rows, :] = il
        ob = (o * il).astype(BF)
        for i, h in enumerate(heads):
            attng[pl.ds(pl.multiple_of(y * TOKL + s * SEG, SEG), SEG), h] = ob[i * SEG:(i + 1) * SEG]

    forward(0)
    forward(1)
    aring.send(0)
    forward(2)
    forward(3)
    aring.send(1)
    aring.forward(0)

    @pl.when(is_src)
    def _():
        for d in (0, 1, 3, 2):
            cx(1 - half, (y + d) % 4, 0).wait_recv()
            cb(1 - half, (y + d) % 4).start()

    wring.wait_near()
    wring.wait_far()

    @pl.when(jnp.logical_not(is_recv))
    def _():
        for h in range(2):
            for yy in range(4):
                cb(h, yy).wait_recv()

    def proj(yy, rows):
        return jnp.dot(cotb[0, yy, rows, :], wg[0:UCOL, :], preferred_element_type=F32) + jnp.dot(
            cotb[1, yy, rows, :], wg[UCOL:2 * UCOL, :], preferred_element_type=F32)

    lo, hi = slice(0, SEG), slice(SEG, 2 * SEG)
    dring.send(0, proj((y + 2) % 4, lo))
    dring.send(1, proj((y + 2) % 4, hi))
    dring.send(2, proj((y + 1) % 4, hi))
    dring.send(3, proj((y + 3) % 4, lo))
    aring.forward(1)
    dnear[0] = proj((y + 1) % 4, lo)
    dnear[1] = proj((y + 3) % 4, hi)
    dnear[2] = proj(y, lo)
    dnear[3] = proj(y, hi)

    for h in range(2):
        for yy in range(4):
            cott[h * UCOL:(h + 1) * UCOL, yy * TOKL:(yy + 1) * TOKL] = cotb[h, yy].T
    dring.add_send(4, dnear[0])
    dring.add_send(5, dnear[1])

    aring.wait_near()
    aring.wait_far()

    def wgrad(zz, p):
        rows = pl.ds(pl.multiple_of(zz * WROWS + p * w_half, 32), w_half)
        return jnp.dot(cott[rows, :], attng[...], preferred_element_type=F32)

    gring.send(0, wgrad((z + 2) % 4, 0))
    gring.send(1, wgrad((z + 2) % 4, 1))
    gring.send(2, wgrad((z + 1) % 4, 1))
    gring.send(3, wgrad((z + 3) % 4, 0))
    gnear[0] = wgrad((z + 1) % 4, 0)
    gnear[1] = wgrad((z + 3) % 4, 1)
    gring.add_send(4, gnear[0])
    gring.add_send(5, gnear[1])

    dring.wait_result()
    for p in range(2):
        dattn[p * SEG:(p + 1) * SEG, :] = dring.result(p, dnear[2 + p]).astype(BF)
    for rb in range(4):
        s, hb = rb // 2, rb % 2
        rows = slice(rb * ROWS, (rb + 1) * ROWS)
        tok = slice(s * SEG, (s + 1) * SEG)
        arow = pl.ds(pl.multiple_of(y * TOKL + s * SEG, SEG), SEG)
        heads = [slice((hb * nh + i) * HD, (hb * nh + i + 1) * HD) for i in range(nh)]
        dob = jnp.concatenate([dattn[tok, h] for h in heads], axis=0)
        at = jnp.concatenate([attng[arow, h] for h in heads], axis=0)
        db = (dob.astype(F32) * il_b[rows, :]).astype(BF)
        dos[rows, :] = db
        dost[rb] = db.T
        dl = jnp.sum(db.astype(F32) * at.astype(F32), axis=1, keepdims=True)
        delta[rows, :] = jnp.broadcast_to(dl, (ROWS, HD))

    def back(rb, kc, vc, pb):
        rows = pl.ds(pl.multiple_of(rb * ROWS, ROWS), ROWS)
        dl = delta[rows, :]
        n = vc.shape[0]
        dp = nt_dot(dos[rows, :], vc)
        ds = (pb.astype(F32) * (dp - jnp.concatenate([dl] * (n // HD), axis=1))).astype(BF)
        return (rows, jnp.dot(ds, kc, preferred_element_type=F32),
                jnp.dot(qt[rb], ds, preferred_element_type=F32),
                jnp.dot(dost[rb], pb, preferred_element_type=F32))

    for rb in range(4):
        s = rb // 2
        rows, dqc, dk, dv = back(rb, kcs[s], vcs[s], p_s[rb * ROWS:(rb + 1) * ROWS, :])
        dqa[rows, :] = dqc
        if rb % 2 == 0:
            accs[s, 0] = dk
            accs[s, 1] = dv
        else:
            accs[s, 0] += dk
            accs[s, 1] += dv
    for j in range(16):
        for k in range(2):
            tot = None
            for s in range(2):
                for i in range(2):
                    v = accs[s, k, :, i * SEG:(i + 1) * SEG] * hot(s, i, j)
                    tot = v if tot is None else tot + v
            segt[j // 4, k, :, (j % 4) * SEG:(j % 4 + 1) * SEG] = tot
    for s in range(2):
        own_cols = pl.ds(pl.multiple_of((zl * 2 + s) * SEG, SEG), SEG)
        for k in range(2):
            segt[y, k, :, own_cols] += accs[s, k, :, 2 * SEG:]
    rring.send(0, segt[(y + 2) % 4])
    rring.send(3, segt[(y + 3) % 4])

    def prefix(j):
        acc[...] = jnp.zeros_like(acc)
        crow = pl.ds(pl.multiple_of(j * CH, CH), CH)

        @pl.loop(0, 4)
        def _(rb):
            rows = pl.ds(pl.multiple_of(rb * ROWS, ROWS), ROWS)
            _, dqc, dk, dv = back(rb, kvg[0, crow, :], kvg[1, crow, :], p_b[j, rows, :])
            dqa[rows, :] += dqc
            acc[0] += dk
            acc[1] += dv

    prefix((y + 2) % 4)
    rring.send(1, acc[...])
    rring.add_send(4, segt[(y + 1) % 4])
    prefix((y + 1) % 4)
    rring.send(2, acc[...])
    prefix((y + 3) % 4)
    rring.add_send(5, acc[...])
    prefix(y)
    for rb in range(4):
        s, hb = rb // 2, rb % 2
        dqb = (dqa[rb * ROWS:(rb + 1) * ROWS, :] * SCALE).astype(BF)
        for i in range(nh):
            odq[s * SEG:(s + 1) * SEG, (hb * nh + i) * HD:(hb * nh + i + 1) * HD] = dqb[i * SEG:(i + 1) * SEG]

    for p in range(2):
        owg[p * w_half:(p + 1) * w_half, :] = wgrad(z, p)

    lanes = lambda v: pl.ds(pl.multiple_of(v * 256, 256), 256)

    def zk(p):
        return rcopy(zsb.at[p], zrb.at[p], zk_s.at[p], zk_r.at[p], place(x, y, z + 1 - 2 * zl, c))

    for p in range(2):
        for i in ((4, 3), (2, 5))[p]:
            rring.copy(i).wait_recv()
        kown[p] = rring.result(p, segt[y] if p == 0 else acc[...])
        zsb[p] = kown[p, :, :, lanes(1 - zl)].astype(BF)
        zk(p).start()

    gring.wait_result()
    for p in range(2):
        rows = slice(p * w_half, (p + 1) * w_half)
        owg[rows, :] = gring.result(p, owg[rows, :])

    for p in range(2):
        zk(p).wait_recv()
        for i in range(2):
            t = kown[p, i, :, lanes(zl)] + zrb[p, i].astype(F32)
            if i == 0:
                t = t * SCALE
            okv[2 * (1 - p) + i] = t.T.astype(BF)

    kz().wait_send()
    for p in range(2):
        zk(p).wait_send()

    @pl.when(jnp.logical_not(is_src))
    def _():
        cy().wait_send()

    @pl.when(is_src)
    def _():
        for yy in range(4):
            for k in range(2):
                cx(half, yy, k).wait_send()

    @pl.when(is_mid)
    def _():
        for yy in range(4):
            cx(0, yy, yy // 2).wait_send()

    @pl.when(is_recv)
    def _():
        for h in range(2):
            for yy in range(4):
                cb(h, yy).wait_send()

    for ring in (wring, kring, aring, dring, rring, gring):
        ring.wait_sends()


def finish_kernel(dq, kv, wgr, o0, o1, o2, o3, o4, o5):
    o0[...] = dq[...]
    for i, o in enumerate((o1, o2, o3, o4)):
        o[...] = kv[i]
    o5[...] = wgr[...]


def on_device(
    queries, prefix_keys, prefix_values, keys, values, ancestors, advantages, upstream, out_weight
):
    dma = pltpu.SemaphoreType.DMA
    sds = jax.ShapeDtypeStruct
    vm = pltpu.VMEM
    half_w = WROWS // 2
    dq, okv, owg = pl.pallas_call(
        whole_kernel,
        out_shape=(
            sds((TOKL, NCOL), BF),
            sds((4, 256, HD), BF),
            sds((WROWS, NCOL), F32),
        ),
        in_specs=[VM] * 9,
        out_specs=(VM, VM, VM),
        scratch_shapes=[
            vm((TOKL, UCOL), BF),
            vm((2, 4, TOKL, UCOL), BF),
            vm((2 * UCOL, 4 * TOKL), BF),
            vm((4 * WROWS, NCOL), BF),
            vm((4, CTX, HD), BF),
            vm((2, SEGCTX, HD), BF),
            vm((2, SEGCTX, HD), BF),
            vm((6, SEG, NCOL), BF),
            vm((6, SEG, NCOL), BF),
            vm((4, SEG, NCOL), F32),
            vm((TOKL, NCOL), BF),
            vm((ROWS, ALLCTX), F32),
            vm((4, 4 * ROWS, CH), BF),
            vm((4 * ROWS, SEGCTX), BF),
            vm((4 * TOKL, NCOL), BF),
            vm((4 * ROWS, HD), F32),
            vm((4 * ROWS, HD), F32),
            vm((4, HD, ROWS), BF),
            vm((4 * ROWS, HD), BF),
            vm((4, HD, ROWS), BF),
            vm((4 * ROWS, HD), F32),
            vm((2, HD, CH), F32),
            vm((2, 2, HD, SEGCTX), F32),
            vm((4, 2, HD, CH), F32),
            vm((6, 2, HD, CH), BF),
            vm((6, 2, HD, CH), BF),
            vm((2, 2, HD, 256), BF),
            vm((2, 2, HD, 256), BF),
            vm((2, 2, HD, CH), F32),
            vm((6, half_w, NCOL), BF),
            vm((6, half_w, NCOL), BF),
            vm((2, half_w, NCOL), F32),
            dma, dma((4,)), dma((4, 2)), dma((2, 4)), dma((2, 4)), dma((2, 4)),
            dma((6,)), dma((6,)), dma, dma, dma((6,)), dma((6,)),
            dma((6,)), dma((6,)), dma((6,)), dma((6,)), dma((6,)), dma((6,)),
            dma((2,)), dma((2,)), dma((6,)), dma((6,)),
        ],
        compiler_params=pltpu.CompilerParams(
            collective_id=0, has_side_effects=True, vmem_limit_bytes=VLIM),
        name="whole",
    )(ancestors, upstream[0], advantages, out_weight, prefix_keys[0], prefix_values[0], keys[0], values[0],
      queries[0])
    outs = pl.pallas_call(
        finish_kernel,
        out_shape=tuple([sds((TOKL, NCOL), BF)] + [sds((256, HD), BF)] * 4 + [sds((WROWS, NCOL), F32)]),
        in_specs=[VM] * 3,
        out_specs=tuple([VM] * 6),
        name="finish",
    )(dq, okv, owg)
    return tuple(o[None] for o in outs[:5]) + (outs[5],)


def solution(mesh):
    return jax.shard_map(
        on_device,
        mesh=mesh,
        in_specs=(
            P("dp", "branch", "tensor"),
            P("dp", "branch", "tensor"),
            P("dp", "branch", "tensor"),
            P("dp", "branch", "tensor"),
            P("dp", "branch", "tensor"),
            P("dp", None, None),
            P("dp", "branch"),
            P("dp", "branch", "tensor"),
            P(("dp", "branch"), "tensor"),
        ),
        out_specs=(
            P("dp", "branch", "tensor"),
            P("dp", "branch", "tensor"),
            P("dp", "branch", "tensor"),
            P("dp", "branch", "tensor"),
            P("dp", "branch", "tensor"),
            P(("dp", "branch"), "tensor"),
        ),
        check_vma=False,
    )
```

```python
import math

import jax
import jax.numpy as jnp
from jax import lax
from jax.experimental import pallas as pl
from jax.experimental.pallas import tpu as pltpu
from jax.sharding import PartitionSpec as P

HD = 128
SEG = 128
GROUP = 8
TOKL = 256
KVB = 8
WROWS = 320
NCOL = 1024
UCOL = 640
CTX = 2048
SEGCTX = 384
ALLCTX = CTX + SEGCTX
CH = 512
ROWS = 512
SCALE = 1.0 / math.sqrt(HD)
LOG2E = 1.4426950408889634
BF = jnp.bfloat16
F32 = jnp.float32
VM = pl.BlockSpec(memory_space=pltpu.VMEM)
VLIM = 60 * 2**20


def coords():
    b = lax.axis_index("branch")
    t = lax.axis_index("tensor")
    return t // 2, b // 2, lax.axis_index("dp") * 2 + b % 2, t % 2


def place(x, y, z, c):
    return {"dp": z // 2, "branch": y * 2 + z % 2, "tensor": x * 2 + c}


def rcopy(src, dst, ss, rs, dev):
    return pltpu.make_async_remote_copy(
        src_ref=src, dst_ref=dst, send_sem=ss, recv_sem=rs,
        device_id=dev, device_id_type=pl.DeviceIdType.MESH,
    )


def signal(sem, dev):
    pl.semaphore_signal(sem, inc=1, device_id=dev, device_id_type=pl.DeviceIdType.MESH)


def nt_dot(a, b):
    return lax.dot_general(a, b, (((1,), (1,)), ((), ())), preferred_element_type=F32)


class GatherRing:
    def __init__(self, me, dev, view, ss, rs):
        self.me, self.dev, self.view, self.ss, self.rs = me, dev, view, ss, rs

    def copy(self, node, piece, kind, step):
        v = self.view(node, piece)
        i = kind * 2 + piece
        return rcopy(v, v, self.ss.at[i], self.rs.at[i], self.dev(step))

    def right(self, p):
        return self.copy(self.me, p, 0, 1)

    def left(self, p):
        return self.copy(self.me, p, 1, 3)

    def fwd(self, p):
        if p == 0:
            return self.copy((self.me + 3) % 4, 0, 2, 1)
        return self.copy((self.me + 1) % 4, 1, 2, 3)

    def send(self, p):
        self.right(p).start()
        self.left(p).start()

    def forward(self, p):
        (self.right if p == 0 else self.left)(p).wait_recv()
        self.fwd(p).start()

    def wait_near(self):
        self.right(1).wait_recv()
        self.left(0).wait_recv()

    def wait_far(self):
        self.fwd(0).wait_recv()
        self.fwd(1).wait_recv()

    def wait_sends(self):
        for p in range(2):
            self.right(p).wait_send()
            self.left(p).wait_send()
            self.fwd(p).wait_send()


class SumRing:
    def __init__(self, dev, sb, rb, ss, rs):
        self.dev, self.sb, self.rb, self.ss, self.rs = dev, sb, rb, ss, rs

    def copy(self, i):
        return rcopy(self.sb.at[i], self.rb.at[i], self.ss.at[i], self.rs.at[i], self.dev(1 if i % 2 == 0 else 3))

    def send(self, i, value):
        self.sb[i] = value.astype(BF)
        self.copy(i).start()

    def add_send(self, i, value):
        self.copy(i - 4).wait_recv()
        self.send(i, value + self.rb[i - 4].astype(F32))

    def wait_result(self):
        for i in range(2, 6):
            self.copy(i).wait_recv()

    def result(self, p, own):
        a, b = ((4, 3), (2, 5))[p]
        return own + self.rb[a].astype(F32) + self.rb[b].astype(F32)

    def wait_sends(self):
        for i in range(6):
            self.copy(i).wait_send()


def whole_kernel(
    anc, up, adv, w, pk, pv, sk, sv, q,
    odq, okv, owg,
    cot, cotb, cott, wg, kvg, kcs, vcs,
    dsb, drb, dnear, dattn,
    s_f, p_b, p_s, attng, il_b, delta, qt, dos, dost, dqa,
    acc, accs, segt, ksb, krb, zsb, zrb, kown,
    gsb, grb, gnear,
    c_s, c_r, x_s, x_r, b_s, b_r, w_s, w_r, kz_s, kz_r, k_s, k_r,
    d_s, d_r, a_s, a_r, r_s, r_r, zk_s, zk_r, g_s, g_r,
):
    x, y, z, c = coords()
    zl = z % 2
    first = lax.axis_index("branch") * 2
    target_y = 2 * (x % 2) + c
    is_recv = c == y % 2
    is_src = target_y == y
    half = x // 2
    sib = place(x, y, z, 1 - c)
    cexp = SCALE * LOG2E

    def ydev(d):
        return place(x, (y + d) % 4, z, c)

    def zdev(d):
        return place(x, y, (z + d) % 4, c)

    def xdev(d):
        return place((x + d) % 4, y, z, c)

    bar = pltpu.get_barrier_semaphore()
    for d in range(1, 4):
        signal(bar, ydev(d))
    signal(bar, zdev(1))
    signal(bar, zdev(3))
    signal(bar, sib)

    @pl.when(is_recv)
    def _():
        signal(bar, xdev(1))
        signal(bar, xdev(3))

    rows_b = lambda b: pl.ds(pl.multiple_of(b * 256, 256), 256)
    own_rows = rows_b(y * 2 + zl)
    for i, r in enumerate((pk, pv, sk, sv)):
        kvg[i, own_rows, :] = r[...]
    wrow = jnp.broadcast_to(adv[...].astype(F32) * 0.25, (TOKL, TOKL))
    ri = lax.broadcasted_iota(jnp.int32, (TOKL, TOKL), 0)
    ci = lax.broadcasted_iota(jnp.int32, (TOKL, TOKL), 1)
    diag = jnp.where(ri == ci, wrow, 0.0).astype(BF)
    cot[...] = jnp.dot(diag, up[...], preferred_element_type=F32).astype(BF)
    w_half = WROWS // 2
    wview = lambda n, p: wg.at[pl.ds(pl.multiple_of(n * WROWS + p * w_half, 32), w_half)]
    wg[pl.ds(pl.multiple_of(z * WROWS, 64), WROWS), :] = w[...]

    pl.semaphore_wait(bar, 6 + 2 * is_recv.astype(jnp.int32))

    wring = GatherRing(z, zdev, wview, w_s, w_r)
    kring = GatherRing(y, ydev, lambda n, p: kvg.at[:, rows_b(n * 2 + p)], k_s, k_r)
    aring = GatherRing(
        y, ydev, lambda n, p: attng.at[p, pl.ds(pl.multiple_of(n * TOKL, TOKL), TOKL)], a_s, a_r)
    dring = SumRing(ydev, dsb, drb, d_s, d_r)
    rring = SumRing(ydev, ksb, krb, r_s, r_r)
    gring = SumRing(zdev, gsb, grb, g_s, g_r)

    def kz():
        v = kvg.at[:, own_rows]
        return rcopy(v, v, kz_s, kz_r, place(x, y, z + 1 - 2 * zl, c))

    def cy():
        return rcopy(cot, cotb.at[half, y], c_s, c_r.at[y], place(x, target_y, z, c))

    def cx(h, yy, k):
        v = cotb.at[h, yy]
        return rcopy(v, v, x_s.at[yy, k], x_r.at[h, yy], xdev((1, 3)[k]))

    def cb(h, yy):
        v = cotb.at[h, yy]
        return rcopy(v, v, b_s.at[h, yy], b_r.at[h, yy], sib)

    is_mid = is_recv & jnp.logical_not(is_src)
    left_half = ((x + 3) % 4) // 2
    right_half = ((x + 1) % 4) // 2

    def mid_block(d):
        yy = (y + d) % 4
        cx(left_half, yy, 0).wait_recv()

        @pl.when(yy < 2)
        def _():
            cx(left_half, yy, 0).start()

        cb(left_half, yy).start()
        cx(right_half, yy, 1).wait_recv()

        @pl.when(yy >= 2)
        def _():
            cx(right_half, yy, 1).start()

        cb(right_half, yy).start()

    kz().start()

    @pl.when(jnp.logical_not(is_src))
    def _():
        cy().start()

    kring.send(zl)

    @pl.when(zl == 0)
    def _():
        for p in range(2):
            wring.left(p).start()

    @pl.when(zl == 1)
    def _():
        for p in range(2):
            wring.right(p).start()

    @pl.when(is_src)
    def _():
        cotb[half, y] = cot[...]
        for k in range(2):
            cx(half, y, k).start()
        cb(half, y).start()

    kz().wait_recv()
    kring.send(1 - zl)

    @pl.when(zl == 0)
    def _():
        for p in range(2):
            wring.right(p).start()

    @pl.when(zl == 1)
    def _():
        for p in range(2):
            wring.left(p).start()

    @pl.when(is_src)
    def _():
        for d in (1, 3, 2):
            yy = (y + d) % 4
            rcopy(cot, cotb.at[half, yy], c_s, c_r.at[yy], sib).wait_recv()
            for k in range(2):
                cx(half, yy, k).start()
            cb(half, yy).start()

    @pl.when(is_mid)
    def _():
        mid_block(0)
        mid_block(1)

    for p in range(2):
        kring.forward(p)

    @pl.when(is_mid)
    def _():
        mid_block(3)
        mid_block(2)

    for p in range(2):
        wring.forward(p)
    kring.wait_near()
    kring.wait_far()

    lane = lax.broadcasted_iota(jnp.int32, (1, 16), 1)
    named = [[jnp.broadcast_to(jnp.sum(jnp.where(lane == first + s, anc[i:i + 1, :].astype(F32), 0.0),
                                       axis=1, keepdims=True), (1, HD)) for i in range(2)] for s in range(2)]

    def hot(s, i, j):
        return (named[s][i] == float(j)).astype(F32)

    for s in range(2):
        own_seg = pl.ds(pl.multiple_of((first + s) * SEG, SEG), SEG)
        for k, dst in enumerate((kcs, vcs)):
            for i in range(2):
                tot = None
                for j in range(16):
                    v = kvg[2 + k, j * SEG:(j + 1) * SEG, :].astype(F32) * hot(s, i, j)
                    tot = v if tot is None else tot + v
                dst[s, i * SEG:(i + 1) * SEG, :] = tot.astype(BF)
            dst[s, 2 * SEG:, :] = kvg[2 + k, own_seg, :]

    nh = ROWS // SEG

    def forward(rb):
        s, hb = rb // 2, rb % 2
        tok = slice(s * SEG, (s + 1) * SEG)
        rows = slice(rb * ROWS, (rb + 1) * ROWS)
        col = lax.broadcasted_iota(jnp.int32, (ROWS, SEG), 1)
        row = lax.broadcasted_iota(jnp.int32, (ROWS, SEG), 0) % SEG
        shut = [jnp.where(named[s][i] >= 0, 0.0, -1e30) for i in range(2)]
        shut.append(jnp.where(col <= row, 0.0, -1e30))
        heads = [slice((hb * nh + i) * HD, (hb * nh + i + 1) * HD) for i in range(nh)]
        qb = jnp.concatenate([q[tok, h] for h in heads], axis=0)
        qt[rb] = qb.T
        mx = None
        for j in range(5):
            kc = kvg[0, j * CH:(j + 1) * CH, :] if j < 4 else kcs[s]
            sc = nt_dot(qb, kc)
            n = sc.shape[1]
            if j == 4:
                sc = jnp.concatenate([sc[:, i * SEG:(i + 1) * SEG] + shut[i] for i in range(3)], axis=1)
            s_f[:, j * CH:j * CH + n] = sc
            for t in range(n // 128):
                part = sc[:, t * 128:(t + 1) * 128]
                mx = part if mx is None else jnp.maximum(mx, part)
        m = jnp.max(mx, axis=1, keepdims=True)
        lsum = None
        o = None
        for j in range(5):
            vc = kvg[1, j * CH:(j + 1) * CH, :] if j < 4 else vcs[s]
            n = vc.shape[0]
            p = jnp.exp2((s_f[:, j * CH:j * CH + n] - m) * cexp)
            for t in range(n // 128):
                part = p[:, t * 128:(t + 1) * 128]
                lsum = part if lsum is None else lsum + part
            pb = p.astype(BF)
            if j < 4:
                p_b[j, rows, :] = pb
            else:
                p_s[rows, :] = pb
            oc = jnp.dot(pb, vc, preferred_element_type=F32)
            o = oc if o is None else o + oc
        il = jnp.broadcast_to(1.0 / jnp.sum(lsum, axis=1, keepdims=True), (ROWS, HD))
        il_b[rows, :] = il
        ob = (o * il).astype(BF)
        for i in range(nh):
            attng[hb, pl.ds(pl.multiple_of(y * TOKL + s * SEG, SEG), SEG), i * HD:(i + 1) * HD] = (
                ob[i * SEG:(i + 1) * SEG])

    forward(0)
    forward(2)
    aring.send(0)

    @pl.when(is_src)
    def _():
        for d in (0, 1, 3, 2):
            cx(1 - half, (y + d) % 4, 0).wait_recv()
            cb(1 - half, (y + d) % 4).start()

    wring.wait_near()
    wring.wait_far()

    @pl.when(jnp.logical_not(is_recv))
    def _():
        for h in range(2):
            for yy in range(4):
                cb(h, yy).wait_recv()

    def proj(yy, rows):
        return jnp.dot(cotb[0, yy, rows, :], wg[0:UCOL, :], preferred_element_type=F32) + jnp.dot(
            cotb[1, yy, rows, :], wg[UCOL:2 * UCOL, :], preferred_element_type=F32)

    lo, hi = slice(0, SEG), slice(SEG, 2 * SEG)
    dring.send(0, proj((y + 2) % 4, lo))
    dring.send(1, proj((y + 2) % 4, hi))
    dring.send(2, proj((y + 1) % 4, hi))
    dring.send(3, proj((y + 3) % 4, lo))
    dnear[0] = proj((y + 1) % 4, lo)
    dnear[1] = proj((y + 3) % 4, hi)
    dnear[2] = proj(y, lo)
    dnear[3] = proj(y, hi)

    forward(1)
    aring.forward(0)
    forward(3)
    dring.add_send(4, dnear[0])
    dring.add_send(5, dnear[1])
    for h in range(2):
        for yy in range(4):
            cott[h * UCOL:(h + 1) * UCOL, yy * TOKL:(yy + 1) * TOKL] = cotb[h, yy].T

    def wgrad(zz, p):
        rows = pl.ds(pl.multiple_of(zz * WROWS, 64), WROWS)
        return jnp.dot(cott[rows, :], attng[p], preferred_element_type=F32)

    aring.left(0).wait_recv()
    aring.fwd(0).wait_recv()
    gring.send(0, wgrad((z + 2) % 4, 0))
    gring.send(3, wgrad((z + 3) % 4, 0))
    gnear[0] = wgrad((z + 1) % 4, 0)
    aring.send(1)

    dring.wait_result()
    for p in range(2):
        dattn[p * SEG:(p + 1) * SEG, :] = dring.result(p, dnear[2 + p]).astype(BF)
    for rb in range(4):
        s, hb = rb // 2, rb % 2
        rows = slice(rb * ROWS, (rb + 1) * ROWS)
        tok = slice(s * SEG, (s + 1) * SEG)
        arow = pl.ds(pl.multiple_of(y * TOKL + s * SEG, SEG), SEG)
        heads = [slice((hb * nh + i) * HD, (hb * nh + i + 1) * HD) for i in range(nh)]
        dob = jnp.concatenate([dattn[tok, h] for h in heads], axis=0)
        at = jnp.concatenate([attng[hb, arow, i * HD:(i + 1) * HD] for i in range(nh)], axis=0)
        db = (dob.astype(F32) * il_b[rows, :]).astype(BF)
        dos[rows, :] = db
        dost[rb] = db.T
        dl = jnp.sum(db.astype(F32) * at.astype(F32), axis=1, keepdims=True)
        delta[rows, :] = jnp.broadcast_to(dl, (ROWS, HD))

    def back(rb, kc, vc, pb):
        rows = pl.ds(pl.multiple_of(rb * ROWS, ROWS), ROWS)
        dl = delta[rows, :]
        n = vc.shape[0]
        dp = nt_dot(dos[rows, :], vc)
        ds = (pb.astype(F32) * (dp - jnp.concatenate([dl] * (n // HD), axis=1))).astype(BF)
        return (rows, jnp.dot(ds, kc, preferred_element_type=F32),
                jnp.dot(qt[rb], ds, preferred_element_type=F32),
                jnp.dot(dost[rb], pb, preferred_element_type=F32))

    for rb in range(4):
        s = rb // 2
        rows, dqc, dk, dv = back(rb, kcs[s], vcs[s], p_s[rb * ROWS:(rb + 1) * ROWS, :])
        dqa[rows, :] = dqc
        if rb % 2 == 0:
            accs[s, 0] = dk
            accs[s, 1] = dv
        else:
            accs[s, 0] += dk
            accs[s, 1] += dv
    for j in range(16):
        for k in range(2):
            tot = None
            for s in range(2):
                for i in range(2):
                    v = accs[s, k, :, i * SEG:(i + 1) * SEG] * hot(s, i, j)
                    tot = v if tot is None else tot + v
            segt[j // 4, k, :, (j % 4) * SEG:(j % 4 + 1) * SEG] = tot
    for s in range(2):
        own_cols = pl.ds(pl.multiple_of((zl * 2 + s) * SEG, SEG), SEG)
        for k in range(2):
            segt[y, k, :, own_cols] += accs[s, k, :, 2 * SEG:]
    rring.send(0, segt[(y + 2) % 4])
    rring.send(3, segt[(y + 3) % 4])

    def prefix(j):
        acc[...] = jnp.zeros_like(acc)
        crow = pl.ds(pl.multiple_of(j * CH, CH), CH)

        @pl.loop(0, 4)
        def _(rb):
            rows = pl.ds(pl.multiple_of(rb * ROWS, ROWS), ROWS)
            _, dqc, dk, dv = back(rb, kvg[0, crow, :], kvg[1, crow, :], p_b[j, rows, :])
            dqa[rows, :] += dqc
            acc[0] += dk
            acc[1] += dv

    gring.add_send(4, gnear[0])
    aring.forward(1)
    prefix((y + 2) % 4)
    rring.send(1, acc[...])
    prefix((y + 1) % 4)
    rring.send(2, acc[...])
    rring.add_send(4, segt[(y + 1) % 4])

    aring.right(1).wait_recv()
    aring.fwd(1).wait_recv()
    gring.send(1, wgrad((z + 2) % 4, 1))
    gring.send(2, wgrad((z + 1) % 4, 1))
    gnear[1] = wgrad((z + 3) % 4, 1)

    prefix((y + 3) % 4)
    rring.add_send(5, acc[...])
    prefix(y)
    for rb in range(4):
        s, hb = rb // 2, rb % 2
        dqb = (dqa[rb * ROWS:(rb + 1) * ROWS, :] * SCALE).astype(BF)
        for i in range(nh):
            odq[s * SEG:(s + 1) * SEG, (hb * nh + i) * HD:(hb * nh + i + 1) * HD] = dqb[i * SEG:(i + 1) * SEG]

    gring.add_send(5, gnear[1])
    for p in range(2):
        owg[:, p * CH:(p + 1) * CH] = wgrad(z, p)

    lanes = lambda v: pl.ds(pl.multiple_of(v * 256, 256), 256)

    def zk(p):
        return rcopy(zsb.at[p], zrb.at[p], zk_s.at[p], zk_r.at[p], place(x, y, z + 1 - 2 * zl, c))

    for p in range(2):
        for i in ((4, 3), (2, 5))[p]:
            rring.copy(i).wait_recv()
        kown[p] = rring.result(p, segt[y] if p == 0 else acc[...])
        zsb[p] = kown[p, :, :, lanes(1 - zl)].astype(BF)
        zk(p).start()

    gring.wait_result()
    for p in range(2):
        cols = slice(p * CH, (p + 1) * CH)
        owg[:, cols] = gring.result(p, owg[:, cols])

    for p in range(2):
        zk(p).wait_recv()
        for i in range(2):
            t = kown[p, i, :, lanes(zl)] + zrb[p, i].astype(F32)
            if i == 0:
                t = t * SCALE
            okv[2 * (1 - p) + i] = t.T.astype(BF)

    kz().wait_send()
    for p in range(2):
        zk(p).wait_send()

    @pl.when(jnp.logical_not(is_src))
    def _():
        cy().wait_send()

    @pl.when(is_src)
    def _():
        for yy in range(4):
            for k in range(2):
                cx(half, yy, k).wait_send()

    @pl.when(is_mid)
    def _():
        for yy in range(4):
            cx(0, yy, yy // 2).wait_send()

    @pl.when(is_recv)
    def _():
        for h in range(2):
            for yy in range(4):
                cb(h, yy).wait_send()

    for ring in (wring, kring, aring, dring, rring, gring):
        ring.wait_sends()


def finish_kernel(dq, kv, wgr, o0, o1, o2, o3, o4, o5):
    o0[...] = dq[...]
    for i, o in enumerate((o1, o2, o3, o4)):
        o[...] = kv[i]
    o5[...] = wgr[...]


def on_device(
    queries, prefix_keys, prefix_values, keys, values, ancestors, advantages, upstream, out_weight
):
    dma = pltpu.SemaphoreType.DMA
    sds = jax.ShapeDtypeStruct
    vm = pltpu.VMEM
    dq, okv, owg = pl.pallas_call(
        whole_kernel,
        out_shape=(
            sds((TOKL, NCOL), BF),
            sds((4, 256, HD), BF),
            sds((WROWS, NCOL), F32),
        ),
        in_specs=[VM] * 9,
        out_specs=(VM, VM, VM),
        scratch_shapes=[
            vm((TOKL, UCOL), BF),
            vm((2, 4, TOKL, UCOL), BF),
            vm((2 * UCOL, 4 * TOKL), BF),
            vm((4 * WROWS, NCOL), BF),
            vm((4, CTX, HD), BF),
            vm((2, SEGCTX, HD), BF),
            vm((2, SEGCTX, HD), BF),
            vm((6, SEG, NCOL), BF),
            vm((6, SEG, NCOL), BF),
            vm((4, SEG, NCOL), F32),
            vm((TOKL, NCOL), BF),
            vm((ROWS, ALLCTX), F32),
            vm((4, 4 * ROWS, CH), BF),
            vm((4 * ROWS, SEGCTX), BF),
            vm((2, 4 * TOKL, CH), BF),
            vm((4 * ROWS, HD), F32),
            vm((4 * ROWS, HD), F32),
            vm((4, HD, ROWS), BF),
            vm((4 * ROWS, HD), BF),
            vm((4, HD, ROWS), BF),
            vm((4 * ROWS, HD), F32),
            vm((2, HD, CH), F32),
            vm((2, 2, HD, SEGCTX), F32),
            vm((4, 2, HD, CH), F32),
            vm((6, 2, HD, CH), BF),
            vm((6, 2, HD, CH), BF),
            vm((2, 2, HD, 256), BF),
            vm((2, 2, HD, 256), BF),
            vm((2, 2, HD, CH), F32),
            vm((6, WROWS, CH), BF),
            vm((6, WROWS, CH), BF),
            vm((2, WROWS, CH), F32),
            dma, dma((4,)), dma((4, 2)), dma((2, 4)), dma((2, 4)), dma((2, 4)),
            dma((6,)), dma((6,)), dma, dma, dma((6,)), dma((6,)),
            dma((6,)), dma((6,)), dma((6,)), dma((6,)), dma((6,)), dma((6,)),
            dma((2,)), dma((2,)), dma((6,)), dma((6,)),
        ],
        compiler_params=pltpu.CompilerParams(
            collective_id=0, has_side_effects=True, vmem_limit_bytes=VLIM),
        name="whole",
    )(ancestors[0].T, upstream[0], advantages, out_weight, prefix_keys[0], prefix_values[0], keys[0], values[0],
      queries[0])
    outs = pl.pallas_call(
        finish_kernel,
        out_shape=tuple([sds((TOKL, NCOL), BF)] + [sds((256, HD), BF)] * 4 + [sds((WROWS, NCOL), F32)]),
        in_specs=[VM] * 3,
        out_specs=tuple([VM] * 6),
        name="finish",
    )(dq, okv, owg)
    return tuple(o[None] for o in outs[:5]) + (outs[5],)


def solution(mesh):
    return jax.shard_map(
        on_device,
        mesh=mesh,
        in_specs=(
            P("dp", "branch", "tensor"),
            P("dp", "branch", "tensor"),
            P("dp", "branch", "tensor"),
            P("dp", "branch", "tensor"),
            P("dp", "branch", "tensor"),
            P("dp", None, None),
            P("dp", "branch"),
            P("dp", "branch", "tensor"),
            P(("dp", "branch"), "tensor"),
        ),
        out_specs=(
            P("dp", "branch", "tensor"),
            P("dp", "branch", "tensor"),
            P("dp", "branch", "tensor"),
            P("dp", "branch", "tensor"),
            P("dp", "branch", "tensor"),
            P(("dp", "branch"), "tensor"),
        ),
        check_vma=False,
    )
```

```python
import math

import jax
import jax.numpy as jnp
from jax import lax
from jax.experimental import pallas as pl
from jax.experimental.pallas import tpu as pltpu
from jax.sharding import PartitionSpec as P

HD = 128
SEG = 128
GROUP = 8
TOKL = 256
KVB = 8
WROWS = 320
NCOL = 1024
UCOL = 640
CTX = 2048
SEGCTX = 384
ALLCTX = CTX + SEGCTX
CH = 512
ROWS = 512
SCALE = 1.0 / math.sqrt(HD)
LOG2E = 1.4426950408889634
BF = jnp.bfloat16
F32 = jnp.float32
VM = pl.BlockSpec(memory_space=pltpu.VMEM)
VLIM = 60 * 2**20


def coords():
    b = lax.axis_index("branch")
    t = lax.axis_index("tensor")
    return t // 2, b // 2, lax.axis_index("dp") * 2 + b % 2, t % 2


def place(x, y, z, c):
    return {"dp": z // 2, "branch": y * 2 + z % 2, "tensor": x * 2 + c}


def rcopy(src, dst, ss, rs, dev):
    return pltpu.make_async_remote_copy(
        src_ref=src, dst_ref=dst, send_sem=ss, recv_sem=rs,
        device_id=dev, device_id_type=pl.DeviceIdType.MESH,
    )


def signal(sem, dev):
    pl.semaphore_signal(sem, inc=1, device_id=dev, device_id_type=pl.DeviceIdType.MESH)


def nt_dot(a, b):
    return lax.dot_general(a, b, (((1,), (1,)), ((), ())), preferred_element_type=F32)


class GatherRing:
    def __init__(self, me, dev, view, ss, rs):
        self.me, self.dev, self.view, self.ss, self.rs = me, dev, view, ss, rs

    def copy(self, node, piece, kind, step):
        v = self.view(node, piece)
        i = kind * 2 + piece
        return rcopy(v, v, self.ss.at[i], self.rs.at[i], self.dev(step))

    def right(self, p):
        return self.copy(self.me, p, 0, 1)

    def left(self, p):
        return self.copy(self.me, p, 1, 3)

    def fwd(self, p):
        if p == 0:
            return self.copy((self.me + 3) % 4, 0, 2, 1)
        return self.copy((self.me + 1) % 4, 1, 2, 3)

    def send(self, p):
        self.right(p).start()
        self.left(p).start()

    def forward(self, p):
        (self.right if p == 0 else self.left)(p).wait_recv()
        self.fwd(p).start()

    def wait_near(self):
        self.right(1).wait_recv()
        self.left(0).wait_recv()

    def wait_far(self):
        self.fwd(0).wait_recv()
        self.fwd(1).wait_recv()

    def wait_sends(self):
        for p in range(2):
            self.right(p).wait_send()
            self.left(p).wait_send()
            self.fwd(p).wait_send()


class SumRing:
    def __init__(self, dev, sb, rb, ss, rs):
        self.dev, self.sb, self.rb, self.ss, self.rs = dev, sb, rb, ss, rs

    def copy(self, i):
        return rcopy(self.sb.at[i], self.rb.at[i], self.ss.at[i], self.rs.at[i], self.dev(1 if i % 2 == 0 else 3))

    def send(self, i, value):
        self.sb[i] = value.astype(BF)
        self.copy(i).start()

    def add_send(self, i, value):
        self.copy(i - 4).wait_recv()
        self.send(i, value + self.rb[i - 4].astype(F32))

    def wait_result(self):
        for i in range(2, 6):
            self.copy(i).wait_recv()

    def result(self, p, own):
        a, b = ((4, 3), (2, 5))[p]
        return own + self.rb[a].astype(F32) + self.rb[b].astype(F32)

    def wait_sends(self):
        for i in range(6):
            self.copy(i).wait_send()


def whole_kernel(
    anc, up, adv, w, pk, pv, sk, sv, q,
    odq, okv, owg,
    cot, cotb, cott, wg, kvg, kcs, vcs,
    dsb, drb, dnear, dattn,
    s_f, p_b, p_s, attng, il_b, delta, qt, dos, dost, dqa,
    acc, accs, segt, ksb, krb, zsb, zrb, kown,
    gsb, grb, gnear,
    c_s, c_r, x_s, x_r, b_s, b_r, w_s, w_r, kz_s, kz_r, k_s, k_r,
    d_s, d_r, a_s, a_r, r_s, r_r, zk_s, zk_r, g_s, g_r,
):
    x, y, z, c = coords()
    zl = z % 2
    first = lax.axis_index("branch") * 2
    target_y = 2 * (x % 2) + c
    is_recv = c == y % 2
    is_src = target_y == y
    is_mid = is_recv & jnp.logical_not(is_src)
    sib = place(x, y, z, 1 - c)
    cexp = SCALE * LOG2E

    def ydev(d):
        return place(x, (y + d) % 4, z, c)

    def zdev(d):
        return place(x, y, (z + d) % 4, c)

    def xdev(d):
        return place((x + d) % 4, y, z, c)

    bar = pltpu.get_barrier_semaphore()
    for d in range(1, 4):
        signal(bar, ydev(d))
    signal(bar, zdev(1))
    signal(bar, zdev(3))
    signal(bar, sib)

    @pl.when(is_recv)
    def _():
        signal(bar, xdev(1))
        signal(bar, xdev(3))

    @pl.when(is_mid)
    def _():
        for d in range(1, 4):
            signal(bar, place((x + 3) % 4, (y + d) % 4, z, c))

    rows_b = lambda b: pl.ds(pl.multiple_of(b * 256, 256), 256)
    own_rows = rows_b(y * 2 + zl)
    for i, r in enumerate((pk, pv, sk, sv)):
        kvg[i, own_rows, :] = r[...]
    wrow = jnp.broadcast_to(adv[...].astype(F32) * 0.25, (TOKL, TOKL))
    ri = lax.broadcasted_iota(jnp.int32, (TOKL, TOKL), 0)
    ci = lax.broadcasted_iota(jnp.int32, (TOKL, TOKL), 1)
    diag = jnp.where(ri == ci, wrow, 0.0).astype(BF)
    cot[...] = jnp.dot(diag, up[...], preferred_element_type=F32).astype(BF)
    w_half = WROWS // 2
    wview = lambda n, p: wg.at[pl.ds(pl.multiple_of(n * WROWS + p * w_half, 32), w_half)]
    wg[pl.ds(pl.multiple_of(z * WROWS, 64), WROWS), :] = w[...]

    pl.semaphore_wait(bar, 6 + 2 * is_recv.astype(jnp.int32) + 1 - is_src.astype(jnp.int32))

    wring = GatherRing(z, zdev, wview, w_s, w_r)
    kring = GatherRing(y, ydev, lambda n, p: kvg.at[:, rows_b(n * 2 + p)], k_s, k_r)
    aring = GatherRing(
        y, ydev, lambda n, p: attng.at[pl.ds(pl.multiple_of(n * TOKL + p * SEG, SEG), SEG)], a_s, a_r)
    dring = SumRing(ydev, dsb, drb, d_s, d_r)
    rring = SumRing(ydev, ksb, krb, r_s, r_r)
    gring = SumRing(zdev, gsb, grb, g_s, g_r)

    def kz():
        v = kvg.at[:, own_rows]
        return rcopy(v, v, kz_s, kz_r, place(x, y, z + 1 - 2 * zl, c))

    def quarter(n, yy):
        second = (n + y // 2) % 2
        return cotb.at[((n + 4 - second) % 4) // 2, yy, pl.ds(pl.multiple_of(second * SEG, SEG), SEG)]

    def quarter_piece(n, p):
        second = (n + y // 2) % 2
        return cotb.at[((n + 4 - second) % 4) // 2, 2 * p:2 * p + 2, pl.ds(pl.multiple_of(second * SEG, SEG), SEG)]

    xring = GatherRing(x, xdev, quarter_piece, x_s, x_r)

    def cy(second):
        dst = cotb.at[x // 2, y, second * SEG:(second + 1) * SEG]
        return rcopy(cot.at[second * SEG:(second + 1) * SEG], dst, c_s.at[second], c_r.at[y],
                     place((x + second) % 4, target_y, z, c))

    def cy_arrived(yy):
        rcopy(cot.at[0:SEG], quarter(x, yy), c_s.at[0], c_r.at[yy], sib).wait_recv()

    def cb(n, p):
        v = quarter_piece(n, p)
        return rcopy(v, v, b_s.at[n, p], b_r.at[n, p], sib)

    kz().start()
    cy(1).start()

    @pl.when(jnp.logical_not(is_src))
    def _():
        cy(0).start()

    kring.send(zl)

    @pl.when(zl == 0)
    def _():
        for p in range(2):
            wring.left(p).start()

    @pl.when(zl == 1)
    def _():
        for p in range(2):
            wring.right(p).start()

    @pl.when(is_src)
    def _():
        cotb[x // 2, y, 0:SEG] = cot[0:SEG]

    kz().wait_recv()
    kring.send(1 - zl)

    @pl.when(zl == 0)
    def _():
        for p in range(2):
            wring.right(p).start()

    @pl.when(zl == 1)
    def _():
        for p in range(2):
            wring.left(p).start()

    @pl.when(is_recv)
    def _():
        for p in range(2):
            for yy in (2 * p, 2 * p + 1):
                @pl.when(jnp.logical_not(is_src & (yy == y)))
                def _():
                    cy_arrived(yy)
            xring.send(p)
            cb(x, p).start()

    for p in range(2):
        kring.forward(p)

    @pl.when(is_recv)
    def _():
        xring.forward(0)
        cb((x + 3) % 4, 0).start()
        xring.forward(1)
        cb((x + 1) % 4, 1).start()

    for p in range(2):
        wring.forward(p)
    kring.wait_near()
    kring.wait_far()

    lane = lax.broadcasted_iota(jnp.int32, (1, 16), 1)
    named = [[jnp.broadcast_to(jnp.sum(jnp.where(lane == first + s, anc[i:i + 1, :].astype(F32), 0.0),
                                       axis=1, keepdims=True), (1, HD)) for i in range(2)] for s in range(2)]

    def hot(s, i, j):
        return (named[s][i] == float(j)).astype(F32)

    for s in range(2):
        own_seg = pl.ds(pl.multiple_of((first + s) * SEG, SEG), SEG)
        for k, dst in enumerate((kcs, vcs)):
            for i in range(2):
                tot = None
                for j in range(16):
                    v = kvg[2 + k, j * SEG:(j + 1) * SEG, :].astype(F32) * hot(s, i, j)
                    tot = v if tot is None else tot + v
                dst[s, i * SEG:(i + 1) * SEG, :] = tot.astype(BF)
            dst[s, 2 * SEG:, :] = kvg[2 + k, own_seg, :]

    nh = ROWS // SEG

    def forward(rb):
        s, hb = rb // 2, rb % 2
        tok = slice(s * SEG, (s + 1) * SEG)
        rows = slice(rb * ROWS, (rb + 1) * ROWS)
        col = lax.broadcasted_iota(jnp.int32, (ROWS, SEG), 1)
        row = lax.broadcasted_iota(jnp.int32, (ROWS, SEG), 0) % SEG
        shut = [jnp.where(named[s][i] >= 0, 0.0, -1e30) for i in range(2)]
        shut.append(jnp.where(col <= row, 0.0, -1e30))
        heads = [slice((hb * nh + i) * HD, (hb * nh + i + 1) * HD) for i in range(nh)]
        qb = jnp.concatenate([q[tok, h] for h in heads], axis=0)
        qt[rb] = qb.T
        mx = None
        for j in range(5):
            kc = kvg[0, j * CH:(j + 1) * CH, :] if j < 4 else kcs[s]
            sc = nt_dot(qb, kc)
            n = sc.shape[1]
            if j == 4:
                sc = jnp.concatenate([sc[:, i * SEG:(i + 1) * SEG] + shut[i] for i in range(3)], axis=1)
            s_f[:, j * CH:j * CH + n] = sc
            for t in range(n // 128):
                part = sc[:, t * 128:(t + 1) * 128]
                mx = part if mx is None else jnp.maximum(mx, part)
        m = jnp.max(mx, axis=1, keepdims=True)
        lsum = None
        o = None
        for j in range(5):
            vc = kvg[1, j * CH:(j + 1) * CH, :] if j < 4 else vcs[s]
            n = vc.shape[0]
            p = jnp.exp2((s_f[:, j * CH:j * CH + n] - m) * cexp)
            for t in range(n // 128):
                part = p[:, t * 128:(t + 1) * 128]
                lsum = part if lsum is None else lsum + part
            pb = p.astype(BF)
            if j < 4:
                p_b[j, rows, :] = pb
            else:
                p_s[rows, :] = pb
            oc = jnp.dot(pb, vc, preferred_element_type=F32)
            o = oc if o is None else o + oc
        il = jnp.broadcast_to(1.0 / jnp.sum(lsum, axis=1, keepdims=True), (ROWS, HD))
        il_b[rows, :] = il
        ob = (o * il).astype(BF)
        for i, h in enumerate(heads):
            attng[pl.ds(pl.multiple_of(y * TOKL + s * SEG, SEG), SEG), h] = ob[i * SEG:(i + 1) * SEG]

    forward(0)
    forward(1)
    aring.send(0)
    forward(2)

    @pl.when(is_recv)
    def _():
        xring.wait_near()
        cb((x + 3) % 4, 1).start()
        cb((x + 1) % 4, 0).start()
        xring.wait_far()
        for p in range(2):
            cb((x + 2) % 4, p).start()

    forward(3)
    aring.send(1)

    wring.wait_near()
    wring.wait_far()

    @pl.when(jnp.logical_not(is_recv))
    def _():
        for n in range(4):
            for p in range(2):
                cb(n, p).wait_recv()

    def proj(yy, rows):
        return jnp.dot(cotb[0, yy, rows, :], wg[0:UCOL, :], preferred_element_type=F32) + jnp.dot(
            cotb[1, yy, rows, :], wg[UCOL:2 * UCOL, :], preferred_element_type=F32)

    lo, hi = slice(0, SEG), slice(SEG, 2 * SEG)
    dring.send(0, proj((y + 2) % 4, lo))
    dring.send(1, proj((y + 2) % 4, hi))
    dring.send(2, proj((y + 1) % 4, hi))
    dring.send(3, proj((y + 3) % 4, lo))
    dnear[0] = proj((y + 1) % 4, lo)
    dnear[1] = proj((y + 3) % 4, hi)
    dnear[2] = proj(y, lo)
    dnear[3] = proj(y, hi)

    for h in range(2):
        for yy in range(4):
            cott[h * UCOL:(h + 1) * UCOL, yy * TOKL:(yy + 1) * TOKL] = cotb[h, yy].T
    for p in range(2):
        aring.forward(p)
    dring.add_send(4, dnear[0])
    dring.add_send(5, dnear[1])

    aring.wait_near()
    aring.wait_far()

    def wgrad(zz, p):
        rows = pl.ds(pl.multiple_of(zz * WROWS + p * w_half, 32), w_half)
        return jnp.dot(cott[rows, :], attng[...], preferred_element_type=F32)

    gring.send(0, wgrad((z + 2) % 4, 0))
    gring.send(1, wgrad((z + 2) % 4, 1))
    gring.send(2, wgrad((z + 1) % 4, 1))
    gring.send(3, wgrad((z + 3) % 4, 0))
    gnear[0] = wgrad((z + 1) % 4, 0)
    gnear[1] = wgrad((z + 3) % 4, 1)

    dring.wait_result()
    for p in range(2):
        dattn[p * SEG:(p + 1) * SEG, :] = dring.result(p, dnear[2 + p]).astype(BF)
    for rb in range(4):
        s, hb = rb // 2, rb % 2
        rows = slice(rb * ROWS, (rb + 1) * ROWS)
        tok = slice(s * SEG, (s + 1) * SEG)
        arow = pl.ds(pl.multiple_of(y * TOKL + s * SEG, SEG), SEG)
        heads = [slice((hb * nh + i) * HD, (hb * nh + i + 1) * HD) for i in range(nh)]
        dob = jnp.concatenate([dattn[tok, h] for h in heads], axis=0)
        at = jnp.concatenate([attng[arow, h] for h in heads], axis=0)
        db = (dob.astype(F32) * il_b[rows, :]).astype(BF)
        dos[rows, :] = db
        dost[rb] = db.T
        dl = jnp.sum(db.astype(F32) * at.astype(F32), axis=1, keepdims=True)
        delta[rows, :] = jnp.broadcast_to(dl, (ROWS, HD))

    def back(rb, kc, vc, pb):
        rows = pl.ds(pl.multiple_of(rb * ROWS, ROWS), ROWS)
        dl = delta[rows, :]
        n = vc.shape[0]
        dp = nt_dot(dos[rows, :], vc)
        ds = (pb.astype(F32) * (dp - jnp.concatenate([dl] * (n // HD), axis=1))).astype(BF)
        return (rows, jnp.dot(ds, kc, preferred_element_type=F32),
                jnp.dot(qt[rb], ds, preferred_element_type=F32),
                jnp.dot(dost[rb], pb, preferred_element_type=F32))

    for rb in range(4):
        s = rb // 2
        rows, dqc, dk, dv = back(rb, kcs[s], vcs[s], p_s[rb * ROWS:(rb + 1) * ROWS, :])
        dqa[rows, :] = dqc
        if rb % 2 == 0:
            accs[s, 0] = dk
            accs[s, 1] = dv
        else:
            accs[s, 0] += dk
            accs[s, 1] += dv
    for j in range(16):
        for k in range(2):
            tot = None
            for s in range(2):
                for i in range(2):
                    v = accs[s, k, :, i * SEG:(i + 1) * SEG] * hot(s, i, j)
                    tot = v if tot is None else tot + v
            segt[j // 4, k, :, (j % 4) * SEG:(j % 4 + 1) * SEG] = tot
    for s in range(2):
        own_cols = pl.ds(pl.multiple_of((zl * 2 + s) * SEG, SEG), SEG)
        for k in range(2):
            segt[y, k, :, own_cols] += accs[s, k, :, 2 * SEG:]
    rring.send(0, segt[(y + 2) % 4])
    rring.send(3, segt[(y + 3) % 4])
    gring.add_send(4, gnear[0])
    gring.add_send(5, gnear[1])

    def prefix(j):
        acc[...] = jnp.zeros_like(acc)
        crow = pl.ds(pl.multiple_of(j * CH, CH), CH)

        @pl.loop(0, 4)
        def _(rb):
            rows = pl.ds(pl.multiple_of(rb * ROWS, ROWS), ROWS)
            _, dqc, dk, dv = back(rb, kvg[0, crow, :], kvg[1, crow, :], p_b[j, rows, :])
            dqa[rows, :] += dqc
            acc[0] += dk
            acc[1] += dv

    prefix((y + 2) % 4)
    rring.send(1, acc[...])
    rring.add_send(4, segt[(y + 1) % 4])
    prefix((y + 1) % 4)
    rring.send(2, acc[...])
    prefix((y + 3) % 4)
    rring.add_send(5, acc[...])
    prefix(y)
    for rb in range(4):
        s, hb = rb // 2, rb % 2
        dqb = (dqa[rb * ROWS:(rb + 1) * ROWS, :] * SCALE).astype(BF)
        for i in range(nh):
            odq[s * SEG:(s + 1) * SEG, (hb * nh + i) * HD:(hb * nh + i + 1) * HD] = dqb[i * SEG:(i + 1) * SEG]

    for p in range(2):
        owg[p * w_half:(p + 1) * w_half, :] = wgrad(z, p)

    lanes = lambda v: pl.ds(pl.multiple_of(v * 256, 256), 256)

    def zk(p):
        return rcopy(zsb.at[p], zrb.at[p], zk_s.at[p], zk_r.at[p], place(x, y, z + 1 - 2 * zl, c))

    for p in range(2):
        for i in ((4, 3), (2, 5))[p]:
            rring.copy(i).wait_recv()
        kown[p] = rring.result(p, segt[y] if p == 0 else acc[...])
        zsb[p] = kown[p, :, :, lanes(1 - zl)].astype(BF)
        zk(p).start()

    gring.wait_result()
    for p in range(2):
        rows = slice(p * w_half, (p + 1) * w_half)
        owg[rows, :] = gring.result(p, owg[rows, :])

    for p in range(2):
        zk(p).wait_recv()
        for i in range(2):
            t = kown[p, i, :, lanes(zl)] + zrb[p, i].astype(F32)
            if i == 0:
                t = t * SCALE
            okv[2 * (1 - p) + i] = t.T.astype(BF)

    kz().wait_send()
    for p in range(2):
        zk(p).wait_send()

    cy(1).wait_send()

    @pl.when(jnp.logical_not(is_src))
    def _():
        cy(0).wait_send()

    @pl.when(is_recv)
    def _():
        xring.wait_sends()
        for n in range(4):
            for p in range(2):
                cb(n, p).wait_send()

    for ring in (wring, kring, aring, dring, rring, gring):
        ring.wait_sends()


def finish_kernel(dq, kv, wgr, o0, o1, o2, o3, o4, o5):
    o0[...] = dq[...]
    for i, o in enumerate((o1, o2, o3, o4)):
        o[...] = kv[i]
    o5[...] = wgr[...]


def on_device(
    queries, prefix_keys, prefix_values, keys, values, ancestors, advantages, upstream, out_weight
):
    dma = pltpu.SemaphoreType.DMA
    sds = jax.ShapeDtypeStruct
    vm = pltpu.VMEM
    half_w = WROWS // 2
    dq, okv, owg = pl.pallas_call(
        whole_kernel,
        out_shape=(
            sds((TOKL, NCOL), BF),
            sds((4, 256, HD), BF),
            sds((WROWS, NCOL), F32),
        ),
        in_specs=[VM] * 9,
        out_specs=(VM, VM, VM),
        scratch_shapes=[
            vm((TOKL, UCOL), BF),
            vm((2, 4, TOKL, UCOL), BF),
            vm((2 * UCOL, 4 * TOKL), BF),
            vm((4 * WROWS, NCOL), BF),
            vm((4, CTX, HD), BF),
            vm((2, SEGCTX, HD), BF),
            vm((2, SEGCTX, HD), BF),
            vm((6, SEG, NCOL), BF),
            vm((6, SEG, NCOL), BF),
            vm((4, SEG, NCOL), F32),
            vm((TOKL, NCOL), BF),
            vm((ROWS, ALLCTX), F32),
            vm((4, 4 * ROWS, CH), BF),
            vm((4 * ROWS, SEGCTX), BF),
            vm((4 * TOKL, NCOL), BF),
            vm((4 * ROWS, HD), F32),
            vm((4 * ROWS, HD), F32),
            vm((4, HD, ROWS), BF),
            vm((4 * ROWS, HD), BF),
            vm((4, HD, ROWS), BF),
            vm((4 * ROWS, HD), F32),
            vm((2, HD, CH), F32),
            vm((2, 2, HD, SEGCTX), F32),
            vm((4, 2, HD, CH), F32),
            vm((6, 2, HD, CH), BF),
            vm((6, 2, HD, CH), BF),
            vm((2, 2, HD, 256), BF),
            vm((2, 2, HD, 256), BF),
            vm((2, 2, HD, CH), F32),
            vm((6, half_w, NCOL), BF),
            vm((6, half_w, NCOL), BF),
            vm((2, half_w, NCOL), F32),
            dma((2,)), dma((4,)), dma((6,)), dma((6,)), dma((4, 2)), dma((4, 2)),
            dma((6,)), dma((6,)), dma, dma, dma((6,)), dma((6,)),
            dma((6,)), dma((6,)), dma((6,)), dma((6,)), dma((6,)), dma((6,)),
            dma((2,)), dma((2,)), dma((6,)), dma((6,)),
        ],
        compiler_params=pltpu.CompilerParams(
            collective_id=0, has_side_effects=True, vmem_limit_bytes=VLIM),
        name="whole",
    )(ancestors[0].T, upstream[0], advantages, out_weight, prefix_keys[0], prefix_values[0], keys[0], values[0],
      queries[0])
    outs = pl.pallas_call(
        finish_kernel,
        out_shape=tuple([sds((TOKL, NCOL), BF)] + [sds((256, HD), BF)] * 4 + [sds((WROWS, NCOL), F32)]),
        in_specs=[VM] * 3,
        out_specs=tuple([VM] * 6),
        name="finish",
    )(dq, okv, owg)
    return tuple(o[None] for o in outs[:5]) + (outs[5],)


def solution(mesh):
    return jax.shard_map(
        on_device,
        mesh=mesh,
        in_specs=(
            P("dp", "branch", "tensor"),
            P("dp", "branch", "tensor"),
            P("dp", "branch", "tensor"),
            P("dp", "branch", "tensor"),
            P("dp", "branch", "tensor"),
            P("dp", None, None),
            P("dp", "branch"),
            P("dp", "branch", "tensor"),
            P(("dp", "branch"), "tensor"),
        ),
        out_specs=(
            P("dp", "branch", "tensor"),
            P("dp", "branch", "tensor"),
            P("dp", "branch", "tensor"),
            P("dp", "branch", "tensor"),
            P("dp", "branch", "tensor"),
            P(("dp", "branch"), "tensor"),
        ),
        check_vma=False,
    )
```

```python
import math

import jax
import jax.numpy as jnp
from jax import lax
from jax.experimental import pallas as pl
from jax.experimental.pallas import tpu as pltpu
from jax.sharding import PartitionSpec as P

HD = 128
SEG = 128
GROUP = 8
TOKL = 256
KVB = 8
WROWS = 320
NCOL = 1024
UCOL = 640
CTX = 2048
SEGCTX = 384
ALLCTX = CTX + SEGCTX
CH = 512
ROWS = 512
SCALE = 1.0 / math.sqrt(HD)
LOG2E = 1.4426950408889634
BF = jnp.bfloat16
F32 = jnp.float32
VM = pl.BlockSpec(memory_space=pltpu.VMEM)
VLIM = 60 * 2**20


def coords():
    b = lax.axis_index("branch")
    t = lax.axis_index("tensor")
    return t // 2, b // 2, lax.axis_index("dp") * 2 + b % 2, t % 2


def place(x, y, z, c):
    return {"dp": z // 2, "branch": y * 2 + z % 2, "tensor": x * 2 + c}


def rcopy(src, dst, ss, rs, dev):
    return pltpu.make_async_remote_copy(
        src_ref=src, dst_ref=dst, send_sem=ss, recv_sem=rs,
        device_id=dev, device_id_type=pl.DeviceIdType.MESH,
    )


def signal(sem, dev):
    pl.semaphore_signal(sem, inc=1, device_id=dev, device_id_type=pl.DeviceIdType.MESH)


def nt_dot(a, b):
    return lax.dot_general(a, b, (((1,), (1,)), ((), ())), preferred_element_type=F32)


class GatherRing:
    def __init__(self, me, dev, view, ss, rs):
        self.me, self.dev, self.view, self.ss, self.rs = me, dev, view, ss, rs

    def copy(self, node, piece, kind, step):
        v = self.view(node, piece)
        i = kind * 2 + piece
        return rcopy(v, v, self.ss.at[i], self.rs.at[i], self.dev(step))

    def right(self, p):
        return self.copy(self.me, p, 0, 1)

    def left(self, p):
        return self.copy(self.me, p, 1, 3)

    def fwd(self, p):
        if p == 0:
            return self.copy((self.me + 3) % 4, 0, 2, 1)
        return self.copy((self.me + 1) % 4, 1, 2, 3)

    def send(self, p):
        self.right(p).start()
        self.left(p).start()

    def forward(self, p):
        (self.right if p == 0 else self.left)(p).wait_recv()
        self.fwd(p).start()

    def wait_near(self):
        self.right(1).wait_recv()
        self.left(0).wait_recv()

    def wait_far(self):
        self.fwd(0).wait_recv()
        self.fwd(1).wait_recv()

    def wait_sends(self):
        for p in range(2):
            self.right(p).wait_send()
            self.left(p).wait_send()
            self.fwd(p).wait_send()


class SumRing:
    def __init__(self, dev, sb, rb, ss, rs):
        self.dev, self.sb, self.rb, self.ss, self.rs = dev, sb, rb, ss, rs

    def copy(self, i):
        return rcopy(self.sb.at[i], self.rb.at[i], self.ss.at[i], self.rs.at[i], self.dev(1 if i % 2 == 0 else 3))

    def send(self, i, value):
        self.sb[i] = value.astype(BF)
        self.copy(i).start()

    def add_send(self, i, value):
        self.copy(i - 4).wait_recv()
        self.send(i, value + self.rb[i - 4].astype(F32))

    def wait_result(self):
        for i in range(2, 6):
            self.copy(i).wait_recv()

    def result(self, p, own):
        a, b = ((4, 3), (2, 5))[p]
        return own + self.rb[a].astype(F32) + self.rb[b].astype(F32)

    def wait_sends(self):
        for i in range(6):
            self.copy(i).wait_send()


def whole_kernel(
    anc, up, adv, w, pk, pv, sk, sv, q,
    odq, okv, owg,
    cot, cotb, cott, wg, kvg, kcs, vcs,
    dsb, drb, dnear, dattn,
    s_f, p_b, p_s, attng, il_b, delta, qt, dos, dost, dqa,
    acc, accs, segt, ksb, krb, zsb, zrb, kown,
    gsb, grb, gnear,
    c_s, c_r, x_s, x_r, b_s, b_r, w_s, w_r, kz_s, kz_r, k_s, k_r,
    d_s, d_r, a_s, a_r, r_s, r_r, zk_s, zk_r, g_s, g_r,
):
    x, y, z, c = coords()
    zl = z % 2
    first = lax.axis_index("branch") * 2
    target_y = 2 * (x % 2) + c
    is_recv = c == y % 2
    is_src = target_y == y
    is_mid = is_recv & jnp.logical_not(is_src)
    sib = place(x, y, z, 1 - c)
    cexp = SCALE * LOG2E

    def ydev(d):
        return place(x, (y + d) % 4, z, c)

    def zdev(d):
        return place(x, y, (z + d) % 4, c)

    def xdev(d):
        return place((x + d) % 4, y, z, c)

    bar = pltpu.get_barrier_semaphore()
    for d in range(1, 4):
        signal(bar, ydev(d))
    signal(bar, zdev(1))
    signal(bar, zdev(3))
    signal(bar, sib)

    @pl.when(is_recv)
    def _():
        signal(bar, xdev(1))
        signal(bar, xdev(3))

    @pl.when(is_mid)
    def _():
        for d in range(1, 4):
            signal(bar, place((x + 3) % 4, (y + d) % 4, z, c))

    rows_b = lambda b: pl.ds(pl.multiple_of(b * 256, 256), 256)
    own_rows = rows_b(y * 2 + zl)
    for i, r in enumerate((pk, pv, sk, sv)):
        kvg[i, own_rows, :] = r[...]
    wrow = jnp.broadcast_to(adv[...].astype(F32) * 0.25, (TOKL, TOKL))
    ri = lax.broadcasted_iota(jnp.int32, (TOKL, TOKL), 0)
    ci = lax.broadcasted_iota(jnp.int32, (TOKL, TOKL), 1)
    diag = jnp.where(ri == ci, wrow, 0.0).astype(BF)
    cot[...] = jnp.dot(diag, up[...], preferred_element_type=F32).astype(BF)
    w_half = WROWS // 2
    wview = lambda n, p: wg.at[pl.ds(pl.multiple_of(n * WROWS + p * w_half, 32), w_half)]
    wg[pl.ds(pl.multiple_of(z * WROWS, 64), WROWS), :] = w[...]

    pl.semaphore_wait(bar, 6 + 2 * is_recv.astype(jnp.int32) + 1 - is_src.astype(jnp.int32))

    wring = GatherRing(z, zdev, wview, w_s, w_r)
    kring = GatherRing(y, ydev, lambda n, p: kvg.at[:, rows_b(n * 2 + p)], k_s, k_r)
    aring = GatherRing(
        y, ydev, lambda n, p: attng.at[pl.ds(pl.multiple_of(n * TOKL + p * SEG, SEG), SEG)], a_s, a_r)
    dring = SumRing(ydev, dsb, drb, d_s, d_r)
    rring = SumRing(ydev, ksb, krb, r_s, r_r)
    gring = SumRing(zdev, gsb, grb, g_s, g_r)

    def kz():
        v = kvg.at[:, own_rows]
        return rcopy(v, v, kz_s, kz_r, place(x, y, z + 1 - 2 * zl, c))

    def quarter(n, yy):
        second = (n + y // 2) % 2
        return cotb.at[((n + 4 - second) % 4) // 2, yy, pl.ds(pl.multiple_of(second * SEG, SEG), SEG)]

    def quarter_piece(n, p):
        second = (n + y // 2) % 2
        return cotb.at[((n + 4 - second) % 4) // 2, 2 * p:2 * p + 2, pl.ds(pl.multiple_of(second * SEG, SEG), SEG)]

    xring = GatherRing(x, xdev, quarter_piece, x_s, x_r)

    def cy(second):
        dst = cotb.at[x // 2, y, second * SEG:(second + 1) * SEG]
        return rcopy(cot.at[second * SEG:(second + 1) * SEG], dst, c_s.at[second], c_r.at[y],
                     place((x + second) % 4, target_y, z, c))

    def cy_arrived(yy):
        rcopy(cot.at[0:SEG], quarter(x, yy), c_s.at[0], c_r.at[yy], sib).wait_recv()

    def cb(n, p):
        v = quarter_piece(n, p)
        return rcopy(v, v, b_s.at[n, p], b_r.at[n, p], sib)

    kz().start()
    cy(1).start()

    @pl.when(jnp.logical_not(is_src))
    def _():
        cy(0).start()

    kring.send(zl)

    @pl.when(zl == 0)
    def _():
        for p in range(2):
            wring.left(p).start()

    @pl.when(zl == 1)
    def _():
        for p in range(2):
            wring.right(p).start()

    @pl.when(is_src)
    def _():
        cotb[x // 2, y, 0:SEG] = cot[0:SEG]

    kz().wait_recv()
    kring.send(1 - zl)

    @pl.when(zl == 0)
    def _():
        for p in range(2):
            wring.right(p).start()

    @pl.when(zl == 1)
    def _():
        for p in range(2):
            wring.left(p).start()

    @pl.when(is_recv)
    def _():
        for p in range(2):
            for yy in (2 * p, 2 * p + 1):
                @pl.when(jnp.logical_not(is_src & (yy == y)))
                def _():
                    cy_arrived(yy)
            xring.send(p)
            cb(x, p).start()

    for p in range(2):
        kring.forward(p)

    @pl.when(is_recv)
    def _():
        xring.forward(0)
        cb((x + 3) % 4, 0).start()
        xring.forward(1)
        cb((x + 1) % 4, 1).start()

    @pl.when(zl == 0)
    def _():
        wring.forward(0)

    @pl.when(zl == 1)
    def _():
        wring.forward(1)

    kring.wait_near()
    nh = ROWS // SEG

    def spot(rb):
        s, hb = rb // 2, rb % 2
        return s, hb, slice(s * SEG, (s + 1) * SEG), slice(rb * ROWS, (rb + 1) * ROWS), [
            slice((hb * nh + i) * HD, (hb * nh + i + 1) * HD) for i in range(nh)]

    def crow(j):
        return pl.ds(pl.multiple_of(j * CH, CH), CH)

    def lane_max(sc, mx):
        for t in range(sc.shape[1] // HD):
            part = sc[:, t * HD:(t + 1) * HD]
            mx = part if mx is None else jnp.maximum(mx, part)
        return mx

    def lane_sum(p, tot):
        for t in range(p.shape[1] // HD):
            part = p[:, t * HD:(t + 1) * HD]
            tot = part if tot is None else tot + part
        return tot

    def forward_near(rb):
        s, hb, tok, rows, heads = spot(rb)
        qb = jnp.concatenate([q[tok, h] for h in heads], axis=0)
        qt[rb] = qb.T
        mx = None
        for i, d in enumerate((0, 1, 3)):
            sc = nt_dot(qb, kvg[0, crow((y + d) % 4), :])
            s_f[:, i * CH:(i + 1) * CH] = sc
            mx = lane_max(sc, mx)
        m = jnp.max(mx, axis=1, keepdims=True)
        lsum = None
        o = None
        for i, d in enumerate((0, 1, 3)):
            j = (y + d) % 4
            p = jnp.exp2((s_f[:, i * CH:(i + 1) * CH] - m) * cexp)
            lsum = lane_sum(p, lsum)
            pb = p.astype(BF)
            p_b[j, rows, :] = pb
            oc = jnp.dot(pb, kvg[1, crow(j), :], preferred_element_type=F32)
            o = oc if o is None else o + oc
        delta[0, rows, :] = lsum
        delta[1, rows, :] = jnp.broadcast_to(m, (ROWS, HD))
        dqa[rows, :] = o

    for rb in range(4):
        forward_near(rb)

    @pl.when(zl == 0)
    def _():
        wring.forward(1)

    @pl.when(zl == 1)
    def _():
        wring.forward(0)

    kring.wait_far()

    lane = lax.broadcasted_iota(jnp.int32, (1, 16), 1)
    named = [[jnp.broadcast_to(jnp.sum(jnp.where(lane == first + s, anc[i:i + 1, :].astype(F32), 0.0),
                                       axis=1, keepdims=True), (1, HD)) for i in range(2)] for s in range(2)]

    def hot(s, i, j):
        return (named[s][i] == float(j)).astype(F32)

    for s in range(2):
        own_seg = pl.ds(pl.multiple_of((first + s) * SEG, SEG), SEG)
        for k, dst in enumerate((kcs, vcs)):
            for i in range(2):
                tot = None
                for j in range(16):
                    v = kvg[2 + k, j * SEG:(j + 1) * SEG, :] * hot(s, i, j).astype(BF)
                    tot = v if tot is None else tot + v
                dst[s, i * SEG:(i + 1) * SEG, :] = tot
            dst[s, 2 * SEG:, :] = kvg[2 + k, own_seg, :]

    def forward_far(rb):
        s, hb, tok, rows, heads = spot(rb)
        col = lax.broadcasted_iota(jnp.int32, (ROWS, SEG), 1)
        row = lax.broadcasted_iota(jnp.int32, (ROWS, SEG), 0) % SEG
        shut = [jnp.where(named[s][i] >= 0, 0.0, -1e30) for i in range(2)]
        shut.append(jnp.where(col <= row, 0.0, -1e30))
        qb = jnp.concatenate([q[tok, h] for h in heads], axis=0)
        far = (y + 2) % 4
        sc = nt_dot(qb, kvg[0, crow(far), :])
        s_f[:, 0:CH] = sc
        mx = lane_max(sc, None)
        sc = nt_dot(qb, kcs[s])
        sc = jnp.concatenate([sc[:, i * SEG:(i + 1) * SEG] + shut[i] for i in range(3)], axis=1)
        s_f[:, CH:CH + SEGCTX] = sc
        mx = lane_max(sc, mx)
        m_near = delta[1, rows, 0:1]
        m = jnp.maximum(jnp.max(mx, axis=1, keepdims=True), m_near)
        p = jnp.exp2((s_f[:, 0:CH] - m) * cexp)
        lsum = lane_sum(p, None)
        pb = p.astype(BF)
        p_b[far, rows, :] = pb
        o = jnp.dot(pb, kvg[1, crow(far), :], preferred_element_type=F32)
        p = jnp.exp2((s_f[:, CH:CH + SEGCTX] - m) * cexp)
        lsum = lane_sum(p, lsum)
        pb = p.astype(BF)
        p_s[rows, :] = pb
        o = o + jnp.dot(pb, vcs[s], preferred_element_type=F32)
        ratio = jnp.broadcast_to(jnp.exp2((m_near - m) * cexp), (ROWS, HD))
        lsum = lsum + delta[0, rows, :] * ratio
        o = o + dqa[rows, :] * ratio
        il = jnp.broadcast_to(1.0 / jnp.sum(lsum, axis=1, keepdims=True), (ROWS, HD))
        il_b[0, rows, :] = il
        il_b[1, rows, :] = il * ratio
        ob = (o * il).astype(BF)
        for i, h in enumerate(heads):
            attng[pl.ds(pl.multiple_of(y * TOKL + s * SEG, SEG), SEG), h] = ob[i * SEG:(i + 1) * SEG]

    forward_far(0)
    forward_far(1)
    aring.send(0)
    forward_far(2)
    forward_far(3)
    aring.send(1)

    @pl.when(is_recv)
    def _():
        xring.wait_near()
        cb((x + 3) % 4, 1).start()
        cb((x + 1) % 4, 0).start()
        xring.wait_far()
        for p in range(2):
            cb((x + 2) % 4, p).start()

    wring.wait_near()
    wring.wait_far()

    @pl.when(jnp.logical_not(is_recv))
    def _():
        for n in range(4):
            for p in range(2):
                cb(n, p).wait_recv()

    def proj(yy, rows):
        return jnp.dot(cotb[0, yy, rows, :], wg[0:UCOL, :], preferred_element_type=F32) + jnp.dot(
            cotb[1, yy, rows, :], wg[UCOL:2 * UCOL, :], preferred_element_type=F32)

    lo, hi = slice(0, SEG), slice(SEG, 2 * SEG)
    dring.send(0, proj((y + 2) % 4, lo))
    dring.send(1, proj((y + 2) % 4, hi))
    dring.send(2, proj((y + 1) % 4, hi))
    dring.send(3, proj((y + 3) % 4, lo))
    dnear[0] = proj((y + 1) % 4, lo)
    dnear[1] = proj((y + 3) % 4, hi)
    dnear[2] = proj(y, lo)
    dnear[3] = proj(y, hi)

    for h in range(2):
        for yy in range(4):
            cott[h * UCOL:(h + 1) * UCOL, yy * TOKL:(yy + 1) * TOKL] = cotb[h, yy].T
    for p in range(2):
        aring.forward(p)
    dring.add_send(4, dnear[0])
    dring.add_send(5, dnear[1])

    aring.wait_near()
    aring.wait_far()

    def wgrad(zz, p):
        rows = pl.ds(pl.multiple_of(zz * WROWS + p * w_half, 32), w_half)
        return jnp.dot(cott[rows, :], attng[...], preferred_element_type=F32)

    gring.send(0, wgrad((z + 2) % 4, 0))
    gring.send(1, wgrad((z + 2) % 4, 1))
    gring.send(2, wgrad((z + 1) % 4, 1))
    gring.send(3, wgrad((z + 3) % 4, 0))
    gnear[0] = wgrad((z + 1) % 4, 0)
    gnear[1] = wgrad((z + 3) % 4, 1)

    dring.wait_result()
    for p in range(2):
        dattn[p * SEG:(p + 1) * SEG, :] = dring.result(p, dnear[2 + p]).astype(BF)
    def scale_grads(g):
        for rb in range(4):
            s, hb, tok, rows, heads = spot(rb)
            arow = pl.ds(pl.multiple_of(y * TOKL + s * SEG, SEG), SEG)
            dob = jnp.concatenate([dattn[tok, h] for h in heads], axis=0)
            at = jnp.concatenate([attng[arow, h] for h in heads], axis=0)
            db = (dob.astype(F32) * il_b[g, rows, :]).astype(BF)
            dos[g, rows, :] = db
            dost[g, rb] = db.T
            dl = jnp.sum(db.astype(F32) * at.astype(F32), axis=1, keepdims=True)
            delta[g, rows, :] = jnp.broadcast_to(dl, (ROWS, HD))

    def back(g, rb, kc, vc, pb):
        rows = pl.ds(pl.multiple_of(rb * ROWS, ROWS), ROWS)
        dl = delta[g, rows, :]
        n = vc.shape[0]
        dp = nt_dot(dos[g, rows, :], vc)
        ds = (pb.astype(F32) * (dp - jnp.concatenate([dl] * (n // HD), axis=1))).astype(BF)
        return (rows, jnp.dot(ds, kc, preferred_element_type=F32),
                jnp.dot(qt[rb], ds, preferred_element_type=F32),
                jnp.dot(dost[g, rb], pb, preferred_element_type=F32))

    def prefix(g, j):
        acc[...] = jnp.zeros_like(acc)

        @pl.loop(0, 4)
        def _(rb):
            rows = pl.ds(pl.multiple_of(rb * ROWS, ROWS), ROWS)
            _, dqc, dk, dv = back(g, rb, kvg[0, crow(j), :], kvg[1, crow(j), :], p_b[j, rows, :])
            dqa[rows, :] += dqc
            acc[0] += dk
            acc[1] += dv

    scale_grads(0)
    dqa[...] = jnp.zeros_like(dqa)
    prefix(0, (y + 2) % 4)
    rring.send(1, acc[...])

    for rb in range(4):
        s = rb // 2
        rows, dqc, dk, dv = back(0, rb, kcs[s], vcs[s], p_s[rb * ROWS:(rb + 1) * ROWS, :])
        dqa[rows, :] += dqc
        if rb % 2 == 0:
            accs[s, 0] = dk
            accs[s, 1] = dv
        else:
            accs[s, 0] += dk
            accs[s, 1] += dv
    for j in range(16):
        for k in range(2):
            tot = None
            for s in range(2):
                for i in range(2):
                    v = accs[s, k, :, i * SEG:(i + 1) * SEG] * hot(s, i, j)
                    tot = v if tot is None else tot + v
            segt[j // 4, k, :, (j % 4) * SEG:(j % 4 + 1) * SEG] = tot
    for s in range(2):
        own_cols = pl.ds(pl.multiple_of((zl * 2 + s) * SEG, SEG), SEG)
        for k in range(2):
            segt[y, k, :, own_cols] += accs[s, k, :, 2 * SEG:]
    rring.send(0, segt[(y + 2) % 4])
    rring.send(3, segt[(y + 3) % 4])
    gring.add_send(4, gnear[0])
    gring.add_send(5, gnear[1])

    scale_grads(1)
    prefix(1, (y + 1) % 4)
    rring.send(2, acc[...])
    rring.add_send(4, segt[(y + 1) % 4])
    prefix(1, (y + 3) % 4)
    rring.add_send(5, acc[...])
    prefix(1, y)
    for rb in range(4):
        s, hb = rb // 2, rb % 2
        dqb = (dqa[rb * ROWS:(rb + 1) * ROWS, :] * SCALE).astype(BF)
        for i in range(nh):
            odq[s * SEG:(s + 1) * SEG, (hb * nh + i) * HD:(hb * nh + i + 1) * HD] = dqb[i * SEG:(i + 1) * SEG]

    for p in range(2):
        owg[p * w_half:(p + 1) * w_half, :] = wgrad(z, p)

    lanes = lambda v: pl.ds(pl.multiple_of(v * 256, 256), 256)

    def zk(p):
        return rcopy(zsb.at[p], zrb.at[p], zk_s.at[p], zk_r.at[p], place(x, y, z + 1 - 2 * zl, c))

    for p in range(2):
        for i in ((4, 3), (2, 5))[p]:
            rring.copy(i).wait_recv()
        kown[p] = rring.result(p, segt[y] if p == 0 else acc[...])
        zsb[p] = kown[p, :, :, lanes(1 - zl)].astype(BF)
        zk(p).start()

    gring.wait_result()
    for p in range(2):
        rows = slice(p * w_half, (p + 1) * w_half)
        owg[rows, :] = gring.result(p, owg[rows, :])

    for p in range(2):
        zk(p).wait_recv()
        for i in range(2):
            t = kown[p, i, :, lanes(zl)] + zrb[p, i].astype(F32)
            if i == 0:
                t = t * SCALE
            okv[2 * (1 - p) + i] = t.T.astype(BF)

    kz().wait_send()
    for p in range(2):
        zk(p).wait_send()

    cy(1).wait_send()

    @pl.when(jnp.logical_not(is_src))
    def _():
        cy(0).wait_send()

    @pl.when(is_recv)
    def _():
        xring.wait_sends()
        for n in range(4):
            for p in range(2):
                cb(n, p).wait_send()

    for ring in (wring, kring, aring, dring, rring, gring):
        ring.wait_sends()


def finish_kernel(dq, kv, wgr, o0, o1, o2, o3, o4, o5):
    o0[...] = dq[...]
    for i, o in enumerate((o1, o2, o3, o4)):
        o[...] = kv[i]
    o5[...] = wgr[...]


def on_device(
    queries, prefix_keys, prefix_values, keys, values, ancestors, advantages, upstream, out_weight
):
    dma = pltpu.SemaphoreType.DMA
    sds = jax.ShapeDtypeStruct
    vm = pltpu.VMEM
    half_w = WROWS // 2
    dq, okv, owg = pl.pallas_call(
        whole_kernel,
        out_shape=(
            sds((TOKL, NCOL), BF),
            sds((4, 256, HD), BF),
            sds((WROWS, NCOL), F32),
        ),
        in_specs=[VM] * 9,
        out_specs=(VM, VM, VM),
        scratch_shapes=[
            vm((TOKL, UCOL), BF),
            vm((2, 4, TOKL, UCOL), BF),
            vm((2 * UCOL, 4 * TOKL), BF),
            vm((4 * WROWS, NCOL), BF),
            vm((4, CTX, HD), BF),
            vm((2, SEGCTX, HD), BF),
            vm((2, SEGCTX, HD), BF),
            vm((6, SEG, NCOL), BF),
            vm((6, SEG, NCOL), BF),
            vm((4, SEG, NCOL), F32),
            vm((TOKL, NCOL), BF),
            vm((ROWS, 3 * CH), F32),
            vm((4, 4 * ROWS, CH), BF),
            vm((4 * ROWS, SEGCTX), BF),
            vm((4 * TOKL, NCOL), BF),
            vm((2, 4 * ROWS, HD), F32),
            vm((2, 4 * ROWS, HD), F32),
            vm((4, HD, ROWS), BF),
            vm((2, 4 * ROWS, HD), BF),
            vm((2, 4, HD, ROWS), BF),
            vm((4 * ROWS, HD), F32),
            vm((2, HD, CH), F32),
            vm((2, 2, HD, SEGCTX), F32),
            vm((4, 2, HD, CH), F32),
            vm((6, 2, HD, CH), BF),
            vm((6, 2, HD, CH), BF),
            vm((2, 2, HD, 256), BF),
            vm((2, 2, HD, 256), BF),
            vm((2, 2, HD, CH), F32),
            vm((6, half_w, NCOL), BF),
            vm((6, half_w, NCOL), BF),
            vm((2, half_w, NCOL), F32),
            dma((2,)), dma((4,)), dma((6,)), dma((6,)), dma((4, 2)), dma((4, 2)),
            dma((6,)), dma((6,)), dma, dma, dma((6,)), dma((6,)),
            dma((6,)), dma((6,)), dma((6,)), dma((6,)), dma((6,)), dma((6,)),
            dma((2,)), dma((2,)), dma((6,)), dma((6,)),
        ],
        compiler_params=pltpu.CompilerParams(
            collective_id=0, has_side_effects=True, vmem_limit_bytes=VLIM),
        name="whole",
    )(ancestors[0].T, upstream[0], advantages, out_weight, prefix_keys[0], prefix_values[0], keys[0], values[0],
      queries[0])
    outs = pl.pallas_call(
        finish_kernel,
        out_shape=tuple([sds((TOKL, NCOL), BF)] + [sds((256, HD), BF)] * 4 + [sds((WROWS, NCOL), F32)]),
        in_specs=[VM] * 3,
        out_specs=tuple([VM] * 6),
        name="finish",
    )(dq, okv, owg)
    return tuple(o[None] for o in outs[:5]) + (outs[5],)


def solution(mesh):
    return jax.shard_map(
        on_device,
        mesh=mesh,
        in_specs=(
            P("dp", "branch", "tensor"),
            P("dp", "branch", "tensor"),
            P("dp", "branch", "tensor"),
            P("dp", "branch", "tensor"),
            P("dp", "branch", "tensor"),
            P("dp", None, None),
            P("dp", "branch"),
            P("dp", "branch", "tensor"),
            P(("dp", "branch"), "tensor"),
        ),
        out_specs=(
            P("dp", "branch", "tensor"),
            P("dp", "branch", "tensor"),
            P("dp", "branch", "tensor"),
            P("dp", "branch", "tensor"),
            P("dp", "branch", "tensor"),
            P(("dp", "branch"), "tensor"),
        ),
        check_vma=False,
    )
```

```python
import math

import jax
import jax.numpy as jnp
from jax import lax
from jax.experimental import pallas as pl
from jax.experimental.pallas import tpu as pltpu
from jax.sharding import PartitionSpec as P

HD = 128
SEG = 128
GROUP = 8
TOKL = 256
KVB = 8
WROWS = 320
NCOL = 1024
UCOL = 640
CTX = 2048
SEGCTX = 384
ALLCTX = CTX + SEGCTX
CH = 512
ROWS = 512
SCALE = 1.0 / math.sqrt(HD)
LOG2E = 1.4426950408889634
BF = jnp.bfloat16
F32 = jnp.float32
VM = pl.BlockSpec(memory_space=pltpu.VMEM)
VLIM = 60 * 2**20


def coords():
    b = lax.axis_index("branch")
    t = lax.axis_index("tensor")
    return t // 2, b // 2, lax.axis_index("dp") * 2 + b % 2, t % 2


def place(x, y, z, c):
    return {"dp": z // 2, "branch": y * 2 + z % 2, "tensor": x * 2 + c}


def rcopy(src, dst, ss, rs, dev):
    return pltpu.make_async_remote_copy(
        src_ref=src, dst_ref=dst, send_sem=ss, recv_sem=rs,
        device_id=dev, device_id_type=pl.DeviceIdType.MESH,
    )


def signal(sem, dev):
    pl.semaphore_signal(sem, inc=1, device_id=dev, device_id_type=pl.DeviceIdType.MESH)


def nt_dot(a, b):
    return lax.dot_general(a, b, (((1,), (1,)), ((), ())), preferred_element_type=F32)


class GatherRing:
    def __init__(self, me, dev, view, ss, rs):
        self.me, self.dev, self.view, self.ss, self.rs = me, dev, view, ss, rs

    def copy(self, node, piece, kind, step):
        v = self.view(node, piece)
        i = kind * 2 + piece
        return rcopy(v, v, self.ss.at[i], self.rs.at[i], self.dev(step))

    def right(self, p):
        return self.copy(self.me, p, 0, 1)

    def left(self, p):
        return self.copy(self.me, p, 1, 3)

    def fwd(self, p):
        if p == 0:
            return self.copy((self.me + 3) % 4, 0, 2, 1)
        return self.copy((self.me + 1) % 4, 1, 2, 3)

    def send(self, p):
        self.right(p).start()
        self.left(p).start()

    def forward(self, p):
        (self.right if p == 0 else self.left)(p).wait_recv()
        self.fwd(p).start()

    def wait_near(self):
        self.right(1).wait_recv()
        self.left(0).wait_recv()

    def wait_far(self):
        self.fwd(0).wait_recv()
        self.fwd(1).wait_recv()

    def wait_sends(self):
        for p in range(2):
            self.right(p).wait_send()
            self.left(p).wait_send()
            self.fwd(p).wait_send()


class SumRing:
    def __init__(self, dev, sb, rb, ss, rs):
        self.dev, self.sb, self.rb, self.ss, self.rs = dev, sb, rb, ss, rs

    def copy(self, i):
        return rcopy(self.sb.at[i], self.rb.at[i], self.ss.at[i], self.rs.at[i], self.dev(1 if i % 2 == 0 else 3))

    def send(self, i, value):
        self.sb[i] = value.astype(BF)
        self.copy(i).start()

    def add_send(self, i, value):
        self.copy(i - 4).wait_recv()
        self.send(i, value + self.rb[i - 4].astype(F32))

    def wait_result(self):
        for i in range(2, 6):
            self.copy(i).wait_recv()

    def result(self, p, own):
        a, b = ((4, 3), (2, 5))[p]
        return own + self.rb[a].astype(F32) + self.rb[b].astype(F32)

    def wait_sends(self):
        for i in range(6):
            self.copy(i).wait_send()


def whole_kernel(
    anc, up, adv, w, pk, pv, sk, sv, q,
    odq, okv, owg,
    cot, cotb, cott, wg, kvg, kcs, vcs,
    dsb, drb, dnear, dattn,
    s_f, p_b, p_s, attng, il_b, delta, qt, dos, dost, dqa,
    acc, accs, segt, ksb, krb, zsb, zrb, kown,
    gsb, grb, gnear,
    c_s, c_r, x_s, x_r, b_s, b_r, w_s, w_r, kz_s, kz_r, k_s, k_r,
    d_s, d_r, a_s, a_r, r_s, r_r, zk_s, zk_r, g_s, g_r,
):
    x, y, z, c = coords()
    zl = z % 2
    first = lax.axis_index("branch") * 2
    target_y = 2 * (x % 2) + c
    is_recv = c == y % 2
    is_src = target_y == y
    is_mid = is_recv & jnp.logical_not(is_src)
    sib = place(x, y, z, 1 - c)
    cexp = SCALE * LOG2E

    def ydev(d):
        return place(x, (y + d) % 4, z, c)

    def zdev(d):
        return place(x, y, (z + d) % 4, c)

    def xdev(d):
        return place((x + d) % 4, y, z, c)

    bar = pltpu.get_barrier_semaphore()
    for d in range(1, 4):
        signal(bar, ydev(d))
    signal(bar, zdev(1))
    signal(bar, zdev(3))
    signal(bar, sib)

    @pl.when(is_recv)
    def _():
        signal(bar, xdev(1))
        signal(bar, xdev(3))

    @pl.when(is_mid)
    def _():
        for d in range(1, 4):
            signal(bar, place((x + 3) % 4, (y + d) % 4, z, c))

    rows_b = lambda b: pl.ds(pl.multiple_of(b * 256, 256), 256)
    own_rows = rows_b(y * 2 + zl)
    for i, r in enumerate((pk, pv, sk, sv)):
        kvg[i, own_rows, :] = r[...]
    wrow = jnp.broadcast_to(adv[...].astype(F32) * 0.25, (TOKL, TOKL))
    ri = lax.broadcasted_iota(jnp.int32, (TOKL, TOKL), 0)
    ci = lax.broadcasted_iota(jnp.int32, (TOKL, TOKL), 1)
    diag = jnp.where(ri == ci, wrow, 0.0).astype(BF)
    cot[...] = jnp.dot(diag, up[...], preferred_element_type=F32).astype(BF)
    w_half = WROWS // 2
    wview = lambda n, p: wg.at[pl.ds(pl.multiple_of(n * WROWS + p * w_half, 32), w_half)]
    wg[pl.ds(pl.multiple_of(z * WROWS, 64), WROWS), :] = w[...]

    pl.semaphore_wait(bar, 6 + 2 * is_recv.astype(jnp.int32) + 1 - is_src.astype(jnp.int32))

    wring = GatherRing(z, zdev, wview, w_s, w_r)
    kring = GatherRing(y, ydev, lambda n, p: kvg.at[:, rows_b(n * 2 + p)], k_s, k_r)
    aring = GatherRing(
        y, ydev, lambda n, p: attng.at[pl.ds(pl.multiple_of(n * TOKL + p * SEG, SEG), SEG)], a_s, a_r)
    dring = SumRing(ydev, dsb, drb, d_s, d_r)
    rring = SumRing(ydev, ksb, krb, r_s, r_r)
    gring = SumRing(zdev, gsb, grb, g_s, g_r)

    def kz():
        v = kvg.at[:, own_rows]
        return rcopy(v, v, kz_s, kz_r, place(x, y, z + 1 - 2 * zl, c))

    def quarter(n, yy):
        second = (n + y // 2) % 2
        return cotb.at[((n + 4 - second) % 4) // 2, yy, pl.ds(pl.multiple_of(second * SEG, SEG), SEG)]

    def quarter_piece(n, p):
        second = (n + y // 2) % 2
        return cotb.at[((n + 4 - second) % 4) // 2, 2 * p:2 * p + 2, pl.ds(pl.multiple_of(second * SEG, SEG), SEG)]

    xring = GatherRing(x, xdev, quarter_piece, x_s, x_r)

    def cy(second):
        dst = cotb.at[x // 2, y, second * SEG:(second + 1) * SEG]
        return rcopy(cot.at[second * SEG:(second + 1) * SEG], dst, c_s.at[second], c_r.at[y],
                     place((x + second) % 4, target_y, z, c))

    def cy_arrived(yy):
        rcopy(cot.at[0:SEG], quarter(x, yy), c_s.at[0], c_r.at[yy], sib).wait_recv()

    def cb(n, p):
        v = quarter_piece(n, p)
        return rcopy(v, v, b_s.at[n, p], b_r.at[n, p], sib)

    kz().start()
    cy(1).start()

    @pl.when(jnp.logical_not(is_src))
    def _():
        cy(0).start()

    kring.send(zl)

    @pl.when(zl == 0)
    def _():
        for p in range(2):
            wring.left(p).start()

    @pl.when(zl == 1)
    def _():
        for p in range(2):
            wring.right(p).start()

    @pl.when(is_src)
    def _():
        cotb[x // 2, y, 0:SEG] = cot[0:SEG]

    kz().wait_recv()
    kring.send(1 - zl)

    @pl.when(zl == 0)
    def _():
        for p in range(2):
            wring.right(p).start()

    @pl.when(zl == 1)
    def _():
        for p in range(2):
            wring.left(p).start()

    @pl.when(is_recv)
    def _():
        for p in range(2):
            for yy in (2 * p, 2 * p + 1):
                @pl.when(jnp.logical_not(is_src & (yy == y)))
                def _():
                    cy_arrived(yy)
            xring.send(p)
            cb(x, p).start()

    for p in range(2):
        kring.forward(p)

    @pl.when(is_recv)
    def _():
        xring.forward(0)
        cb((x + 3) % 4, 0).start()
        xring.forward(1)
        cb((x + 1) % 4, 1).start()

    @pl.when(zl == 0)
    def _():
        wring.forward(0)

    @pl.when(zl == 1)
    def _():
        wring.forward(1)

    kring.wait_near()
    nh = ROWS // SEG

    def spot(rb):
        s, hb = rb // 2, rb % 2
        return s, hb, slice(s * SEG, (s + 1) * SEG), slice(rb * ROWS, (rb + 1) * ROWS), [
            slice((hb * nh + i) * HD, (hb * nh + i + 1) * HD) for i in range(nh)]

    def crow(j):
        return pl.ds(pl.multiple_of(j * CH, CH), CH)

    def lane_max(sc, mx):
        for t in range(sc.shape[1] // HD):
            part = sc[:, t * HD:(t + 1) * HD]
            mx = part if mx is None else jnp.maximum(mx, part)
        return mx

    def lane_sum(p, tot):
        for t in range(p.shape[1] // HD):
            part = p[:, t * HD:(t + 1) * HD]
            tot = part if tot is None else tot + part
        return tot

    def forward_near(rb):
        s, hb, tok, rows, heads = spot(rb)
        qb = jnp.concatenate([q[tok, h] for h in heads], axis=0)
        qt[rb] = qb.T
        mx = None
        for i, d in enumerate((0, 1, 3)):
            sc = nt_dot(qb, kvg[0, crow((y + d) % 4), :])
            s_f[:, i * CH:(i + 1) * CH] = sc
            mx = lane_max(sc, mx)
        m = jnp.max(mx, axis=1, keepdims=True)
        lsum = None
        o = None
        for i, d in enumerate((0, 1, 3)):
            j = (y + d) % 4
            p = jnp.exp2((s_f[:, i * CH:(i + 1) * CH] - m) * cexp)
            lsum = lane_sum(p, lsum)
            pb = p.astype(BF)
            p_b[j, rows, :] = pb
            oc = jnp.dot(pb, kvg[1, crow(j), :], preferred_element_type=F32)
            o = oc if o is None else o + oc
        delta[0, rows, :] = lsum
        delta[1, rows, :] = jnp.broadcast_to(m, (ROWS, HD))
        dqa[rows, :] = o

    for rb in range(4):
        forward_near(rb)

    @pl.when(zl == 0)
    def _():
        wring.forward(1)

    @pl.when(zl == 1)
    def _():
        wring.forward(0)

    kring.wait_far()

    lane = lax.broadcasted_iota(jnp.int32, (1, 16), 1)
    named = [[jnp.broadcast_to(jnp.sum(jnp.where(lane == first + s, anc[i:i + 1, :].astype(F32), 0.0),
                                       axis=1, keepdims=True), (1, HD)) for i in range(2)] for s in range(2)]

    def hot(s, i, j):
        return (named[s][i] == float(j)).astype(F32)

    for s in range(2):
        own_seg = pl.ds(pl.multiple_of((first + s) * SEG, SEG), SEG)
        for k, dst in enumerate((kcs, vcs)):
            for i in range(2):
                tot = None
                for j in range(16):
                    v = kvg[2 + k, j * SEG:(j + 1) * SEG, :] * hot(s, i, j).astype(BF)
                    tot = v if tot is None else tot + v
                dst[s, i * SEG:(i + 1) * SEG, :] = tot
            dst[s, 2 * SEG:, :] = kvg[2 + k, own_seg, :]

    def forward_far(rb):
        s, hb, tok, rows, heads = spot(rb)
        col = lax.broadcasted_iota(jnp.int32, (ROWS, SEG), 1)
        row = lax.broadcasted_iota(jnp.int32, (ROWS, SEG), 0) % SEG
        shut = [jnp.where(named[s][i] >= 0, 0.0, -1e30) for i in range(2)]
        shut.append(jnp.where(col <= row, 0.0, -1e30))
        qb = jnp.concatenate([q[tok, h] for h in heads], axis=0)
        far = (y + 2) % 4
        sc = nt_dot(qb, kvg[0, crow(far), :])
        s_f[:, 0:CH] = sc
        mx = lane_max(sc, None)
        sc = nt_dot(qb, kcs[s])
        sc = jnp.concatenate([sc[:, i * SEG:(i + 1) * SEG] + shut[i] for i in range(3)], axis=1)
        s_f[:, CH:CH + SEGCTX] = sc
        mx = lane_max(sc, mx)
        m_near = delta[1, rows, 0:1]
        m = jnp.maximum(jnp.max(mx, axis=1, keepdims=True), m_near)
        p = jnp.exp2((s_f[:, 0:CH] - m) * cexp)
        lsum = lane_sum(p, None)
        pb = p.astype(BF)
        p_b[far, rows, :] = pb
        o = jnp.dot(pb, kvg[1, crow(far), :], preferred_element_type=F32)
        p = jnp.exp2((s_f[:, CH:CH + SEGCTX] - m) * cexp)
        lsum = lane_sum(p, lsum)
        pb = p.astype(BF)
        p_s[rows, :] = pb
        o = o + jnp.dot(pb, vcs[s], preferred_element_type=F32)
        ratio = jnp.broadcast_to(jnp.exp2((m_near - m) * cexp), (ROWS, HD))
        lsum = lsum + delta[0, rows, :] * ratio
        o = o + dqa[rows, :] * ratio
        il = jnp.broadcast_to(1.0 / jnp.sum(lsum, axis=1, keepdims=True), (ROWS, HD))
        il_b[rows, :] = il
        delta[1, rows, :] = ratio
        ob = (o * il).astype(BF)
        for i, h in enumerate(heads):
            attng[pl.ds(pl.multiple_of(y * TOKL + s * SEG, SEG), SEG), h] = ob[i * SEG:(i + 1) * SEG]

    forward_far(0)
    forward_far(1)
    aring.send(0)
    forward_far(2)
    forward_far(3)
    aring.send(1)

    @pl.when(is_recv)
    def _():
        xring.wait_near()
        cb((x + 3) % 4, 1).start()
        cb((x + 1) % 4, 0).start()
        xring.wait_far()
        for p in range(2):
            cb((x + 2) % 4, p).start()

    aring.forward(0)

    wring.wait_near()
    wring.wait_far()

    @pl.when(jnp.logical_not(is_recv))
    def _():
        for n in range(4):
            for p in range(2):
                cb(n, p).wait_recv()

    def proj(yy, rows):
        return jnp.dot(cotb[0, yy, rows, :], wg[0:UCOL, :], preferred_element_type=F32) + jnp.dot(
            cotb[1, yy, rows, :], wg[UCOL:2 * UCOL, :], preferred_element_type=F32)

    lo, hi = slice(0, SEG), slice(SEG, 2 * SEG)
    dring.send(0, proj((y + 2) % 4, lo))
    dring.send(1, proj((y + 2) % 4, hi))
    dring.send(2, proj((y + 1) % 4, hi))
    dring.send(3, proj((y + 3) % 4, lo))
    dnear[0] = proj((y + 1) % 4, lo)
    dnear[1] = proj((y + 3) % 4, hi)
    dnear[2] = proj(y, lo)
    dnear[3] = proj(y, hi)

    aring.forward(1)
    for h in range(2):
        for yy in range(4):
            cott[h * UCOL:(h + 1) * UCOL, yy * TOKL:(yy + 1) * TOKL] = cotb[h, yy].T
    for d in (0, 1, 3):
        for rb in range(4):
            j, rows = (y + d) % 4, slice(rb * ROWS, (rb + 1) * ROWS)
            ratio = jnp.concatenate([delta[1, rows, :]] * (CH // HD), axis=1)
            p_b[j, rows, :] = (p_b[j, rows, :].astype(F32) * ratio).astype(BF)
    dring.add_send(4, dnear[0])
    dring.add_send(5, dnear[1])

    aring.wait_near()
    aring.wait_far()

    def wgrad(zz, p):
        rows = pl.ds(pl.multiple_of(zz * WROWS + p * w_half, 32), w_half)
        return jnp.dot(cott[rows, :], attng[...], preferred_element_type=F32)

    gring.send(0, wgrad((z + 2) % 4, 0))
    gring.send(1, wgrad((z + 2) % 4, 1))
    gring.send(2, wgrad((z + 1) % 4, 1))
    gring.send(3, wgrad((z + 3) % 4, 0))
    gnear[0] = wgrad((z + 1) % 4, 0)
    gnear[1] = wgrad((z + 3) % 4, 1)

    dring.wait_result()
    for p in range(2):
        dattn[p * SEG:(p + 1) * SEG, :] = dring.result(p, dnear[2 + p]).astype(BF)
    for rb in range(4):
        s, hb, tok, rows, heads = spot(rb)
        arow = pl.ds(pl.multiple_of(y * TOKL + s * SEG, SEG), SEG)
        dob = jnp.concatenate([dattn[tok, h] for h in heads], axis=0)
        at = jnp.concatenate([attng[arow, h] for h in heads], axis=0)
        db = (dob.astype(F32) * il_b[rows, :]).astype(BF)
        dos[rows, :] = db
        dost[rb] = db.T
        dl = jnp.sum(db.astype(F32) * at.astype(F32), axis=1, keepdims=True)
        delta[0, rows, :] = jnp.broadcast_to(dl, (ROWS, HD))

    def back(rb, kc, vc, pb):
        rows = pl.ds(pl.multiple_of(rb * ROWS, ROWS), ROWS)
        dl = delta[0, rows, :]
        n = vc.shape[0]
        dp = nt_dot(dos[rows, :], vc)
        ds = (pb.astype(F32) * (dp - jnp.concatenate([dl] * (n // HD), axis=1))).astype(BF)
        return (rows, jnp.dot(ds, kc, preferred_element_type=F32),
                jnp.dot(qt[rb], ds, preferred_element_type=F32),
                jnp.dot(dost[rb], pb, preferred_element_type=F32))

    def prefix(j):
        acc[...] = jnp.zeros_like(acc)

        @pl.loop(0, 4)
        def _(rb):
            rows = pl.ds(pl.multiple_of(rb * ROWS, ROWS), ROWS)
            _, dqc, dk, dv = back(rb, kvg[0, crow(j), :], kvg[1, crow(j), :], p_b[j, rows, :])
            dqa[rows, :] += dqc
            acc[0] += dk
            acc[1] += dv

    for rb in range(4):
        s = rb // 2
        rows, dqc, dk, dv = back(rb, kcs[s], vcs[s], p_s[rb * ROWS:(rb + 1) * ROWS, :])
        dqa[rows, :] = dqc
        if rb % 2 == 0:
            accs[s, 0] = dk
            accs[s, 1] = dv
        else:
            accs[s, 0] += dk
            accs[s, 1] += dv
    for j in range(16):
        for k in range(2):
            tot = None
            for s in range(2):
                for i in range(2):
                    v = accs[s, k, :, i * SEG:(i + 1) * SEG] * hot(s, i, j)
                    tot = v if tot is None else tot + v
            segt[j // 4, k, :, (j % 4) * SEG:(j % 4 + 1) * SEG] = tot
    for s in range(2):
        own_cols = pl.ds(pl.multiple_of((zl * 2 + s) * SEG, SEG), SEG)
        for k in range(2):
            segt[y, k, :, own_cols] += accs[s, k, :, 2 * SEG:]
    rring.send(0, segt[(y + 2) % 4])
    rring.send(3, segt[(y + 3) % 4])
    gring.add_send(4, gnear[0])
    gring.add_send(5, gnear[1])

    prefix((y + 2) % 4)
    rring.send(1, acc[...])
    prefix((y + 1) % 4)
    rring.send(2, acc[...])
    rring.add_send(4, segt[(y + 1) % 4])
    prefix((y + 3) % 4)
    rring.add_send(5, acc[...])
    prefix(y)
    for rb in range(4):
        s, hb = rb // 2, rb % 2
        dqb = (dqa[rb * ROWS:(rb + 1) * ROWS, :] * SCALE).astype(BF)
        for i in range(nh):
            odq[s * SEG:(s + 1) * SEG, (hb * nh + i) * HD:(hb * nh + i + 1) * HD] = dqb[i * SEG:(i + 1) * SEG]

    for p in range(2):
        owg[p * w_half:(p + 1) * w_half, :] = wgrad(z, p)

    lanes = lambda v: pl.ds(pl.multiple_of(v * 256, 256), 256)

    def zk(p):
        return rcopy(zsb.at[p], zrb.at[p], zk_s.at[p], zk_r.at[p], place(x, y, z + 1 - 2 * zl, c))

    for p in range(2):
        for i in ((4, 3), (2, 5))[p]:
            rring.copy(i).wait_recv()
        kown[p] = rring.result(p, segt[y] if p == 0 else acc[...])
        zsb[p] = kown[p, :, :, lanes(1 - zl)].astype(BF)
        zk(p).start()

    gring.wait_result()
    for p in range(2):
        rows = slice(p * w_half, (p + 1) * w_half)
        owg[rows, :] = gring.result(p, owg[rows, :])

    for p in range(2):
        zk(p).wait_recv()
        for i in range(2):
            t = kown[p, i, :, lanes(zl)] + zrb[p, i].astype(F32)
            if i == 0:
                t = t * SCALE
            okv[2 * (1 - p) + i] = t.T.astype(BF)

    kz().wait_send()
    for p in range(2):
        zk(p).wait_send()

    cy(1).wait_send()

    @pl.when(jnp.logical_not(is_src))
    def _():
        cy(0).wait_send()

    @pl.when(is_recv)
    def _():
        xring.wait_sends()
        for n in range(4):
            for p in range(2):
                cb(n, p).wait_send()

    for ring in (wring, kring, aring, dring, rring, gring):
        ring.wait_sends()


def finish_kernel(dq, kv, wgr, o0, o1, o2, o3, o4, o5):
    o0[...] = dq[...]
    for i, o in enumerate((o1, o2, o3, o4)):
        o[...] = kv[i]
    o5[...] = wgr[...]


def on_device(
    queries, prefix_keys, prefix_values, keys, values, ancestors, advantages, upstream, out_weight
):
    dma = pltpu.SemaphoreType.DMA
    sds = jax.ShapeDtypeStruct
    vm = pltpu.VMEM
    half_w = WROWS // 2
    dq, okv, owg = pl.pallas_call(
        whole_kernel,
        out_shape=(
            sds((TOKL, NCOL), BF),
            sds((4, 256, HD), BF),
            sds((WROWS, NCOL), F32),
        ),
        in_specs=[VM] * 9,
        out_specs=(VM, VM, VM),
        scratch_shapes=[
            vm((TOKL, UCOL), BF),
            vm((2, 4, TOKL, UCOL), BF),
            vm((2 * UCOL, 4 * TOKL), BF),
            vm((4 * WROWS, NCOL), BF),
            vm((4, CTX, HD), BF),
            vm((2, SEGCTX, HD), BF),
            vm((2, SEGCTX, HD), BF),
            vm((6, SEG, NCOL), BF),
            vm((6, SEG, NCOL), BF),
            vm((4, SEG, NCOL), F32),
            vm((TOKL, NCOL), BF),
            vm((ROWS, 3 * CH), F32),
            vm((4, 4 * ROWS, CH), BF),
            vm((4 * ROWS, SEGCTX), BF),
            vm((4 * TOKL, NCOL), BF),
            vm((4 * ROWS, HD), F32),
            vm((2, 4 * ROWS, HD), F32),
            vm((4, HD, ROWS), BF),
            vm((4 * ROWS, HD), BF),
            vm((4, HD, ROWS), BF),
            vm((4 * ROWS, HD), F32),
            vm((2, HD, CH), F32),
            vm((2, 2, HD, SEGCTX), F32),
            vm((4, 2, HD, CH), F32),
            vm((6, 2, HD, CH), BF),
            vm((6, 2, HD, CH), BF),
            vm((2, 2, HD, 256), BF),
            vm((2, 2, HD, 256), BF),
            vm((2, 2, HD, CH), F32),
            vm((6, half_w, NCOL), BF),
            vm((6, half_w, NCOL), BF),
            vm((2, half_w, NCOL), F32),
            dma((2,)), dma((4,)), dma((6,)), dma((6,)), dma((4, 2)), dma((4, 2)),
            dma((6,)), dma((6,)), dma, dma, dma((6,)), dma((6,)),
            dma((6,)), dma((6,)), dma((6,)), dma((6,)), dma((6,)), dma((6,)),
            dma((2,)), dma((2,)), dma((6,)), dma((6,)),
        ],
        compiler_params=pltpu.CompilerParams(
            collective_id=0, has_side_effects=True, vmem_limit_bytes=VLIM),
        name="whole",
    )(ancestors[0].T, upstream[0], advantages, out_weight, prefix_keys[0], prefix_values[0], keys[0], values[0],
      queries[0])
    outs = pl.pallas_call(
        finish_kernel,
        out_shape=tuple([sds((TOKL, NCOL), BF)] + [sds((256, HD), BF)] * 4 + [sds((WROWS, NCOL), F32)]),
        in_specs=[VM] * 3,
        out_specs=tuple([VM] * 6),
        name="finish",
    )(dq, okv, owg)
    return tuple(o[None] for o in outs[:5]) + (outs[5],)


def solution(mesh):
    return jax.shard_map(
        on_device,
        mesh=mesh,
        in_specs=(
            P("dp", "branch", "tensor"),
            P("dp", "branch", "tensor"),
            P("dp", "branch", "tensor"),
            P("dp", "branch", "tensor"),
            P("dp", "branch", "tensor"),
            P("dp", None, None),
            P("dp", "branch"),
            P("dp", "branch", "tensor"),
            P(("dp", "branch"), "tensor"),
        ),
        out_specs=(
            P("dp", "branch", "tensor"),
            P("dp", "branch", "tensor"),
            P("dp", "branch", "tensor"),
            P("dp", "branch", "tensor"),
            P("dp", "branch", "tensor"),
            P(("dp", "branch"), "tensor"),
        ),
        check_vma=False,
    )
```

```python
import math

import jax
import jax.numpy as jnp
from jax import lax
from jax.experimental import pallas as pl
from jax.experimental.pallas import tpu as pltpu
from jax.sharding import PartitionSpec as P

HD = 128
SEG = 128
GROUP = 8
TOKL = 256
KVB = 8
WROWS = 320
NCOL = 1024
UCOL = 640
CTX = 2048
SEGCTX = 384
ALLCTX = CTX + SEGCTX
CH = 512
ROWS = 512
SCALE = 1.0 / math.sqrt(HD)
LOG2E = 1.4426950408889634
BF = jnp.bfloat16
F32 = jnp.float32
VM = pl.BlockSpec(memory_space=pltpu.VMEM)
VLIM = 60 * 2**20


def coords():
    b = lax.axis_index("branch")
    t = lax.axis_index("tensor")
    return t // 2, b // 2, lax.axis_index("dp") * 2 + b % 2, t % 2


def place(x, y, z, c):
    return {"dp": z // 2, "branch": y * 2 + z % 2, "tensor": x * 2 + c}


def rcopy(src, dst, ss, rs, dev):
    return pltpu.make_async_remote_copy(
        src_ref=src, dst_ref=dst, send_sem=ss, recv_sem=rs,
        device_id=dev, device_id_type=pl.DeviceIdType.MESH,
    )


def signal(sem, dev):
    pl.semaphore_signal(sem, inc=1, device_id=dev, device_id_type=pl.DeviceIdType.MESH)


def nt_dot(a, b):
    return lax.dot_general(a, b, (((1,), (1,)), ((), ())), preferred_element_type=F32)


class GatherRing:
    def __init__(self, me, dev, view, ss, rs):
        self.me, self.dev, self.view, self.ss, self.rs = me, dev, view, ss, rs

    def copy(self, node, piece, kind, step):
        v = self.view(node, piece)
        i = kind * 2 + piece
        return rcopy(v, v, self.ss.at[i], self.rs.at[i], self.dev(step))

    def right(self, p):
        return self.copy(self.me, p, 0, 1)

    def left(self, p):
        return self.copy(self.me, p, 1, 3)

    def fwd(self, p):
        if p == 0:
            return self.copy((self.me + 3) % 4, 0, 2, 1)
        return self.copy((self.me + 1) % 4, 1, 2, 3)

    def send(self, p):
        self.right(p).start()
        self.left(p).start()

    def forward(self, p):
        (self.right if p == 0 else self.left)(p).wait_recv()
        self.fwd(p).start()

    def wait_near(self):
        self.right(1).wait_recv()
        self.left(0).wait_recv()

    def wait_far(self):
        self.fwd(0).wait_recv()
        self.fwd(1).wait_recv()

    def wait_sends(self):
        for p in range(2):
            self.right(p).wait_send()
            self.left(p).wait_send()
            self.fwd(p).wait_send()


class SumRing:
    def __init__(self, dev, sb, rb, ss, rs):
        self.dev, self.sb, self.rb, self.ss, self.rs = dev, sb, rb, ss, rs

    def copy(self, i):
        return rcopy(self.sb.at[i], self.rb.at[i], self.ss.at[i], self.rs.at[i], self.dev(1 if i % 2 == 0 else 3))

    def send(self, i, value):
        self.sb[i] = value.astype(BF)
        self.copy(i).start()

    def add_send(self, i, value):
        self.copy(i - 4).wait_recv()
        self.send(i, value + self.rb[i - 4].astype(F32))

    def wait_result(self):
        for i in range(2, 6):
            self.copy(i).wait_recv()

    def result(self, p, own):
        a, b = ((4, 3), (2, 5))[p]
        return own + self.rb[a].astype(F32) + self.rb[b].astype(F32)

    def wait_sends(self):
        for i in range(6):
            self.copy(i).wait_send()


def whole_kernel(
    anc, up, adv, w, pk, pv, sk, sv, q,
    odq, okv, owg,
    cot, cotb, cott, wg, kvg, kcs, vcs,
    dsb, drb, dnear, dattn,
    s_f, p_b, p_s, attng, il_b, delta, qt, dos, dost, dqa,
    acc, accs, segt, ksb, krb, zsb, zrb, kown,
    gsb, grb, gnear,
    c_s, c_r, x_s, x_r, b_s, b_r, w_s, w_r, kz_s, kz_r, k_s, k_r,
    d_s, d_r, a_s, a_r, r_s, r_r, zk_s, zk_r, g_s, g_r,
):
    x, y, z, c = coords()
    zl = z % 2
    first = lax.axis_index("branch") * 2
    target_y = 2 * (x % 2) + c
    is_recv = c == y % 2
    is_src = target_y == y
    is_mid = is_recv & jnp.logical_not(is_src)
    sib = place(x, y, z, 1 - c)
    cexp = SCALE * LOG2E

    def ydev(d):
        return place(x, (y + d) % 4, z, c)

    def zdev(d):
        return place(x, y, (z + d) % 4, c)

    def xdev(d):
        return place((x + d) % 4, y, z, c)

    bar = pltpu.get_barrier_semaphore()
    for d in range(1, 4):
        signal(bar, ydev(d))
    signal(bar, zdev(1))
    signal(bar, zdev(3))
    signal(bar, sib)

    @pl.when(is_recv)
    def _():
        signal(bar, xdev(1))
        signal(bar, xdev(3))

    @pl.when(is_mid)
    def _():
        for d in range(1, 4):
            signal(bar, place((x + 3) % 4, (y + d) % 4, z, c))

    rows_b = lambda b: pl.ds(pl.multiple_of(b * 256, 256), 256)
    own_rows = rows_b(y * 2 + zl)
    for i, r in enumerate((pk, pv, sk, sv)):
        kvg[i, own_rows, :] = r[...]
    wrow = jnp.broadcast_to(adv[...].astype(F32) * 0.25, (TOKL, TOKL))
    ri = lax.broadcasted_iota(jnp.int32, (TOKL, TOKL), 0)
    ci = lax.broadcasted_iota(jnp.int32, (TOKL, TOKL), 1)
    diag = jnp.where(ri == ci, wrow, 0.0).astype(BF)
    cot[...] = jnp.dot(diag, up[...], preferred_element_type=F32).astype(BF)
    w_half = WROWS // 2
    wview = lambda n, p: wg.at[pl.ds(pl.multiple_of(n * WROWS + p * w_half, 32), w_half)]
    wg[pl.ds(pl.multiple_of(z * WROWS, 64), WROWS), :] = w[...]

    pl.semaphore_wait(bar, 6 + 2 * is_recv.astype(jnp.int32) + 1 - is_src.astype(jnp.int32))

    wring = GatherRing(z, zdev, wview, w_s, w_r)
    kring = GatherRing(y, ydev, lambda n, p: kvg.at[:, rows_b(n * 2 + p)], k_s, k_r)
    aring = GatherRing(
        y, ydev, lambda n, p: attng.at[pl.ds(pl.multiple_of(n * TOKL + p * SEG, SEG), SEG)], a_s, a_r)
    dring = SumRing(ydev, dsb, drb, d_s, d_r)
    pring = SumRing(ydev, ksb.at[0], krb.at[0], r_s.at[0], r_r.at[0])
    sring = SumRing(ydev, ksb.at[1], krb.at[1], r_s.at[1], r_r.at[1])
    gring = SumRing(zdev, gsb, grb, g_s, g_r)

    def kz():
        v = kvg.at[:, own_rows]
        return rcopy(v, v, kz_s, kz_r, place(x, y, z + 1 - 2 * zl, c))

    def quarter(n, yy):
        second = (n + y // 2) % 2
        return cotb.at[((n + 4 - second) % 4) // 2, yy, pl.ds(pl.multiple_of(second * SEG, SEG), SEG)]

    def quarter_piece(n, p):
        second = (n + y // 2) % 2
        return cotb.at[((n + 4 - second) % 4) // 2, 2 * p:2 * p + 2, pl.ds(pl.multiple_of(second * SEG, SEG), SEG)]

    xring = GatherRing(x, xdev, quarter_piece, x_s, x_r)

    def cy(second):
        dst = cotb.at[x // 2, y, second * SEG:(second + 1) * SEG]
        return rcopy(cot.at[second * SEG:(second + 1) * SEG], dst, c_s.at[second], c_r.at[y],
                     place((x + second) % 4, target_y, z, c))

    def cy_arrived(yy):
        rcopy(cot.at[0:SEG], quarter(x, yy), c_s.at[0], c_r.at[yy], sib).wait_recv()

    def cb(n, p):
        v = quarter_piece(n, p)
        return rcopy(v, v, b_s.at[n, p], b_r.at[n, p], sib)

    kz().start()
    cy(1).start()

    @pl.when(jnp.logical_not(is_src))
    def _():
        cy(0).start()

    kring.send(zl)

    @pl.when(zl == 0)
    def _():
        for p in range(2):
            wring.left(p).start()

    @pl.when(zl == 1)
    def _():
        for p in range(2):
            wring.right(p).start()

    @pl.when(is_src)
    def _():
        cotb[x // 2, y, 0:SEG] = cot[0:SEG]

    kz().wait_recv()
    kring.send(1 - zl)

    @pl.when(zl == 0)
    def _():
        for p in range(2):
            wring.right(p).start()

    @pl.when(zl == 1)
    def _():
        for p in range(2):
            wring.left(p).start()

    @pl.when(is_recv)
    def _():
        for p in range(2):
            for yy in (2 * p, 2 * p + 1):
                @pl.when(jnp.logical_not(is_src & (yy == y)))
                def _():
                    cy_arrived(yy)
            xring.send(p)
            cb(x, p).start()

    for p in range(2):
        kring.forward(p)

    @pl.when(is_recv)
    def _():
        xring.forward(0)
        cb((x + 3) % 4, 0).start()
        xring.forward(1)
        cb((x + 1) % 4, 1).start()

    @pl.when(zl == 0)
    def _():
        wring.forward(0)

    @pl.when(zl == 1)
    def _():
        wring.forward(1)

    kring.wait_near()
    nh = ROWS // SEG

    def spot(rb):
        s, hb = rb // 2, rb % 2
        return s, hb, slice(s * SEG, (s + 1) * SEG), slice(rb * ROWS, (rb + 1) * ROWS), [
            slice((hb * nh + i) * HD, (hb * nh + i + 1) * HD) for i in range(nh)]

    def crow(j):
        return pl.ds(pl.multiple_of(j * CH, CH), CH)

    def lane_max(sc, mx):
        for t in range(sc.shape[1] // HD):
            part = sc[:, t * HD:(t + 1) * HD]
            mx = part if mx is None else jnp.maximum(mx, part)
        return mx

    def lane_sum(p, tot):
        for t in range(p.shape[1] // HD):
            part = p[:, t * HD:(t + 1) * HD]
            tot = part if tot is None else tot + part
        return tot

    def forward_near(rb):
        s, hb, tok, rows, heads = spot(rb)
        qb = jnp.concatenate([q[tok, h] for h in heads], axis=0)
        qt[rb] = qb.T
        mx = None
        for i, d in enumerate((0, 1, 3)):
            sc = nt_dot(qb, kvg[0, crow((y + d) % 4), :])
            s_f[:, i * CH:(i + 1) * CH] = sc
            mx = lane_max(sc, mx)
        m = jnp.max(mx, axis=1, keepdims=True)
        lsum = None
        o = None
        for i, d in enumerate((0, 1, 3)):
            j = (y + d) % 4
            p = jnp.exp2((s_f[:, i * CH:(i + 1) * CH] - m) * cexp)
            lsum = lane_sum(p, lsum)
            pb = p.astype(BF)
            p_b[j, rows, :] = pb
            oc = jnp.dot(pb, kvg[1, crow(j), :], preferred_element_type=F32)
            o = oc if o is None else o + oc
        delta[0, rows, :] = lsum
        delta[1, rows, :] = jnp.broadcast_to(m, (ROWS, HD))
        dqa[rows, :] = o

    for rb in range(4):
        forward_near(rb)

    @pl.when(zl == 0)
    def _():
        wring.forward(1)

    @pl.when(zl == 1)
    def _():
        wring.forward(0)

    kring.wait_far()

    lane = lax.broadcasted_iota(jnp.int32, (1, 16), 1)
    named = [[jnp.broadcast_to(jnp.sum(jnp.where(lane == first + s, anc[i:i + 1, :].astype(F32), 0.0),
                                       axis=1, keepdims=True), (1, HD)) for i in range(2)] for s in range(2)]

    def hot(s, i, j):
        return (named[s][i] == float(j)).astype(F32)

    for s in range(2):
        own_seg = pl.ds(pl.multiple_of((first + s) * SEG, SEG), SEG)
        for k, dst in enumerate((kcs, vcs)):
            for i in range(2):
                tot = None
                for j in range(16):
                    v = kvg[2 + k, j * SEG:(j + 1) * SEG, :] * hot(s, i, j).astype(BF)
                    tot = v if tot is None else tot + v
                dst[s, i * SEG:(i + 1) * SEG, :] = tot
            dst[s, 2 * SEG:, :] = kvg[2 + k, own_seg, :]

    def forward_far(rb):
        s, hb, tok, rows, heads = spot(rb)
        col = lax.broadcasted_iota(jnp.int32, (ROWS, SEG), 1)
        row = lax.broadcasted_iota(jnp.int32, (ROWS, SEG), 0) % SEG
        shut = [jnp.where(named[s][i] >= 0, 0.0, -1e30) for i in range(2)]
        shut.append(jnp.where(col <= row, 0.0, -1e30))
        qb = jnp.concatenate([q[tok, h] for h in heads], axis=0)
        far = (y + 2) % 4
        sc = nt_dot(qb, kvg[0, crow(far), :])
        s_f[:, 0:CH] = sc
        mx = lane_max(sc, None)
        sc = nt_dot(qb, kcs[s])
        sc = jnp.concatenate([sc[:, i * SEG:(i + 1) * SEG] + shut[i] for i in range(3)], axis=1)
        s_f[:, CH:CH + SEGCTX] = sc
        mx = lane_max(sc, mx)
        m_near = delta[1, rows, 0:1]
        m = jnp.maximum(jnp.max(mx, axis=1, keepdims=True), m_near)
        p = jnp.exp2((s_f[:, 0:CH] - m) * cexp)
        lsum = lane_sum(p, None)
        pb = p.astype(BF)
        p_b[far, rows, :] = pb
        o = jnp.dot(pb, kvg[1, crow(far), :], preferred_element_type=F32)
        p = jnp.exp2((s_f[:, CH:CH + SEGCTX] - m) * cexp)
        lsum = lane_sum(p, lsum)
        pb = p.astype(BF)
        p_s[rows, :] = pb
        o = o + jnp.dot(pb, vcs[s], preferred_element_type=F32)
        ratio = jnp.broadcast_to(jnp.exp2((m_near - m) * cexp), (ROWS, HD))
        lsum = lsum + delta[0, rows, :] * ratio
        o = o + dqa[rows, :] * ratio
        il = jnp.broadcast_to(1.0 / jnp.sum(lsum, axis=1, keepdims=True), (ROWS, HD))
        il_b[rows, :] = il
        delta[1, rows, :] = ratio
        ob = (o * il).astype(BF)
        for i, h in enumerate(heads):
            attng[pl.ds(pl.multiple_of(y * TOKL + s * SEG, SEG), SEG), h] = ob[i * SEG:(i + 1) * SEG]

    forward_far(0)
    forward_far(1)
    aring.send(0)
    forward_far(2)
    forward_far(3)
    aring.send(1)

    @pl.when(is_recv)
    def _():
        xring.wait_near()
        cb((x + 3) % 4, 1).start()
        cb((x + 1) % 4, 0).start()
        xring.wait_far()
        for p in range(2):
            cb((x + 2) % 4, p).start()

    aring.forward(0)

    wring.wait_near()
    wring.wait_far()

    @pl.when(jnp.logical_not(is_recv))
    def _():
        for n in range(4):
            for p in range(2):
                cb(n, p).wait_recv()

    def proj(yy, rows):
        return jnp.dot(cotb[0, yy, rows, :], wg[0:UCOL, :], preferred_element_type=F32) + jnp.dot(
            cotb[1, yy, rows, :], wg[UCOL:2 * UCOL, :], preferred_element_type=F32)

    lo, hi = slice(0, SEG), slice(SEG, 2 * SEG)
    dring.send(0, proj((y + 2) % 4, lo))
    dring.send(1, proj((y + 2) % 4, hi))
    dring.send(2, proj((y + 1) % 4, hi))
    dring.send(3, proj((y + 3) % 4, lo))
    dnear[0] = proj((y + 1) % 4, lo)
    dnear[1] = proj((y + 3) % 4, hi)
    dnear[2] = proj(y, lo)
    dnear[3] = proj(y, hi)

    aring.forward(1)
    for h in range(2):
        for yy in range(4):
            cott[h * UCOL:(h + 1) * UCOL, yy * TOKL:(yy + 1) * TOKL] = cotb[h, yy].T
    for d in (0, 1, 3):
        for rb in range(4):
            j, rows = (y + d) % 4, slice(rb * ROWS, (rb + 1) * ROWS)
            ratio = jnp.concatenate([delta[1, rows, :]] * (CH // HD), axis=1)
            p_b[j, rows, :] = (p_b[j, rows, :].astype(F32) * ratio).astype(BF)
    dring.add_send(4, dnear[0])
    dring.add_send(5, dnear[1])

    aring.wait_near()
    aring.wait_far()

    def wgrad(zz, p):
        rows = pl.ds(pl.multiple_of(zz * WROWS + p * w_half, 32), w_half)
        return jnp.dot(cott[rows, :], attng[...], preferred_element_type=F32)

    gring.send(0, wgrad((z + 2) % 4, 0))
    gring.send(1, wgrad((z + 2) % 4, 1))
    gring.send(2, wgrad((z + 1) % 4, 1))
    gring.send(3, wgrad((z + 3) % 4, 0))
    gnear[0] = wgrad((z + 1) % 4, 0)
    gnear[1] = wgrad((z + 3) % 4, 1)

    dqa[...] = jnp.zeros_like(dqa)
    dring.wait_result()
    for p in range(2):
        dattn[p * SEG:(p + 1) * SEG, :] = dring.result(p, dnear[2 + p]).astype(BF)
    for rb in range(4):
        s, hb, tok, rows, heads = spot(rb)
        arow = pl.ds(pl.multiple_of(y * TOKL + s * SEG, SEG), SEG)
        dob = jnp.concatenate([dattn[tok, h] for h in heads], axis=0)
        at = jnp.concatenate([attng[arow, h] for h in heads], axis=0)
        db = (dob.astype(F32) * il_b[rows, :]).astype(BF)
        dos[rows, :] = db
        dost[rb] = db.T
        dl = jnp.sum(db.astype(F32) * at.astype(F32), axis=1, keepdims=True)
        delta[0, rows, :] = jnp.broadcast_to(dl, (ROWS, HD))

    def back(rb, kc, vc, pb):
        rows = pl.ds(pl.multiple_of(rb * ROWS, ROWS), ROWS)
        dl = delta[0, rows, :]
        n = vc.shape[0]
        dp = nt_dot(dos[rows, :], vc)
        ds = (pb.astype(F32) * (dp - jnp.concatenate([dl] * (n // HD), axis=1))).astype(BF)
        return (rows, jnp.dot(ds, kc, preferred_element_type=F32),
                jnp.dot(qt[rb], ds, preferred_element_type=F32),
                jnp.dot(dost[rb], pb, preferred_element_type=F32))

    def prefix(j):
        acc[...] = jnp.zeros_like(acc)

        @pl.loop(0, 4)
        def _(rb):
            rows = pl.ds(pl.multiple_of(rb * ROWS, ROWS), ROWS)
            _, dqc, dk, dv = back(rb, kvg[0, crow(j), :], kvg[1, crow(j), :], p_b[j, rows, :])
            dqa[rows, :] += dqc
            acc[0] += dk
            acc[1] += dv

    prefix((y + 2) % 4)
    for k in range(2):
        pring.send(k, acc[k])

    for rb in range(4):
        s = rb // 2
        rows, dqc, dk, dv = back(rb, kcs[s], vcs[s], p_s[rb * ROWS:(rb + 1) * ROWS, :])
        dqa[rows, :] += dqc
        if rb % 2 == 0:
            accs[s, 0] = dk
            accs[s, 1] = dv
        else:
            accs[s, 0] += dk
            accs[s, 1] += dv
    for j in range(16):
        for k in range(2):
            tot = None
            for s in range(2):
                for i in range(2):
                    v = accs[s, k, :, i * SEG:(i + 1) * SEG] * hot(s, i, j)
                    tot = v if tot is None else tot + v
            segt[j // 4, k, :, (j % 4) * SEG:(j % 4 + 1) * SEG] = tot
    for s in range(2):
        own_cols = pl.ds(pl.multiple_of((zl * 2 + s) * SEG, SEG), SEG)
        for k in range(2):
            segt[y, k, :, own_cols] += accs[s, k, :, 2 * SEG:]
    for k in range(2):
        sring.send(k, segt[(y + 2) % 4, k])
    sring.send(2, segt[(y + 1) % 4, 1])
    sring.send(3, segt[(y + 3) % 4, 0])
    gring.add_send(4, gnear[0])
    gring.add_send(5, gnear[1])

    prefix((y + 1) % 4)
    pring.send(2, acc[1])
    pring.add_send(4, acc[0])
    sring.add_send(4, segt[(y + 1) % 4, 0])
    sring.add_send(5, segt[(y + 3) % 4, 1])
    prefix((y + 3) % 4)
    pring.send(3, acc[0])
    pring.add_send(5, acc[1])
    prefix(y)
    for rb in range(4):
        s, hb = rb // 2, rb % 2
        dqb = (dqa[rb * ROWS:(rb + 1) * ROWS, :] * SCALE).astype(BF)
        for i in range(nh):
            odq[s * SEG:(s + 1) * SEG, (hb * nh + i) * HD:(hb * nh + i + 1) * HD] = dqb[i * SEG:(i + 1) * SEG]

    for p in range(2):
        owg[p * w_half:(p + 1) * w_half, :] = wgrad(z, p)

    lanes = lambda v: pl.ds(pl.multiple_of(v * 256, 256), 256)

    def zk(p):
        return rcopy(zsb.at[p], zrb.at[p], zk_s.at[p], zk_r.at[p], place(x, y, z + 1 - 2 * zl, c))

    for p in range(2):
        ring = (sring, pring)[p]
        ring.wait_result()
        for k in range(2):
            kown[p, k] = ring.result(k, segt[y, k] if p == 0 else acc[k])
        zsb[p] = kown[p, :, :, lanes(1 - zl)].astype(BF)
        zk(p).start()

    gring.wait_result()
    for p in range(2):
        rows = slice(p * w_half, (p + 1) * w_half)
        owg[rows, :] = gring.result(p, owg[rows, :])

    for p in range(2):
        zk(p).wait_recv()
        for i in range(2):
            t = kown[p, i, :, lanes(zl)] + zrb[p, i].astype(F32)
            if i == 0:
                t = t * SCALE
            okv[2 * (1 - p) + i] = t.T.astype(BF)

    kz().wait_send()
    for p in range(2):
        zk(p).wait_send()

    cy(1).wait_send()

    @pl.when(jnp.logical_not(is_src))
    def _():
        cy(0).wait_send()

    @pl.when(is_recv)
    def _():
        xring.wait_sends()
        for n in range(4):
            for p in range(2):
                cb(n, p).wait_send()

    for ring in (wring, kring, aring, dring, pring, sring, gring):
        ring.wait_sends()


def finish_kernel(dq, kv, wgr, o0, o1, o2, o3, o4, o5):
    o0[...] = dq[...]
    for i, o in enumerate((o1, o2, o3, o4)):
        o[...] = kv[i]
    o5[...] = wgr[...]


def on_device(
    queries, prefix_keys, prefix_values, keys, values, ancestors, advantages, upstream, out_weight
):
    dma = pltpu.SemaphoreType.DMA
    sds = jax.ShapeDtypeStruct
    vm = pltpu.VMEM
    half_w = WROWS // 2
    dq, okv, owg = pl.pallas_call(
        whole_kernel,
        out_shape=(
            sds((TOKL, NCOL), BF),
            sds((4, 256, HD), BF),
            sds((WROWS, NCOL), F32),
        ),
        in_specs=[VM] * 9,
        out_specs=(VM, VM, VM),
        scratch_shapes=[
            vm((TOKL, UCOL), BF),
            vm((2, 4, TOKL, UCOL), BF),
            vm((2 * UCOL, 4 * TOKL), BF),
            vm((4 * WROWS, NCOL), BF),
            vm((4, CTX, HD), BF),
            vm((2, SEGCTX, HD), BF),
            vm((2, SEGCTX, HD), BF),
            vm((6, SEG, NCOL), BF),
            vm((6, SEG, NCOL), BF),
            vm((4, SEG, NCOL), F32),
            vm((TOKL, NCOL), BF),
            vm((ROWS, 3 * CH), F32),
            vm((4, 4 * ROWS, CH), BF),
            vm((4 * ROWS, SEGCTX), BF),
            vm((4 * TOKL, NCOL), BF),
            vm((4 * ROWS, HD), F32),
            vm((2, 4 * ROWS, HD), F32),
            vm((4, HD, ROWS), BF),
            vm((4 * ROWS, HD), BF),
            vm((4, HD, ROWS), BF),
            vm((4 * ROWS, HD), F32),
            vm((2, HD, CH), F32),
            vm((2, 2, HD, SEGCTX), F32),
            vm((4, 2, HD, CH), F32),
            vm((2, 6, HD, CH), BF),
            vm((2, 6, HD, CH), BF),
            vm((2, 2, HD, 256), BF),
            vm((2, 2, HD, 256), BF),
            vm((2, 2, HD, CH), F32),
            vm((6, half_w, NCOL), BF),
            vm((6, half_w, NCOL), BF),
            vm((2, half_w, NCOL), F32),
            dma((2,)), dma((4,)), dma((6,)), dma((6,)), dma((4, 2)), dma((4, 2)),
            dma((6,)), dma((6,)), dma, dma, dma((6,)), dma((6,)),
            dma((6,)), dma((6,)), dma((6,)), dma((6,)), dma((2, 6)), dma((2, 6)),
            dma((2,)), dma((2,)), dma((6,)), dma((6,)),
        ],
        compiler_params=pltpu.CompilerParams(
            collective_id=0, has_side_effects=True, vmem_limit_bytes=VLIM),
        name="whole",
    )(ancestors[0].T, upstream[0], advantages, out_weight, prefix_keys[0], prefix_values[0], keys[0], values[0],
      queries[0])
    outs = pl.pallas_call(
        finish_kernel,
        out_shape=tuple([sds((TOKL, NCOL), BF)] + [sds((256, HD), BF)] * 4 + [sds((WROWS, NCOL), F32)]),
        in_specs=[VM] * 3,
        out_specs=tuple([VM] * 6),
        name="finish",
    )(dq, okv, owg)
    return tuple(o[None] for o in outs[:5]) + (outs[5],)


def solution(mesh):
    return jax.shard_map(
        on_device,
        mesh=mesh,
        in_specs=(
            P("dp", "branch", "tensor"),
            P("dp", "branch", "tensor"),
            P("dp", "branch", "tensor"),
            P("dp", "branch", "tensor"),
            P("dp", "branch", "tensor"),
            P("dp", None, None),
            P("dp", "branch"),
            P("dp", "branch", "tensor"),
            P(("dp", "branch"), "tensor"),
        ),
        out_specs=(
            P("dp", "branch", "tensor"),
            P("dp", "branch", "tensor"),
            P("dp", "branch", "tensor"),
            P("dp", "branch", "tensor"),
            P("dp", "branch", "tensor"),
            P(("dp", "branch"), "tensor"),
        ),
        check_vma=False,
    )
```

```python
import math

import jax
import jax.numpy as jnp
from jax import lax
from jax.experimental import pallas as pl
from jax.experimental.pallas import tpu as pltpu
from jax.sharding import PartitionSpec as P

HD = 128
SEG = 128
GROUP = 8
TOKL = 256
KVB = 8
WROWS = 320
NCOL = 1024
UCOL = 640
CTX = 2048
SEGCTX = 384
ALLCTX = CTX + SEGCTX
CH = 512
ROWS = 512
SCALE = 1.0 / math.sqrt(HD)
LOG2E = 1.4426950408889634
BF = jnp.bfloat16
F32 = jnp.float32
VM = pl.BlockSpec(memory_space=pltpu.VMEM)
VLIM = 60 * 2**20


def coords():
    b = lax.axis_index("branch")
    t = lax.axis_index("tensor")
    return t // 2, b // 2, lax.axis_index("dp") * 2 + b % 2, t % 2


def place(x, y, z, c):
    return {"dp": z // 2, "branch": y * 2 + z % 2, "tensor": x * 2 + c}


def rcopy(src, dst, ss, rs, dev):
    return pltpu.make_async_remote_copy(
        src_ref=src, dst_ref=dst, send_sem=ss, recv_sem=rs,
        device_id=dev, device_id_type=pl.DeviceIdType.MESH,
    )


def signal(sem, dev):
    pl.semaphore_signal(sem, inc=1, device_id=dev, device_id_type=pl.DeviceIdType.MESH)


def nt_dot(a, b):
    return lax.dot_general(a, b, (((1,), (1,)), ((), ())), preferred_element_type=F32)


class GatherRing:
    def __init__(self, me, dev, view, ss, rs):
        self.me, self.dev, self.view, self.ss, self.rs = me, dev, view, ss, rs

    def copy(self, node, piece, kind, step):
        v = self.view(node, piece)
        i = kind * 2 + piece
        return rcopy(v, v, self.ss.at[i], self.rs.at[i], self.dev(step))

    def right(self, p):
        return self.copy(self.me, p, 0, 1)

    def left(self, p):
        return self.copy(self.me, p, 1, 3)

    def fwd(self, p):
        if p == 0:
            return self.copy((self.me + 3) % 4, 0, 2, 1)
        return self.copy((self.me + 1) % 4, 1, 2, 3)

    def send(self, p):
        self.right(p).start()
        self.left(p).start()

    def forward(self, p):
        (self.right if p == 0 else self.left)(p).wait_recv()
        self.fwd(p).start()

    def wait_near(self):
        self.right(1).wait_recv()
        self.left(0).wait_recv()

    def wait_far(self):
        self.fwd(0).wait_recv()
        self.fwd(1).wait_recv()

    def wait_sends(self):
        for p in range(2):
            self.right(p).wait_send()
            self.left(p).wait_send()
            self.fwd(p).wait_send()


class SumRing:
    def __init__(self, dev, sb, rb, ss, rs):
        self.dev, self.sb, self.rb, self.ss, self.rs = dev, sb, rb, ss, rs

    def copy(self, i):
        return rcopy(self.sb.at[i], self.rb.at[i], self.ss.at[i], self.rs.at[i], self.dev(1 if i % 2 == 0 else 3))

    def send(self, i, value):
        self.sb[i] = value.astype(BF)
        self.copy(i).start()

    def add_send(self, i, value):
        self.copy(i - 4).wait_recv()
        self.send(i, value + self.rb[i - 4].astype(F32))

    def wait_result(self):
        for i in range(2, 6):
            self.copy(i).wait_recv()

    def result(self, p, own):
        a, b = ((4, 3), (2, 5))[p]
        return own + self.rb[a].astype(F32) + self.rb[b].astype(F32)

    def wait_sends(self):
        for i in range(6):
            self.copy(i).wait_send()


def whole_kernel(
    anc, up, adv, w, pk, pv, sk, sv, q,
    odq, okv, owg,
    cot, cotb, cott, wg, kvg, kcs, vcs,
    dsb, drb, dnear, dattn,
    s_f, p_b, p_s, attng, il_b, delta, qt, dos, dost, dqa,
    acc, accs, segt, ksb, krb, zsb, zrb, kown,
    gsb, grb, gnear,
    c_s, c_r, x_s, x_r, b_s, b_r, w_s, w_r, kz_s, kz_r, k_s, k_r,
    d_s, d_r, a_s, a_r, r_s, r_r, zk_s, zk_r, g_s, g_r,
):
    x, y, z, c = coords()
    zl = z % 2
    first = lax.axis_index("branch") * 2
    target_y = 2 * (x % 2) + c
    is_recv = c == y % 2
    is_src = target_y == y
    is_mid = is_recv & jnp.logical_not(is_src)
    sib = place(x, y, z, 1 - c)
    cexp = SCALE * LOG2E

    def ydev(d):
        return place(x, (y + d) % 4, z, c)

    def zdev(d):
        return place(x, y, (z + d) % 4, c)

    def xdev(d):
        return place((x + d) % 4, y, z, c)

    bar = pltpu.get_barrier_semaphore()
    for d in range(1, 4):
        signal(bar, ydev(d))
    signal(bar, zdev(1))
    signal(bar, zdev(3))
    signal(bar, sib)

    @pl.when(is_recv)
    def _():
        signal(bar, xdev(1))
        signal(bar, xdev(3))

    @pl.when(is_mid)
    def _():
        for d in range(1, 4):
            signal(bar, place((x + 3) % 4, (y + d) % 4, z, c))

    rows_b = lambda b: pl.ds(pl.multiple_of(b * 256, 256), 256)
    own_rows = rows_b(y * 2 + zl)
    for i, r in enumerate((pk, pv, sk, sv)):
        kvg[i, own_rows, :] = r[...]
    wrow = jnp.broadcast_to(adv[...].astype(F32) * 0.25, (TOKL, TOKL))
    ri = lax.broadcasted_iota(jnp.int32, (TOKL, TOKL), 0)
    ci = lax.broadcasted_iota(jnp.int32, (TOKL, TOKL), 1)
    diag = jnp.where(ri == ci, wrow, 0.0).astype(BF)
    cot[...] = jnp.dot(diag, up[...], preferred_element_type=F32).astype(BF)
    w_half = WROWS // 2
    wview = lambda n, p: wg.at[pl.ds(pl.multiple_of(n * WROWS + p * w_half, 32), w_half)]
    wg[pl.ds(pl.multiple_of(z * WROWS, 64), WROWS), :] = w[...]

    pl.semaphore_wait(bar, 6 + 2 * is_recv.astype(jnp.int32) + 1 - is_src.astype(jnp.int32))

    wring = GatherRing(z, zdev, wview, w_s, w_r)
    kring = GatherRing(y, ydev, lambda n, p: kvg.at[:, rows_b(n * 2 + p)], k_s, k_r)
    aring = GatherRing(
        y, ydev, lambda n, p: attng.at[pl.ds(pl.multiple_of(n * TOKL + p * SEG, SEG), SEG)], a_s, a_r)
    dring = SumRing(ydev, dsb, drb, d_s, d_r)
    rring = SumRing(ydev, ksb, krb, r_s, r_r)
    gring = SumRing(zdev, gsb, grb, g_s, g_r)

    def kz():
        v = kvg.at[:, own_rows]
        return rcopy(v, v, kz_s, kz_r, place(x, y, z + 1 - 2 * zl, c))

    def quarter(n, yy):
        second = (n + y // 2) % 2
        return cotb.at[((n + 4 - second) % 4) // 2, yy, pl.ds(pl.multiple_of(second * SEG, SEG), SEG)]

    def quarter_piece(n, p):
        second = (n + y // 2) % 2
        return cotb.at[((n + 4 - second) % 4) // 2, 2 * p:2 * p + 2, pl.ds(pl.multiple_of(second * SEG, SEG), SEG)]

    xring = GatherRing(x, xdev, quarter_piece, x_s, x_r)

    def cy(second):
        dst = cotb.at[x // 2, y, second * SEG:(second + 1) * SEG]
        return rcopy(cot.at[second * SEG:(second + 1) * SEG], dst, c_s.at[second], c_r.at[y],
                     place((x + second) % 4, target_y, z, c))

    def cy_arrived(yy):
        rcopy(cot.at[0:SEG], quarter(x, yy), c_s.at[0], c_r.at[yy], sib).wait_recv()

    def cb(n, p):
        v = quarter_piece(n, p)
        return rcopy(v, v, b_s.at[n, p], b_r.at[n, p], sib)

    kz().start()
    cy(1).start()

    @pl.when(jnp.logical_not(is_src))
    def _():
        cy(0).start()

    kring.send(zl)

    @pl.when(zl == 0)
    def _():
        for p in range(2):
            wring.left(p).start()

    @pl.when(zl == 1)
    def _():
        for p in range(2):
            wring.right(p).start()

    @pl.when(is_src)
    def _():
        cotb[x // 2, y, 0:SEG] = cot[0:SEG]

    kz().wait_recv()
    kring.send(1 - zl)

    @pl.when(zl == 0)
    def _():
        for p in range(2):
            wring.right(p).start()

    @pl.when(zl == 1)
    def _():
        for p in range(2):
            wring.left(p).start()

    @pl.when(is_recv)
    def _():
        for p in range(2):
            for yy in (2 * p, 2 * p + 1):
                @pl.when(jnp.logical_not(is_src & (yy == y)))
                def _():
                    cy_arrived(yy)
            xring.send(p)
            cb(x, p).start()

    for p in range(2):
        kring.forward(p)

    @pl.when(is_recv)
    def _():
        xring.forward(0)
        cb((x + 3) % 4, 0).start()
        xring.forward(1)
        cb((x + 1) % 4, 1).start()

    @pl.when(zl == 0)
    def _():
        wring.forward(0)

    @pl.when(zl == 1)
    def _():
        wring.forward(1)

    kring.wait_near()
    nh = ROWS // SEG

    def spot(rb):
        s, hb = rb // 2, rb % 2
        return s, hb, slice(s * SEG, (s + 1) * SEG), slice(rb * ROWS, (rb + 1) * ROWS), [
            slice((hb * nh + i) * HD, (hb * nh + i + 1) * HD) for i in range(nh)]

    def crow(j):
        return pl.ds(pl.multiple_of(j * CH, CH), CH)

    def lane_max(sc, mx):
        for t in range(sc.shape[1] // HD):
            part = sc[:, t * HD:(t + 1) * HD]
            mx = part if mx is None else jnp.maximum(mx, part)
        return mx

    def lane_sum(p, tot):
        for t in range(p.shape[1] // HD):
            part = p[:, t * HD:(t + 1) * HD]
            tot = part if tot is None else tot + part
        return tot

    def forward_near(rb):
        s, hb, tok, rows, heads = spot(rb)
        qb = jnp.concatenate([q[tok, h] for h in heads], axis=0)
        qt[rb] = qb.T
        mx = None
        for i, d in enumerate((0, 1, 3)):
            sc = nt_dot(qb, kvg[0, crow((y + d) % 4), :])
            s_f[:, i * CH:(i + 1) * CH] = sc
            mx = lane_max(sc, mx)
        m = jnp.max(mx, axis=1, keepdims=True)
        lsum = None
        o = None
        for i, d in enumerate((0, 1, 3)):
            j = (y + d) % 4
            p = jnp.exp2((s_f[:, i * CH:(i + 1) * CH] - m) * cexp)
            lsum = lane_sum(p, lsum)
            pb = p.astype(BF)
            p_b[j, rows, :] = pb
            oc = jnp.dot(pb, kvg[1, crow(j), :], preferred_element_type=F32)
            o = oc if o is None else o + oc
        delta[0, rows, :] = lsum
        delta[1, rows, :] = jnp.broadcast_to(m, (ROWS, HD))
        dqa[rows, :] = o

    for rb in range(4):
        forward_near(rb)

    @pl.when(zl == 0)
    def _():
        wring.forward(1)

    @pl.when(zl == 1)
    def _():
        wring.forward(0)

    kring.wait_far()

    lane = lax.broadcasted_iota(jnp.int32, (1, 16), 1)
    named = [[jnp.broadcast_to(jnp.sum(jnp.where(lane == first + s, anc[i:i + 1, :].astype(F32), 0.0),
                                       axis=1, keepdims=True), (1, HD)) for i in range(2)] for s in range(2)]

    def hot(s, i, j):
        return (named[s][i] == float(j)).astype(F32)

    for s in range(2):
        own_seg = pl.ds(pl.multiple_of((first + s) * SEG, SEG), SEG)
        for k, dst in enumerate((kcs, vcs)):
            for i in range(2):
                tot = None
                for j in range(16):
                    v = kvg[2 + k, j * SEG:(j + 1) * SEG, :] * hot(s, i, j).astype(BF)
                    tot = v if tot is None else tot + v
                dst[s, i * SEG:(i + 1) * SEG, :] = tot
            dst[s, 2 * SEG:, :] = kvg[2 + k, own_seg, :]

    def forward_far(rb):
        s, hb, tok, rows, heads = spot(rb)
        col = lax.broadcasted_iota(jnp.int32, (ROWS, SEG), 1)
        row = lax.broadcasted_iota(jnp.int32, (ROWS, SEG), 0) % SEG
        shut = [jnp.where(named[s][i] >= 0, 0.0, -1e30) for i in range(2)]
        shut.append(jnp.where(col <= row, 0.0, -1e30))
        qb = jnp.concatenate([q[tok, h] for h in heads], axis=0)
        far = (y + 2) % 4
        sc = nt_dot(qb, kvg[0, crow(far), :])
        s_f[:, 0:CH] = sc
        mx = lane_max(sc, None)
        sc = nt_dot(qb, kcs[s])
        sc = jnp.concatenate([sc[:, i * SEG:(i + 1) * SEG] + shut[i] for i in range(3)], axis=1)
        s_f[:, CH:CH + SEGCTX] = sc
        mx = lane_max(sc, mx)
        m_near = delta[1, rows, 0:1]
        m = jnp.maximum(jnp.max(mx, axis=1, keepdims=True), m_near)
        p = jnp.exp2((s_f[:, 0:CH] - m) * cexp)
        lsum = lane_sum(p, None)
        pb = p.astype(BF)
        p_b[far, rows, :] = pb
        o = jnp.dot(pb, kvg[1, crow(far), :], preferred_element_type=F32)
        p = jnp.exp2((s_f[:, CH:CH + SEGCTX] - m) * cexp)
        lsum = lane_sum(p, lsum)
        pb = p.astype(BF)
        p_s[rows, :] = pb
        o = o + jnp.dot(pb, vcs[s], preferred_element_type=F32)
        ratio = jnp.broadcast_to(jnp.exp2((m_near - m) * cexp), (ROWS, HD))
        lsum = lsum + delta[0, rows, :] * ratio
        o = o + dqa[rows, :] * ratio
        il = jnp.broadcast_to(1.0 / jnp.sum(lsum, axis=1, keepdims=True), (ROWS, HD))
        il_b[rows, :] = il
        delta[1, rows, :] = ratio
        ob = (o * il).astype(BF)
        for i, h in enumerate(heads):
            attng[pl.ds(pl.multiple_of(y * TOKL + s * SEG, SEG), SEG), h] = ob[i * SEG:(i + 1) * SEG]

    forward_far(0)
    forward_far(1)
    aring.send(0)
    forward_far(2)
    forward_far(3)
    aring.send(1)

    @pl.when(is_recv)
    def _():
        xring.wait_near()
        cb((x + 3) % 4, 1).start()
        cb((x + 1) % 4, 0).start()
        xring.wait_far()
        for p in range(2):
            cb((x + 2) % 4, p).start()

    aring.forward(0)

    wring.wait_near()
    wring.wait_far()

    @pl.when(jnp.logical_not(is_recv))
    def _():
        for n in range(4):
            for p in range(2):
                cb(n, p).wait_recv()

    def proj(yy, rows):
        return jnp.dot(cotb[0, yy, rows, :], wg[0:UCOL, :], preferred_element_type=F32) + jnp.dot(
            cotb[1, yy, rows, :], wg[UCOL:2 * UCOL, :], preferred_element_type=F32)

    lo, hi = slice(0, SEG), slice(SEG, 2 * SEG)
    dring.send(0, proj((y + 2) % 4, lo))
    dring.send(1, proj((y + 2) % 4, hi))
    dring.send(2, proj((y + 1) % 4, hi))
    dring.send(3, proj((y + 3) % 4, lo))
    dnear[0] = proj((y + 1) % 4, lo)
    dnear[1] = proj((y + 3) % 4, hi)
    dnear[2] = proj(y, lo)
    dnear[3] = proj(y, hi)

    aring.forward(1)
    for h in range(2):
        for yy in range(4):
            cott[h * UCOL:(h + 1) * UCOL, yy * TOKL:(yy + 1) * TOKL] = cotb[h, yy].T
    for d in (0, 1, 3):
        for rb in range(4):
            j, rows = (y + d) % 4, slice(rb * ROWS, (rb + 1) * ROWS)
            ratio = jnp.concatenate([delta[1, rows, :]] * (CH // HD), axis=1)
            p_b[j, rows, :] = (p_b[j, rows, :].astype(F32) * ratio).astype(BF)
    dring.add_send(4, dnear[0])
    dring.add_send(5, dnear[1])

    aring.wait_near()
    aring.wait_far()

    def wgrad(zz, p):
        rows = pl.ds(pl.multiple_of(zz * WROWS + p * w_half, 32), w_half)
        return jnp.dot(cott[rows, :], attng[...], preferred_element_type=F32)

    gring.send(0, wgrad((z + 2) % 4, 0))
    gring.send(1, wgrad((z + 2) % 4, 1))
    gring.send(2, wgrad((z + 1) % 4, 1))
    gring.send(3, wgrad((z + 3) % 4, 0))
    gnear[0] = wgrad((z + 1) % 4, 0)
    gnear[1] = wgrad((z + 3) % 4, 1)

    dring.wait_result()
    for p in range(2):
        dattn[p * SEG:(p + 1) * SEG, :] = dring.result(p, dnear[2 + p]).astype(BF)
    for rb in range(4):
        s, hb, tok, rows, heads = spot(rb)
        arow = pl.ds(pl.multiple_of(y * TOKL + s * SEG, SEG), SEG)
        dob = jnp.concatenate([dattn[tok, h] for h in heads], axis=0)
        at = jnp.concatenate([attng[arow, h] for h in heads], axis=0)
        db = (dob.astype(F32) * il_b[rows, :]).astype(BF)
        dos[rows, :] = db
        dost[rb] = db.T
        dl = jnp.sum(db.astype(F32) * at.astype(F32), axis=1, keepdims=True)
        delta[0, rows, :] = jnp.broadcast_to(dl, (ROWS, HD))

    def back(rb, kc, vc, pb):
        rows = pl.ds(pl.multiple_of(rb * ROWS, ROWS), ROWS)
        dl = delta[0, rows, :]
        n = vc.shape[0]
        dp = nt_dot(dos[rows, :], vc)
        ds = (pb.astype(F32) * (dp - jnp.concatenate([dl] * (n // HD), axis=1))).astype(BF)
        return (rows, jnp.dot(ds, kc, preferred_element_type=F32),
                jnp.dot(qt[rb], ds, preferred_element_type=F32),
                jnp.dot(dost[rb], pb, preferred_element_type=F32))

    def prefix(j):
        acc[...] = jnp.zeros_like(acc)

        @pl.loop(0, 4)
        def _(rb):
            rows = pl.ds(pl.multiple_of(rb * ROWS, ROWS), ROWS)
            _, dqc, dk, dv = back(rb, kvg[0, crow(j), :], kvg[1, crow(j), :], p_b[j, rows, :])
            dqa[rows, :] += dqc
            acc[0] += dk
            acc[1] += dv

    for rb in range(4):
        s = rb // 2
        rows, dqc, dk, dv = back(rb, kcs[s], vcs[s], p_s[rb * ROWS:(rb + 1) * ROWS, :])
        dqa[rows, :] = dqc
        if rb % 2 == 0:
            accs[s, 0] = dk
            accs[s, 1] = dv
        else:
            accs[s, 0] += dk
            accs[s, 1] += dv
    for j in range(16):
        for k in range(2):
            tot = None
            for s in range(2):
                for i in range(2):
                    v = accs[s, k, :, i * SEG:(i + 1) * SEG] * hot(s, i, j)
                    tot = v if tot is None else tot + v
            segt[j // 4, k, :, (j % 4) * SEG:(j % 4 + 1) * SEG] = tot
    for s in range(2):
        own_cols = pl.ds(pl.multiple_of((zl * 2 + s) * SEG, SEG), SEG)
        for k in range(2):
            segt[y, k, :, own_cols] += accs[s, k, :, 2 * SEG:]
    rring.send(0, segt[(y + 2) % 4])
    rring.send(3, segt[(y + 3) % 4])

    prefix((y + 2) % 4)
    rring.send(1, acc[...])
    gring.add_send(4, gnear[0])
    gring.add_send(5, gnear[1])
    prefix((y + 1) % 4)
    rring.send(2, acc[...])
    rring.add_send(4, segt[(y + 1) % 4])
    prefix((y + 3) % 4)
    rring.add_send(5, acc[...])
    prefix(y)
    for rb in range(4):
        s, hb = rb // 2, rb % 2
        dqb = (dqa[rb * ROWS:(rb + 1) * ROWS, :] * SCALE).astype(BF)
        for i in range(nh):
            odq[s * SEG:(s + 1) * SEG, (hb * nh + i) * HD:(hb * nh + i + 1) * HD] = dqb[i * SEG:(i + 1) * SEG]

    for p in range(2):
        owg[p * w_half:(p + 1) * w_half, :] = wgrad(z, p)

    lanes = lambda v: pl.ds(pl.multiple_of(v * 256, 256), 256)

    def zk(p):
        return rcopy(zsb.at[p], zrb.at[p], zk_s.at[p], zk_r.at[p], place(x, y, z + 1 - 2 * zl, c))

    for p in range(2):
        for i in ((4, 3), (2, 5))[p]:
            rring.copy(i).wait_recv()
        kown[p] = rring.result(p, segt[y] if p == 0 else acc[...])
        zsb[p] = kown[p, :, :, lanes(1 - zl)].astype(BF)
        zk(p).start()

    gring.wait_result()
    for p in range(2):
        rows = slice(p * w_half, (p + 1) * w_half)
        owg[rows, :] = gring.result(p, owg[rows, :])

    for p in range(2):
        zk(p).wait_recv()
        for i in range(2):
            t = kown[p, i, :, lanes(zl)] + zrb[p, i].astype(F32)
            if i == 0:
                t = t * SCALE
            okv[2 * (1 - p) + i] = t.T.astype(BF)

    kz().wait_send()
    for p in range(2):
        zk(p).wait_send()

    cy(1).wait_send()

    @pl.when(jnp.logical_not(is_src))
    def _():
        cy(0).wait_send()

    @pl.when(is_recv)
    def _():
        xring.wait_sends()
        for n in range(4):
            for p in range(2):
                cb(n, p).wait_send()

    for ring in (wring, kring, aring, dring, rring, gring):
        ring.wait_sends()


def finish_kernel(dq, kv, wgr, o0, o1, o2, o3, o4, o5):
    o0[...] = dq[...]
    for i, o in enumerate((o1, o2, o3, o4)):
        o[...] = kv[i]
    o5[...] = wgr[...]


def on_device(
    queries, prefix_keys, prefix_values, keys, values, ancestors, advantages, upstream, out_weight
):
    dma = pltpu.SemaphoreType.DMA
    sds = jax.ShapeDtypeStruct
    vm = pltpu.VMEM
    half_w = WROWS // 2
    dq, okv, owg = pl.pallas_call(
        whole_kernel,
        out_shape=(
            sds((TOKL, NCOL), BF),
            sds((4, 256, HD), BF),
            sds((WROWS, NCOL), F32),
        ),
        in_specs=[VM] * 9,
        out_specs=(VM, VM, VM),
        scratch_shapes=[
            vm((TOKL, UCOL), BF),
            vm((2, 4, TOKL, UCOL), BF),
            vm((2 * UCOL, 4 * TOKL), BF),
            vm((4 * WROWS, NCOL), BF),
            vm((4, CTX, HD), BF),
            vm((2, SEGCTX, HD), BF),
            vm((2, SEGCTX, HD), BF),
            vm((6, SEG, NCOL), BF),
            vm((6, SEG, NCOL), BF),
            vm((4, SEG, NCOL), F32),
            vm((TOKL, NCOL), BF),
            vm((ROWS, 3 * CH), F32),
            vm((4, 4 * ROWS, CH), BF),
            vm((4 * ROWS, SEGCTX), BF),
            vm((4 * TOKL, NCOL), BF),
            vm((4 * ROWS, HD), F32),
            vm((2, 4 * ROWS, HD), F32),
            vm((4, HD, ROWS), BF),
            vm((4 * ROWS, HD), BF),
            vm((4, HD, ROWS), BF),
            vm((4 * ROWS, HD), F32),
            vm((2, HD, CH), F32),
            vm((2, 2, HD, SEGCTX), F32),
            vm((4, 2, HD, CH), F32),
            vm((6, 2, HD, CH), BF),
            vm((6, 2, HD, CH), BF),
            vm((2, 2, HD, 256), BF),
            vm((2, 2, HD, 256), BF),
            vm((2, 2, HD, CH), F32),
            vm((6, half_w, NCOL), BF),
            vm((6, half_w, NCOL), BF),
            vm((2, half_w, NCOL), F32),
            dma((2,)), dma((4,)), dma((6,)), dma((6,)), dma((4, 2)), dma((4, 2)),
            dma((6,)), dma((6,)), dma, dma, dma((6,)), dma((6,)),
            dma((6,)), dma((6,)), dma((6,)), dma((6,)), dma((6,)), dma((6,)),
            dma((2,)), dma((2,)), dma((6,)), dma((6,)),
        ],
        compiler_params=pltpu.CompilerParams(
            collective_id=0, has_side_effects=True, vmem_limit_bytes=VLIM),
        name="whole",
    )(ancestors[0].T, upstream[0], advantages, out_weight, prefix_keys[0], prefix_values[0], keys[0], values[0],
      queries[0])
    outs = pl.pallas_call(
        finish_kernel,
        out_shape=tuple([sds((TOKL, NCOL), BF)] + [sds((256, HD), BF)] * 4 + [sds((WROWS, NCOL), F32)]),
        in_specs=[VM] * 3,
        out_specs=tuple([VM] * 6),
        name="finish",
    )(dq, okv, owg)
    return tuple(o[None] for o in outs[:5]) + (outs[5],)


def solution(mesh):
    return jax.shard_map(
        on_device,
        mesh=mesh,
        in_specs=(
            P("dp", "branch", "tensor"),
            P("dp", "branch", "tensor"),
            P("dp", "branch", "tensor"),
            P("dp", "branch", "tensor"),
            P("dp", "branch", "tensor"),
            P("dp", None, None),
            P("dp", "branch"),
            P("dp", "branch", "tensor"),
            P(("dp", "branch"), "tensor"),
        ),
        out_specs=(
            P("dp", "branch", "tensor"),
            P("dp", "branch", "tensor"),
            P("dp", "branch", "tensor"),
            P("dp", "branch", "tensor"),
            P("dp", "branch", "tensor"),
            P(("dp", "branch"), "tensor"),
        ),
        check_vma=False,
    )
```
